512 devices in a mesh: coil: 16 (over z_lo, core), slab: 32 (over x, z_hi, y).
Axes of the slice: x: 4, y: 4, z: 16 (z_hi: 2, z_lo: 8; z = z_hi * 8 + z_lo), core: 2. Of those that a mesh axis runs over, the one named last changes fastest.
Arguments:
- kspace_data: bfloat16 [32, 2, 128, 128, 128], P('coil', None, None, 'slab'), may hold values from -4 to 4
- coil_maps: bfloat16 [32, 2, 128, 128, 128], P('coil', None, 'slab'), may hold values from -1.796875 to 1.796875
- sample_mask: int32 [32, 128, 128], P('coil', None, 'slab'), may hold values 0 or 1
- initial_image: float32 [2, 128, 128, 128], P(None, 'slab', 'coil'), may hold values from -6 to 6
Outputs:
- image: float32 [2, 128, 128, 128], P(None, 'slab', 'coil')
The draws below stay inside these ranges and needn't reach their ends.
All inputs are finite; a program needn't handle non-finite values. No bound on the sum of `sample_mask` on one device may be relied on, other than what follows from the above.
Results may differ from the reference program's by a relative error of at most 0.0045.
Values may be sent and summed in bfloat16 or wider, within the bound.
No kernel may reach another device: no remote copies, remote signals or barrier semaphores. Data moves between devices by JAX's collectives and lax.ppermute only.
A program may use at most 64 MiB of HBM per device.

```python
import math
import jax
import jax.numpy as jnp
from jax import lax

NX = 128
NY = 128
NZ = 128
COILS = 32
ITERS = 2


def touch_ends(entries, own_key, smallest, top_value):
    dims = entries.shape
    spot = [jax.random.randint(jax.random.fold_in(own_key, axis), (), 0, dims[axis]) for axis in range(len(dims))]
    entries = entries.at[tuple(spot)].set(smallest)
    longest = dims.index(max(dims))
    spot[longest] = (spot[longest] + 1) % dims[longest]
    return entries.at[tuple(spot)].set(top_value)


def spiked(entries, rng, source, target, blocks, factor):
    owner, partner = [(jnp.arange(entries.shape[axis_at]) // (entries.shape[axis_at] // blocks)).reshape([-1 if axis == axis_at else 1 for axis in range(entries.ndim)]) for axis_at in (source, target)]
    chosen = jax.random.permutation(rng, blocks)[partner]
    strong = (owner == chosen) | (owner == (partner + blocks // 2) % blocks)
    return jnp.where(strong, factor * entries, entries)


def block_scale(stream_key, dims, cuts, low, high):
    loudness = 1.0
    for position, shards_of in cuts:
        heights = jax.random.uniform(jax.random.fold_in(jax.random.fold_in(stream_key, 6), position), (shards_of,), jnp.float32, low / len(cuts), high / len(cuts))
        loudness = loudness * jnp.repeat(jnp.exp(heights), dims[position] // shards_of).reshape((-1,) + (1,) * (len(dims) - 1 - position))
    return loudness


def normal_values(stream_key, shape, scale, limit, cuts=(), kind=jnp.bfloat16):
    level = block_scale(stream_key, shape, cuts, -0.22, 0.18) if cuts else 1.0
    entries = jax.random.normal(stream_key, shape, jnp.float32) * scale * level
    return jnp.minimum(jnp.maximum(entries, -limit), limit).astype(kind)


def bell_draw_with(rng, shape, scale, bound, cuts, heavy, kind=jnp.bfloat16):
    array = scale * jax.random.normal(rng, shape, jnp.float32)
    if cuts:
        array = array * block_scale(rng, shape, cuts, -0.22, 0.18)
    return jnp.clip(spiked(array, jax.random.fold_in(rng, 3), *heavy), -bound, bound).astype(kind)


def setup_inputs(seed: int = 0) -> dict:
    key_list = jax.random.split(jax.random.key(seed), 5)
    kspace_data = normal_values(key_list[0], (COILS, 2, NZ, NY, NX), 0.5, 4.0, ((0, 16), (3, 32)))
    coil_maps = bell_draw_with(key_list[1], (COILS, 2, NZ, NY, NX), 0.3, 1.796875, ((0, 16), (2, 32)), (0, 3, 16, 2.0))
    sample_mask = touch_ends((jax.random.randint(key_list[2], (COILS, NZ, NY), 0, 3) < 1).astype(jnp.int32), jax.random.fold_in(key_list[2], 1), 0, 1)
    initial_image = normal_values(key_list[3], (2, NZ, NY, NX), 1.0, 6.0, ((1, 32), (2, 16)), jnp.float32)
    return {"kspace_data": kspace_data, "coil_maps": coil_maps, "sample_mask": sample_mask, "initial_image": initial_image}


dual_step = 0.25
primal_step = 0.25
tv_weight = 0.5

def dft_table(length, inverse):
    counter = jnp.arange(length, dtype=jnp.int32)
    product = counter[:, None] * counter[None, :] % length
    phase = 2.0 * math.pi / length * product.astype(jnp.float32)
    scale = 1.0 / math.sqrt(length)
    real_part = jnp.cos(phase) * scale
    imag_part = jnp.sin(phase) * scale
    if not inverse:
        imag_part = -imag_part
    table = jnp.stack([jnp.stack([real_part, imag_part]), jnp.stack([-imag_part, real_part])])
    return table.astype(jnp.bfloat16)

def along_x(field, table):
    return jnp.einsum('kzyx,kjxw->jzyw', field.astype(jnp.float32), table.astype(jnp.float32))

def along_y(field, table):
    return jnp.einsum('kzyx,kjyv->jzvx', field.astype(jnp.float32), table.astype(jnp.float32))

def along_z(field, table):
    return jnp.einsum('kzyx,kjzw->jwyx', field.astype(jnp.float32), table.astype(jnp.float32))

def forward_diff(field, axis_pos):
    length = field.shape[axis_pos]
    upper = lax.slice_in_dim(field, 1, length, axis=axis_pos)
    lower = lax.slice_in_dim(field, 0, length - 1, axis=axis_pos)
    zero_slice = jnp.zeros_like(lax.slice_in_dim(field, 0, 1, axis=axis_pos))
    return jnp.concatenate([upper - lower, zero_slice], axis_pos)

def backward_diff(field, axis_pos):
    length = field.shape[axis_pos]
    lower = lax.slice_in_dim(field, 0, length - 1, axis=axis_pos)
    zero_slice = jnp.zeros_like(lax.slice_in_dim(field, 0, 1, axis=axis_pos))
    return jnp.concatenate([zero_slice, lower], axis_pos) - field

def reference(kspace_data, coil_maps, sample_mask, initial_image):
    forward_x = dft_table(NX, False)
    forward_y = dft_table(NY, False)
    forward_z = dft_table(NZ, False)
    inverse_x = dft_table(NX, True)
    inverse_y = dft_table(NY, True)
    inverse_z = dft_table(NZ, True)
    current = initial_image
    guess = initial_image
    dual_data = jnp.zeros(kspace_data.shape, jnp.float32)
    duals = (jnp.zeros_like(current), jnp.zeros_like(current), jnp.zeros_like(current))
    for turn_index in range(ITERS):

        def per_coil(total, items):
            maps_one, data_one, mask_one, dual_one = items
            maps_real = maps_one[0].astype(jnp.float32)
            maps_imag = maps_one[1].astype(jnp.float32)
            pieces = jnp.stack([maps_real * guess[0] - maps_imag * guess[1], maps_real * guess[1] + maps_imag * guess[0]]).astype(jnp.bfloat16)
            pieces = along_x(pieces, forward_x).astype(jnp.bfloat16)
            pieces = along_y(pieces, forward_y).astype(jnp.bfloat16)
            spectrum = along_z(pieces, forward_z)
            sampled = mask_one[None, :, :, None].astype(jnp.float32)
            dual_new = (dual_one + dual_step * (sampled * (spectrum - data_one.astype(jnp.float32)))) / (1.0 + dual_step)
            back_field = along_z(dual_new.astype(jnp.bfloat16), inverse_z).astype(jnp.bfloat16)
            back_field = along_y(back_field, inverse_y).astype(jnp.bfloat16)
            back_field = along_x(back_field, inverse_x)
            combined = jnp.stack([maps_real * back_field[0] + maps_imag * back_field[1], maps_real * back_field[1] - maps_imag * back_field[0]])
            return (total + combined, dual_new)
        data_grad, dual_data = lax.scan(per_coil, jnp.zeros_like(current), (coil_maps, kspace_data, sample_mask, dual_data))
        grads = (forward_diff(guess, 1), forward_diff(guess, 2), forward_diff(guess, 3))
        moved = [duals[num] + dual_step * grads[num] for num in range(3)]
        magnitude = jnp.sqrt(lax.optimization_barrier(jnp.sum(moved[0] * moved[0], 0)) + lax.optimization_barrier(jnp.sum(moved[1] * moved[1], 0)) + lax.optimization_barrier(jnp.sum(moved[2] * moved[2], 0)))
        factor = 1.0 / jnp.maximum(1.0, magnitude / tv_weight)
        duals = (moved[0] * factor, moved[1] * factor, moved[2] * factor)
        spread = backward_diff(duals[0], 1) + backward_diff(duals[1], 2) + backward_diff(duals[2], 3)
        updated = current - primal_step * (data_grad + spread)
        guess = 2.0 * updated - current
        current = updated
    return current
```

```python
import math

import jax
import jax.numpy as jnp
from jax import lax
from jax.sharding import Mesh
from jax.sharding import PartitionSpec as P

ITERS = 2
dual_step = 0.25
primal_step = 0.25
tv_weight = 0.5

COLUMN = ("zq", "x", "zhi", "y")
GROUP = ("zp", "core")
bf16 = jnp.bfloat16
f32 = jnp.float32


def dft_table(length, inverse):
    counter = jnp.arange(length, dtype=jnp.int32)
    product = counter[:, None] * counter[None, :] % length
    phase = 2.0 * math.pi / length * product.astype(jnp.float32)
    scale = 1.0 / math.sqrt(length)
    real_part = jnp.cos(phase) * scale
    imag_part = jnp.sin(phase) * scale
    if not inverse:
        imag_part = -imag_part
    table = jnp.stack([jnp.stack([real_part, imag_part]), jnp.stack([-imag_part, real_part])])
    return table.astype(bf16)


def matmul(spec, a, b):
    return jnp.einsum(spec, a, b, preferred_element_type=f32)


def data_term(guess, maps, data, mask, dual, fwd, inv):
    pieces = jnp.stack(
        [maps[:, 0] * guess[0] - maps[:, 1] * guess[1], maps[:, 0] * guess[1] + maps[:, 1] * guess[0]],
        1,
    ).astype(bf16)
    pieces = matmul("ckzy,kjzw->cjwy", pieces, fwd).astype(bf16)
    spectrum = matmul("ckwy,kjyv->cjvw", pieces, fwd)
    dual = (dual + dual_step * (mask * (spectrum - data))) / (1.0 + dual_step)
    back = matmul("ckvw,kjwz->cjzv", dual.astype(bf16), inv).astype(bf16)
    back = matmul("ckzv,kjvy->cjzy", back, inv)
    real_sum = jnp.sum(maps[:, 0] * back[:, 0] + maps[:, 1] * back[:, 1], 0)
    imag_sum = jnp.sum(maps[:, 0] * back[:, 1] - maps[:, 1] * back[:, 0], 0)
    return jnp.stack([real_sum, imag_sum]), dual


def diff_up(a, axis):
    n = a.shape[axis]
    up = lax.slice_in_dim(a, 1, n, axis=axis) - lax.slice_in_dim(a, 0, n - 1, axis=axis)
    return jnp.concatenate([up, jnp.zeros_like(lax.slice_in_dim(a, 0, 1, axis=axis))], axis)


def diff_back(a, axis):
    n = a.shape[axis]
    low = lax.slice_in_dim(a, 0, n - 1, axis=axis)
    return jnp.concatenate([jnp.zeros_like(lax.slice_in_dim(a, 0, 1, axis=axis)), low], axis) - a


def shrink(here, ahead, duals):
    moved = (
        duals[0] + dual_step * diff_up(here, 1),
        duals[1] + dual_step * diff_up(here, 2),
        duals[2] + dual_step * (ahead - here),
    )
    size = jnp.sqrt(sum(jnp.sum(m * m, 0) for m in moved))
    factor = 1.0 / jnp.maximum(1.0, size / tv_weight)
    return tuple(m * factor for m in moved)


def on_device(kspace_data, coil_maps, sample_mask, initial_image):
    coils, _, planes, ny, nx = coil_maps.shape
    nz, lines = kspace_data.shape[2:4]
    rows = initial_image.shape[2]
    zq, x, zhi, y = (lax.axis_size(a) for a in COLUMN)
    group = lax.axis_size(GROUP)
    count = zhi * zq * x * y
    fwd, inv = dft_table(nz, False), dft_table(nz, True)
    inv_x = dft_table(nx, True)
    me = lax.axis_index(COLUMN)

    def spread(blocks):
        return lax.all_to_all(blocks, COLUMN, 0, 0, tiled=True)

    high = initial_image.astype(bf16)
    low = (initial_image - high.astype(f32)).astype(bf16)
    image_row = jnp.stack([high, low]).transpose(4, 0, 1, 2, 3).reshape(nx, 1, 1, ny)
    image_row = jnp.pad(image_row, ((0, 0), (0, 0), (0, planes - 1), (0, 0)))
    map_rows = coil_maps.transpose(4, 0, 1, 2, 3).reshape(nx, coils * 2, planes, ny)
    first = spread(jnp.concatenate([map_rows, image_row], 1))

    turned = matmul("ckzyw,kjwx->xcjyz", kspace_data, inv_x).astype(bf16)
    turned = turned.reshape(nx, coils * 2, lines, nz)
    mask_rows = jnp.broadcast_to(sample_mask.transpose(0, 2, 1).astype(bf16), (nx, coils, lines, nz))
    second = spread(jnp.concatenate([turned, mask_rows], 1))

    def to_planes(blocks, per):
        blocks = blocks.reshape(zq, -1, coils, per, blocks.shape[-2], blocks.shape[-1])
        return blocks.transpose(0, 2, 3, 1, 4, 5).reshape(zq * coils, per, -1, blocks.shape[-1])

    maps = to_planes(first[:, : 2 * coils], 2).astype(f32)
    data = to_planes(second[:, : 2 * coils], 2).astype(f32)
    mask = to_planes(second[:, 2 * coils :], 1).astype(f32)

    part = first[:, 2 * coils, 0].astype(f32).reshape(zq, -1, 2, 2, planes, rows).sum(2)
    part = part.transpose(2, 1, 3, 0, 4).reshape(2, nz, zq, rows)
    current = lax.all_gather(part, GROUP, axis=3, tiled=False).reshape(2, nz, ny)

    def neighbours(a):
        before = lax.ppermute(a, COLUMN, [(i, i + 1) for i in range(count - 1)])
        after = lax.ppermute(a, COLUMN, [(i + 1, i) for i in range(count - 1)])
        return before, jnp.where(me < count - 1, after, a)

    guess = current
    dual = jnp.zeros_like(data)
    zero = jnp.zeros_like(current)
    duals, duals_before = (zero,) * 3, (zero,) * 3
    for turn in range(ITERS):
        before, after = neighbours(guess)
        grad, dual = data_term(guess, maps, data, mask, dual, fwd, inv)
        duals = shrink(guess, after, duals)
        duals_before = shrink(before, guess, duals_before)
        spread_sum = (
            diff_back(duals[0], 1)
            + diff_back(duals[1], 2)
            + jnp.where(me > 0, duals_before[2], 0.0)
            - duals[2]
        )
        if turn < ITERS - 1:
            grad = lax.all_gather(grad.astype(bf16), GROUP, axis=0).astype(f32).sum(0)
            updated = current - primal_step * (grad + spread_sum)
            guess = 2.0 * updated - current
            current = updated
    grad = grad.reshape(2, nz, zq, group, rows).transpose(3, 0, 1, 2, 4).astype(bf16)
    grad = lax.all_to_all(grad, GROUP, 0, 0, tiled=True).astype(f32).sum(0)
    rest = (current - primal_step * spread_sum).reshape(2, nz, zq, group, rows)
    rest = lax.dynamic_index_in_dim(rest, lax.axis_index(GROUP), 3, keepdims=False)
    result = rest - primal_step * grad
    result = result.reshape(2, -1, planes, zq, rows).transpose(3, 1, 0, 2, 4)
    result = spread(result.reshape(count, 2 * planes * rows))
    return result.T.reshape(2, planes, rows, nx)


def solution(mesh):
    devices = mesh.devices.reshape(4, 2, 2, 4, 2, 4)
    split = Mesh(devices, ("zq", "zp", "core", "x", "zhi", "y"))
    coil, slab = ("zq", "zp", "core"), ("x", "zhi", "y")
    return jax.shard_map(
        on_device,
        mesh=split,
        in_specs=(
            P(coil, None, None, slab, None),
            P(coil, None, slab, None, None),
            P(coil, None, slab),
            P(None, slab, coil, None),
        ),
        out_specs=P(None, slab, coil, None),
        check_vma=False,
    )
```

```python
import functools
import math

import jax
import jax.numpy as jnp
import ml_dtypes
import numpy as np
from jax import lax
from jax.experimental import pallas as pl
from jax.experimental.pallas import tpu as pltpu
from jax.sharding import Mesh
from jax.sharding import PartitionSpec as P

dual_step = 0.25
primal_step = 0.25
tv_weight = 0.5

COLUMN = ("zq", "x", "zhi", "y")
GROUP = ("zp", "core")
bf16 = jnp.bfloat16
f32 = jnp.float32


def table(length, inverse):
    product = np.outer(np.arange(length), np.arange(length)) % length
    phase = (2.0 * math.pi / length) * product
    real = np.cos(phase) / math.sqrt(length)
    imag = np.sin(phase) / math.sqrt(length) * (1.0 if inverse else -1.0)
    whole = np.stack([np.stack([real, -imag], 1), np.stack([imag, real], 1)])
    return whole.astype(np.float32).astype(ml_dtypes.bfloat16)


def snake(zq, x, zhi, y):
    column = np.zeros((zq, x, zhi, y), np.int32)
    for a in range(zq):
        for h in range(zhi):
            turn = h * zq + a
            for i in range(x):
                for j in range(y):
                    step = i * y + (j if i % 2 == 0 else y - 1 - j)
                    column[a, i, h, j] = turn * x * y + (step if turn % 2 == 0 else x * y - 1 - step)
    return column.reshape(-1)


def dot(a, b):
    return lax.dot_general(a, b, (((1,), (0,)), ((), ())), preferred_element_type=f32)


def dot_t(a, b):
    return lax.dot_general(a, b, (((1,), (1,)), ((), ())), preferred_element_type=f32)


def lanes_to_rows(value, coils):
    n = value.shape[0] // 2
    m = value.shape[1] // coils
    return jnp.concatenate(
        [
            jnp.concatenate([value[p * n : (p + 1) * n, c * m : (c + 1) * m] for p in range(2)], 1)
            for c in range(coils)
        ],
        0,
    )


def to_kspace(maps, image, fz, fy):
    columns = []
    for c in range(maps.shape[0]):
        real, imag = maps[c, 0].astype(f32), maps[c, 1].astype(f32)
        columns.append(
            jnp.concatenate(
                [real * image[0] - imag * image[1], real * image[1] + imag * image[0]], 0
            ).astype(bf16)
        )
    half = dot(fz, jnp.concatenate(columns, 1)).astype(bf16)
    return dot_t(fy, lanes_to_rows(half, maps.shape[0]))


def to_image(dual, maps, gy, gz):
    coils, n = maps.shape[0], maps.shape[2]
    half = dot(gy, dual).astype(bf16)
    field = dot_t(gz, lanes_to_rows(half, coils))
    real_sum, imag_sum = 0.0, 0.0
    for c in range(coils):
        real, imag = maps[c, 0].astype(f32), maps[c, 1].astype(f32)
        m = field.shape[1] // coils
        h_real, h_imag = field[:n, c * m : (c + 1) * m], field[n:, c * m : (c + 1) * m]
        real_sum += real * h_real + imag * h_imag
        imag_sum += real * h_imag - imag * h_real
    return real_sum, imag_sum


def as_lines(data, coils):
    data = data.astype(f32)
    per = data.shape[1] // coils
    return jnp.concatenate(
        [data[:, c * per : (c + 1) * per].reshape(-1, data.shape[2]) for c in range(coils)], 1
    )


def accumulate(sums_ref, out_ref, parts):
    step = pl.program_id(0)

    @pl.when(step == 0)
    def _():
        sums_ref[...] = jnp.zeros_like(sums_ref)

    sums_ref[0] += parts[0]
    sums_ref[1] += parts[1]

    @pl.when(step == pl.num_programs(0) - 1)
    def _():
        out_ref[...] = sums_ref[...].astype(out_ref.dtype)


def spectrum_kernel(maps_ref, image_ref, fz_ref, fy_ref, out_ref):
    out_ref[0] = to_kspace(maps_ref[0], image_ref, fz_ref[...], fy_ref[...])


def first_kernel(spectrum_ref, data_ref, mask_ref, maps_ref, gy_ref, gz_ref, dual_ref, out_ref, sums_ref):
    maps = maps_ref[0]
    data = as_lines(data_ref[0], maps.shape[0])
    mask = mask_ref[0].astype(f32)
    dual = (dual_step * (mask * (spectrum_ref[0] - data))) * (1.0 / (1.0 + dual_step))
    dual_ref[0] = dual
    accumulate(sums_ref, out_ref, to_image(dual.astype(bf16), maps, gy_ref[...], gz_ref[...]))


def second_kernel(
    guess_ref, dual_ref, data_ref, mask_ref, maps_ref, fz_ref, fy_ref, gy_ref, gz_ref, out_ref, sums_ref
):
    maps = maps_ref[0]
    spectrum = to_kspace(maps, guess_ref, fz_ref[...], fy_ref[...])
    data = as_lines(data_ref[0], maps.shape[0])
    mask = mask_ref[0].astype(f32)
    dual = (dual_ref[0] + dual_step * (mask * (spectrum - data))) * (1.0 / (1.0 + dual_step))
    accumulate(sums_ref, out_ref, to_image(dual.astype(bf16), maps, gy_ref[...], gz_ref[...]))


def step_block(a):
    rest = (0,) * (a.ndim - 1)
    return pl.BlockSpec((1, *a.shape[1:]), lambda i: (i, *rest))


def whole_block(a):
    zeros = (0,) * a.ndim
    return pl.BlockSpec(a.shape, lambda i: zeros)


def call(kernel, out, stepped, *operands, sums=None):
    like = jax.tree.leaves(out)
    specs = [step_block(a) if s else whole_block(a) for a, s in zip((*operands, *like), stepped)]
    return pl.pallas_call(
        kernel,
        grid=(next(a.shape[0] for a, s in zip(operands, stepped) if s),),
        in_specs=specs[: len(operands)],
        out_specs=specs[len(operands) :],
        out_shape=like,
        scratch_shapes=[] if sums is None else [pltpu.VMEM(sums, f32)],
        compiler_params=pltpu.CompilerParams(vmem_limit_bytes=40 * 1024 * 1024),
    )(*operands)


def diff_up(a, axis):
    n = a.shape[axis]
    up = lax.slice_in_dim(a, 1, n, axis=axis) - lax.slice_in_dim(a, 0, n - 1, axis=axis)
    return jnp.concatenate([up, jnp.zeros_like(lax.slice_in_dim(a, 0, 1, axis=axis))], axis)


def diff_back(a, axis):
    n = a.shape[axis]
    low = lax.slice_in_dim(a, 0, n - 1, axis=axis)
    return jnp.concatenate([jnp.zeros_like(lax.slice_in_dim(a, 0, 1, axis=axis)), low], axis) - a


def shrink(here, ahead, duals):
    moved = (
        duals[0] + dual_step * diff_up(here, 1),
        duals[1] + dual_step * diff_up(here, 2),
        duals[2] + dual_step * (ahead - here),
    )
    size = jnp.sqrt(sum(jnp.sum(m * m, 0) for m in moved))
    factor = 1.0 / jnp.maximum(1.0, size / tv_weight)
    return tuple(m * factor for m in moved)


def on_device(kspace_data, coil_maps, sample_mask, initial_image):
    coils, _, planes, ny, nx = coil_maps.shape
    nz, lines = kspace_data.shape[2:4]
    rows = initial_image.shape[2]
    sizes = [lax.axis_size(a) for a in COLUMN]
    zq, group = sizes[0], lax.axis_size(GROUP)
    count = math.prod(sizes)
    slabs = count // zq
    column_of = snake(*sizes)
    place_of = np.argsort(column_of)
    me = lax.axis_index(COLUMN)
    is_first, is_last = me == int(place_of[0]), me == int(place_of[-1])
    quarters = sizes[3]

    def spread(blocks):
        return lax.all_to_all(blocks, COLUMN, 0, 0, tiled=True)

    pick = np.eye(nx, dtype=np.float32)[column_of]
    near = [pick, np.roll(pick, -1, 1), np.roll(pick, 1, 1)]
    map_rows = jnp.einsum(
        "wx,iryx->wiry", pick.astype(ml_dtypes.bfloat16), coil_maps.reshape(coils * 2, planes, ny, nx),
        preferred_element_type=f32,
    ).astype(bf16)
    high = initial_image.astype(bf16)
    low = (initial_image - high.astype(f32)).astype(bf16)
    image_rows = jnp.einsum(
        "wx,kx->wk",
        np.concatenate(near).astype(ml_dtypes.bfloat16),
        jnp.concatenate([high.reshape(-1, nx), low.reshape(-1, nx)]),
        preferred_element_type=f32,
    ).astype(bf16)
    half = image_rows.shape[1] // 2
    image_rows = jnp.concatenate(
        [image_rows[:nx], image_rows[nx : 2 * nx, :half], image_rows[2 * nx :, :half]], 1
    ).reshape(nx, 2, 4 * half // 2)
    mask_rows = sample_mask.transpose(0, 2, 1).astype(bf16).reshape(quarters, -1, nz)
    mask_rows = jnp.broadcast_to(mask_rows[None], (count // quarters, *mask_rows.shape))
    extra = jnp.concatenate([image_rows, mask_rows.reshape(nx, -1, nz)], 1)
    first = spread(jnp.concatenate([map_rows, extra[:, None]], 1))

    inv_x = table(nx, True)[:, column_of]
    turned = jnp.einsum(
        "ckzyw,jxkw->xcjyz", kspace_data, inv_x, preferred_element_type=f32
    ).astype(bf16)
    second = spread(turned.reshape(nx, coils * 2 * lines, nz))

    maps = first[:, : 2 * coils].reshape(zq, slabs, coils, 2, planes, ny)
    maps = maps.transpose(0, 2, 3, 1, 4, 5).reshape(zq, coils, 2, nz, ny)

    mask = lax.all_gather(first[:, 2 * coils, 2:], COLUMN[3], axis=0)
    mask = mask.reshape(coils, quarters // coils, zq, slabs, 1, -1, nz)
    mask = jnp.broadcast_to(
        mask.transpose(2, 3, 4, 1, 5, 0, 6), (zq, slabs, 2, quarters // coils, mask.shape[5], coils, nz)
    ).reshape(zq, slabs * 2 * lines, coils * nz)

    image = first[:, 2 * coils, :2].reshape(zq, slabs, 4, 2, planes, rows)
    image = lax.all_gather(image.transpose(2, 3, 1, 4, 0, 5), GROUP, axis=5)
    image = image.reshape(4, 2, nz, ny).astype(f32)
    current = image[0] + image[1]
    before = image[2]
    after = jnp.where(is_last, current, image[3])

    ny_order = np.arange(ny).reshape(slabs, lines)
    fz = table(nz, False).reshape(2 * nz, 2 * nz)
    fy = table(ny, False)[:, ny_order].transpose(1, 0, 2, 3, 4).reshape(2 * ny, 2 * ny)
    gy = table(ny, True)[..., ny_order].transpose(0, 1, 3, 2, 4).reshape(2 * ny, 2 * ny)
    gz = table(nz, True).reshape(2 * nz, 2 * nz)
    dual_like = jax.ShapeDtypeStruct((zq, 2 * ny, coils * nz), f32)
    image_like = jax.ShapeDtypeStruct((2, nz, ny), bf16)

    spectrum = call(spectrum_kernel, dual_like, (1, 0, 0, 0, 1), maps, current, fz, fy)[0]
    zero = jnp.zeros_like(current)
    duals = shrink(current, after, (zero,) * 3)
    duals_before = shrink(before, current, (zero,) * 3)

    def tv_gradient():
        return (
            diff_back(duals[0], 1)
            + diff_back(duals[1], 2)
            + jnp.where(is_first, 0.0, duals_before[2])
            - duals[2]
        )

    settled = current - primal_step * tv_gradient()
    data = second.reshape(zq, slabs, coils * 2 * lines, nz)
    dual, grad = call(
        first_kernel, (dual_like, image_like), (1, 1, 1, 1, 0, 0, 1, 0),
        spectrum, data, mask, maps, gy, gz, sums=image_like.shape,
    )
    grad = lax.all_gather(grad, GROUP, axis=0).astype(f32).sum(0)
    updated = settled - primal_step * grad
    guess = 2.0 * updated - current

    forth = [(int(place_of[i]), int(place_of[i + 1])) for i in range(count - 1)]
    before = lax.ppermute(guess, COLUMN, forth)
    after = jnp.where(is_last, guess, lax.ppermute(guess, COLUMN, [(b, a) for a, b in forth]))
    (grad,) = call(
        second_kernel, image_like, (0, 1, 1, 1, 1, 0, 0, 0, 0, 0),
        guess, dual, data, mask, maps, fz, fy, gy, gz, sums=image_like.shape,
    )
    grad = grad.reshape(2, nz, zq, group, rows).transpose(3, 0, 1, 2, 4)
    grad = lax.all_to_all(grad, GROUP, 0, 0, tiled=True).astype(f32).sum(0)

    duals = shrink(guess, after, duals)
    duals_before = shrink(before, guess, duals_before)
    rest = (updated - primal_step * tv_gradient()).reshape(2, nz, zq, group, rows)
    rest = lax.dynamic_index_in_dim(rest, lax.axis_index(GROUP), 3, keepdims=False)
    result = rest - primal_step * grad
    result = result.reshape(2, slabs, planes, zq, rows).transpose(3, 1, 0, 2, 4)
    result = spread(result.reshape(count, 2 * planes * rows))
    return result[place_of].T.reshape(2, planes, rows, nx)


def solution(mesh):
    devices = mesh.devices.reshape(4, 2, 2, 4, 2, 4)
    split = Mesh(devices, ("zq", "zp", "core", "x", "zhi", "y"))
    coil, slab = ("zq", "zp", "core"), ("x", "zhi", "y")
    return jax.shard_map(
        on_device,
        mesh=split,
        in_specs=(
            P(coil, None, None, slab, None),
            P(coil, None, slab, None, None),
            P(coil, None, slab),
            P(None, slab, coil, None),
        ),
        out_specs=P(None, slab, coil, None),
        check_vma=False,
    )
```

```python
import math

import jax
import jax.numpy as jnp
import ml_dtypes
import numpy as np
from jax import lax
from jax.experimental import pallas as pl
from jax.experimental.pallas import tpu as pltpu
from jax.sharding import Mesh
from jax.sharding import PartitionSpec as P

dual_step = 0.25
primal_step = 0.25
tv_weight = 0.5

COLUMN = ("zq", "x", "zhi", "y")
GROUP = ("zp", "core")
bf16 = jnp.bfloat16
f32 = jnp.float32


def table(length, inverse):
    product = np.outer(np.arange(length), np.arange(length)) % length
    phase = (2.0 * math.pi / length) * product
    real = np.cos(phase) / math.sqrt(length)
    imag = np.sin(phase) / math.sqrt(length) * (1.0 if inverse else -1.0)
    whole = np.stack([np.stack([real, -imag], 1), np.stack([imag, real], 1)])
    return whole.astype(np.float32).astype(ml_dtypes.bfloat16)


def snake(zq, x, zhi, y):
    column = np.zeros((zq, x, zhi, y), np.int32)
    for a in range(zq):
        for h in range(zhi):
            turn = h * zq + a
            for i in range(x):
                for j in range(y):
                    step = i * y + (j if i % 2 == 0 else y - 1 - j)
                    column[a, i, h, j] = turn * x * y + (step if turn % 2 == 0 else x * y - 1 - step)
    return column.reshape(-1)


def dot(a, b):
    return lax.dot_general(a, b, (((1,), (0,)), ((), ())), preferred_element_type=f32)


def dot_t(a, b):
    return lax.dot_general(a, b, (((1,), (1,)), ((), ())), preferred_element_type=f32)


def lanes_to_rows(value, coils):
    n = value.shape[0] // 2
    m = value.shape[1] // coils
    return jnp.concatenate(
        [
            jnp.concatenate([value[p * n : (p + 1) * n, c * m : (c + 1) * m] for p in range(2)], 1)
            for c in range(coils)
        ],
        0,
    )


def to_kspace(maps, image, fz, fy):
    columns = []
    for real, imag in maps:
        columns.append(
            jnp.concatenate(
                [real * image[0] - imag * image[1], real * image[1] + imag * image[0]], 0
            ).astype(bf16)
        )
    half = dot(fz, jnp.concatenate(columns, 1)).astype(bf16)
    return dot_t(fy, lanes_to_rows(half, len(maps)))


def to_image(dual, maps, gy, gz):
    coils, n = len(maps), maps[0][0].shape[0]
    half = dot(gy, dual).astype(bf16)
    field = dot_t(gz, lanes_to_rows(half, coils))
    real_sum, imag_sum = 0.0, 0.0
    for c, (real, imag) in enumerate(maps):
        m = field.shape[1] // coils
        h_real, h_imag = field[:n, c * m : (c + 1) * m], field[n:, c * m : (c + 1) * m]
        real_sum += real * h_real + imag * h_imag
        imag_sum += real * h_imag - imag * h_real
    return real_sum, imag_sum


def accumulate(sums_ref, out_ref, parts):
    step = pl.program_id(0)

    @pl.when(step == 0)
    def _():
        sums_ref[...] = jnp.zeros_like(sums_ref)

    sums_ref[0] += parts[0]
    sums_ref[1] += parts[1]

    @pl.when(step == pl.num_programs(0) - 1)
    def _():
        out_ref[...] = sums_ref[...].astype(out_ref.dtype)


def split_blocks(block_ref, coils):
    n = block_ref.shape[1]

    def lane(i):
        return block_ref[0, :, i * n : (i + 1) * n].astype(f32)

    maps = [[lane(2 * c + p) for p in range(2)] for c in range(coils)]
    data = jnp.concatenate(
        [
            jnp.concatenate([lane(2 * coils + 2 * c + p) for c in range(coils)], 1)
            for p in range(2)
        ],
        0,
    )
    return maps, data


def masked(mask_ref, value):
    mask = mask_ref[0].astype(f32)
    return jnp.concatenate([mask, mask], 0) * value


def shifted(a, axis, step):
    n = a.shape[axis]
    if step > 0:
        pieces = (lax.slice_in_dim(a, 1, n, axis=axis), lax.slice_in_dim(a, 0, 1, axis=axis))
    else:
        pieces = (lax.slice_in_dim(a, n - 1, n, axis=axis), lax.slice_in_dim(a, 0, n - 1, axis=axis))
    return jnp.concatenate(pieces, axis)


def position(shape, axis):
    return lax.broadcasted_iota(jnp.int32, shape, axis)


def shrink(here, ahead, duals):
    moved = []
    for p in range(2):
        a = here[p]
        up_z = jnp.where(position(a.shape, 0) < a.shape[0] - 1, shifted(a, 0, 1) - a, 0.0)
        up_y = jnp.where(position(a.shape, 1) < a.shape[1] - 1, shifted(a, 1, 1) - a, 0.0)
        steps = [dual_step * up_z, dual_step * up_y, dual_step * (ahead[p] - a)]
        moved.append(steps if duals is None else [d + s for d, s in zip(duals[p], steps)])
    size = jnp.sqrt(sum(m * m for part in moved for m in part))
    factor = 1.0 / jnp.maximum(1.0, size / tv_weight)
    return [[m * factor for m in part] for part in moved]


def divergence(duals, duals_before, has_before):
    sums = []
    for p in range(2):
        d_z, d_y, d_x = duals[p]
        back_z = jnp.where(position(d_z.shape, 0) > 0, shifted(d_z, 0, -1), 0.0)
        back_y = jnp.where(position(d_y.shape, 1) > 0, shifted(d_y, 1, -1), 0.0)
        sums.append((back_z - d_z) + (back_y - d_y) + (has_before * duals_before[p][2] - d_x))
    return sums


def read_start(edge_ref, start_ref):
    here = [start_ref[0, p].astype(f32) + start_ref[1, p].astype(f32) for p in range(2)]
    before = [start_ref[2, p].astype(f32) for p in range(2)]
    has_after = edge_ref[1]
    after = [jnp.where(has_after > 0.0, start_ref[3, p].astype(f32), here[p]) for p in range(2)]
    return before, here, after


def first_kernel(
    edge_ref, start_ref, block_ref, mask_ref, fz_ref, fy_ref, gy_ref, gz_ref,
    dual_ref, out_ref, settled_ref, image_ref, sums_ref,
):
    @pl.when(pl.program_id(0) == 0)
    def _():
        before, here, after = read_start(edge_ref, start_ref)
        spread = divergence(shrink(here, after, None), shrink(before, here, None), edge_ref[0])
        for p in range(2):
            image_ref[p] = here[p]
            settled_ref[p] = here[p] - primal_step * spread[p]

    maps, data = split_blocks(block_ref, mask_ref.shape[2] // mask_ref.shape[1])
    spectrum = to_kspace(maps, image_ref, fz_ref[...], fy_ref[...])
    dual = (dual_step * masked(mask_ref, spectrum - data)) * (1.0 / (1.0 + dual_step))
    dual_ref[0] = dual
    accumulate(sums_ref, out_ref, to_image(dual.astype(bf16), maps, gy_ref[...], gz_ref[...]))


def second_kernel(
    guess_ref, dual_ref, block_ref, mask_ref, fz_ref, fy_ref, gy_ref, gz_ref, out_ref, sums_ref
):
    maps, data = split_blocks(block_ref, mask_ref.shape[2] // mask_ref.shape[1])
    spectrum = to_kspace(maps, guess_ref, fz_ref[...], fy_ref[...])
    dual = (dual_ref[0] + dual_step * masked(mask_ref, spectrum - data)) * (1.0 / (1.0 + dual_step))
    accumulate(sums_ref, out_ref, to_image(dual.astype(bf16), maps, gy_ref[...], gz_ref[...]))


def last_kernel(edge_ref, start_ref, updated_ref, guess_ref, before_ref, after_ref, out_ref):
    old_before, old_here, old_after = read_start(edge_ref, start_ref)
    has_after = edge_ref[1]
    here = [guess_ref[p] for p in range(2)]
    before = [before_ref[p] for p in range(2)]
    after = [jnp.where(has_after > 0.0, after_ref[p], here[p]) for p in range(2)]
    duals = shrink(here, after, shrink(old_here, old_after, None))
    duals_before = shrink(before, here, shrink(old_before, old_here, None))
    spread = divergence(duals, duals_before, edge_ref[0])
    for p in range(2):
        out_ref[p] = updated_ref[p] - primal_step * spread[p]


def step_block(a):
    rest = (0,) * (a.ndim - 1)
    return pl.BlockSpec((1, *a.shape[1:]), lambda i: (i, *rest))


def whole_block(a):
    if a.ndim == 1:
        return pl.BlockSpec(memory_space=pltpu.SMEM)
    zeros = (0,) * a.ndim
    return pl.BlockSpec(a.shape, lambda i: zeros)


def call(kernel, outs, stepped, *operands, steps, scratch=()):
    specs = [step_block(a) if s else whole_block(a) for a, s in zip((*operands, *outs), stepped)]
    return pl.pallas_call(
        kernel,
        grid=(steps,),
        in_specs=specs[: len(operands)],
        out_specs=specs[len(operands) :],
        out_shape=outs,
        scratch_shapes=[pltpu.VMEM(shape, f32) for shape in scratch],
        compiler_params=pltpu.CompilerParams(vmem_limit_bytes=40 * 1024 * 1024),
    )(*operands)


def on_device(kspace_data, coil_maps, sample_mask, initial_image):
    coils, _, planes, ny, nx = coil_maps.shape
    nz, lines = kspace_data.shape[2:4]
    rows = initial_image.shape[2]
    sizes = [lax.axis_size(a) for a in COLUMN]
    zq, group = sizes[0], lax.axis_size(GROUP)
    count = math.prod(sizes)
    slabs = count // zq
    column_of = snake(*sizes)
    place_of = np.argsort(column_of)
    me = lax.axis_index(COLUMN)
    is_first, is_last = me == int(place_of[0]), me == int(place_of[-1])
    quarters = sizes[3]

    def spread(blocks):
        return lax.all_to_all(blocks, COLUMN, 0, 0, tiled=True)

    pick = np.eye(nx, dtype=np.float32)[column_of]
    near = [pick, np.roll(pick, -1, 1), np.roll(pick, 1, 1)]
    map_rows = jnp.einsum(
        "wx,iryx->wriy", pick.astype(ml_dtypes.bfloat16), coil_maps.reshape(coils * 2, planes, ny, nx),
        preferred_element_type=f32,
    ).astype(bf16)
    inv_x = table(nx, True)[:, column_of]
    turned = jnp.einsum(
        "ckzyw,jxkw->xycjz", kspace_data, inv_x, preferred_element_type=f32
    ).astype(bf16)
    high = initial_image.astype(bf16)
    low = (initial_image - high.astype(f32)).astype(bf16)
    image_rows = jnp.einsum(
        "wx,kx->wk",
        np.concatenate(near).astype(ml_dtypes.bfloat16),
        jnp.concatenate([high.reshape(-1, nx), low.reshape(-1, nx)]),
        preferred_element_type=f32,
    ).astype(bf16)
    half = image_rows.shape[1] // 2
    image_rows = jnp.concatenate(
        [image_rows[:nx], image_rows[nx : 2 * nx, :half], image_rows[2 * nx :, :half]], 1
    ).reshape(nx, 2, 2 * half)
    mask_rows = sample_mask.transpose(0, 2, 1).astype(bf16).reshape(quarters, -1, nz)
    mask_rows = jnp.broadcast_to(mask_rows[None], (count // quarters, *mask_rows.shape))
    extra = jnp.concatenate([image_rows, mask_rows.reshape(nx, -1, nz)], 1)
    lanes = coils * 2 * ny
    blocks = spread(
        jnp.concatenate([map_rows.reshape(nx, planes, lanes), turned.reshape(nx, lines, lanes), extra], 2)
    )
    extra = blocks[:, :, 2 * lanes :]
    blocks = blocks.reshape(zq, nz, -1)

    mask = lax.all_gather(extra[:, 2:], COLUMN[3], axis=0)
    mask = mask.reshape(coils, quarters // coils, zq, slabs, -1, nz)
    mask = mask.transpose(2, 3, 1, 4, 0, 5).reshape(zq, slabs * lines, coils * nz)

    start = extra[:, :2].reshape(zq, slabs, 4, 2, planes, rows)
    start = lax.all_gather(start.transpose(2, 3, 1, 4, 0, 5), GROUP, axis=5)
    start = start.reshape(4, 2, nz, ny)
    edge = jnp.stack([1.0 - is_first.astype(f32), 1.0 - is_last.astype(f32)])

    fz, fy = (table(n, False).reshape(2 * n, 2 * n) for n in (nz, ny))
    gy, gz = (table(n, True).reshape(2 * n, 2 * n) for n in (ny, nz))
    dual_like = jax.ShapeDtypeStruct((zq, 2 * ny, coils * nz), f32)
    grad_like = jax.ShapeDtypeStruct((2, nz, ny), bf16)
    image_like = jax.ShapeDtypeStruct((2, nz, ny), f32)

    dual, grad, settled, current = call(
        first_kernel, (dual_like, grad_like, image_like, image_like), (0, 0, 1, 1, 0, 0, 0, 0, 1, 0, 0, 0),
        edge, start, blocks, mask, fz, fy, gy, gz, steps=zq, scratch=[image_like.shape],
    )
    grad = lax.all_gather(grad, GROUP, axis=0).astype(f32).sum(0)
    updated = settled - primal_step * grad
    guess = 2.0 * updated - current

    forth = [(int(place_of[i]), int(place_of[i + 1])) for i in range(count - 1)]
    before = lax.ppermute(guess, COLUMN, forth)
    after = lax.ppermute(guess, COLUMN, [(b, a) for a, b in forth])
    (grad,) = call(
        second_kernel, (grad_like,), (0, 1, 1, 1, 0, 0, 0, 0, 0),
        guess, dual, blocks, mask, fz, fy, gy, gz, steps=zq, scratch=[image_like.shape],
    )
    grad = grad.reshape(2, nz, zq, group, rows).transpose(3, 0, 1, 2, 4)
    grad = lax.all_to_all(grad, GROUP, 0, 0, tiled=True).astype(f32).sum(0)

    (rest,) = call(
        last_kernel, (image_like,), (0,) * 7, edge, start, updated, guess, before, after, steps=1
    )
    rest = rest.reshape(2, nz, zq, group, rows)
    rest = lax.dynamic_index_in_dim(rest, lax.axis_index(GROUP), 3, keepdims=False)
    result = rest - primal_step * grad
    result = result.reshape(2, slabs, planes, zq, rows).transpose(3, 1, 0, 2, 4)
    result = spread(result.reshape(count, 2 * planes * rows))
    return result[place_of].T.reshape(2, planes, rows, nx)


def solution(mesh):
    devices = mesh.devices.reshape(4, 2, 2, 4, 2, 4)
    split = Mesh(devices, ("zq", "zp", "core", "x", "zhi", "y"))
    coil, slab = ("zq", "zp", "core"), ("x", "zhi", "y")
    return jax.shard_map(
        on_device,
        mesh=split,
        in_specs=(
            P(coil, None, None, slab, None),
            P(coil, None, slab, None, None),
            P(coil, None, slab),
            P(None, slab, coil, None),
        ),
        out_specs=P(None, slab, coil, None),
        check_vma=False,
    )
```

```python
import math

import jax
import jax.numpy as jnp
import ml_dtypes
import numpy as np
from jax import lax
from jax.experimental import pallas as pl
from jax.experimental.pallas import tpu as pltpu
from jax.sharding import Mesh
from jax.sharding import PartitionSpec as P

dual_step = 0.25
primal_step = 0.25
tv_weight = 0.5

COLUMN = ("zq", "x", "zhi", "y")
GROUP = ("zp", "core")
bf16 = jnp.bfloat16
f32 = jnp.float32


def table(length, inverse):
    product = np.outer(np.arange(length), np.arange(length)) % length
    phase = (2.0 * math.pi / length) * product
    real = np.cos(phase) / math.sqrt(length)
    imag = np.sin(phase) / math.sqrt(length) * (1.0 if inverse else -1.0)
    whole = np.stack([np.stack([real, -imag], 1), np.stack([imag, real], 1)])
    return whole.astype(np.float32).astype(ml_dtypes.bfloat16)


def snake(zq, x, zhi, y):
    column = np.zeros((zq, x, zhi, y), np.int32)
    for a in range(zq):
        for h in range(zhi):
            turn = h * zq + a
            for i in range(x):
                for j in range(y):
                    step = i * y + (j if i % 2 == 0 else y - 1 - j)
                    column[a, i, h, j] = turn * x * y + (step if turn % 2 == 0 else x * y - 1 - step)
    return column.reshape(-1)


def dot(a, b):
    return lax.dot_general(a, b, (((1,), (0,)), ((), ())), preferred_element_type=f32)


def dot_t(a, b):
    return lax.dot_general(a, b, (((1,), (1,)), ((), ())), preferred_element_type=f32)


def lanes_to_rows(value, coils):
    n = value.shape[0] // 2
    m = value.shape[1] // coils
    return jnp.concatenate(
        [
            jnp.concatenate([value[p * n : (p + 1) * n, c * m : (c + 1) * m] for p in range(2)], 1)
            for c in range(coils)
        ],
        0,
    )


def to_kspace(maps, image, fz, fy):
    columns = []
    for real, imag in maps:
        columns.append(
            jnp.concatenate(
                [real * image[0] - imag * image[1], real * image[1] + imag * image[0]], 0
            ).astype(bf16)
        )
    half = dot(fz, jnp.concatenate(columns, 1)).astype(bf16)
    return dot_t(fy, lanes_to_rows(half, len(maps)))


def to_image(dual, maps, gy, gz):
    coils, n = len(maps), maps[0][0].shape[0]
    half = dot(gy, dual).astype(bf16)
    field = dot_t(gz, lanes_to_rows(half, coils))
    real_sum, imag_sum = 0.0, 0.0
    for c, (real, imag) in enumerate(maps):
        m = field.shape[1] // coils
        h_real, h_imag = field[:n, c * m : (c + 1) * m], field[n:, c * m : (c + 1) * m]
        real_sum += real * h_real + imag * h_imag
        imag_sum += real * h_imag - imag * h_real
    return real_sum, imag_sum


def accumulate(sums_ref, out_ref, parts):
    step = pl.program_id(0)

    @pl.when(step == 0)
    def _():
        sums_ref[...] = jnp.zeros_like(sums_ref)

    sums_ref[0] += parts[0]
    sums_ref[1] += parts[1]

    @pl.when(step == pl.num_programs(0) - 1)
    def _():
        out_ref[...] = sums_ref[...].astype(out_ref.dtype)


def split_blocks(block_ref, coils):
    n = block_ref.shape[1]

    def lane(i):
        return block_ref[0, :, i * n : (i + 1) * n].astype(f32)

    maps = [[lane(2 * c + p) for p in range(2)] for c in range(coils)]
    data = jnp.concatenate(
        [
            jnp.concatenate([lane(2 * coils + 2 * c + p) for c in range(coils)], 1)
            for p in range(2)
        ],
        0,
    )
    return maps, data


def masked(mask_ref, value):
    mask = mask_ref[0].astype(f32)
    return jnp.concatenate([mask, mask], 0) * value


def shifted(a, axis, step):
    n = a.shape[axis]
    if step > 0:
        pieces = (lax.slice_in_dim(a, 1, n, axis=axis), lax.slice_in_dim(a, 0, 1, axis=axis))
    else:
        pieces = (lax.slice_in_dim(a, n - 1, n, axis=axis), lax.slice_in_dim(a, 0, n - 1, axis=axis))
    return jnp.concatenate(pieces, axis)


def position(shape, axis):
    return lax.broadcasted_iota(jnp.int32, shape, axis)


def shrink(here, ahead, duals):
    moved = []
    for p in range(2):
        a = here[p]
        up_z = jnp.where(position(a.shape, 0) < a.shape[0] - 1, shifted(a, 0, 1) - a, 0.0)
        up_y = jnp.where(position(a.shape, 1) < a.shape[1] - 1, shifted(a, 1, 1) - a, 0.0)
        steps = [dual_step * up_z, dual_step * up_y, dual_step * (ahead[p] - a)]
        moved.append(steps if duals is None else [d + s for d, s in zip(duals[p], steps)])
    size = jnp.sqrt(sum(m * m for part in moved for m in part))
    factor = 1.0 / jnp.maximum(1.0, size / tv_weight)
    return [[m * factor for m in part] for part in moved]


def divergence(duals, duals_before, has_before):
    sums = []
    for p in range(2):
        d_z, d_y, d_x = duals[p]
        back_z = jnp.where(position(d_z.shape, 0) > 0, shifted(d_z, 0, -1), 0.0)
        back_y = jnp.where(position(d_y.shape, 1) > 0, shifted(d_y, 1, -1), 0.0)
        sums.append((back_z - d_z) + (back_y - d_y) + (has_before * duals_before[p][2] - d_x))
    return sums


def read_start(edge_ref, start_ref):
    here = [start_ref[0, p].astype(f32) + start_ref[1, p].astype(f32) for p in range(2)]
    before = [start_ref[2, p].astype(f32) for p in range(2)]
    has_after = edge_ref[1]
    after = [jnp.where(has_after > 0.0, start_ref[3, p].astype(f32), here[p]) for p in range(2)]
    return before, here, after


def spectrum_kernel(edge_ref, start_ref, block_ref, fz_ref, fy_ref, spectrum_ref, settled_ref, image_ref):
    @pl.when(pl.program_id(0) == 0)
    def _():
        before, here, after = read_start(edge_ref, start_ref)
        spread = divergence(shrink(here, after, None), shrink(before, here, None), edge_ref[0])
        for p in range(2):
            image_ref[p] = here[p]
            settled_ref[p] = here[p] - primal_step * spread[p]

    maps, data = split_blocks(block_ref, spectrum_ref.shape[2] // block_ref.shape[1])
    spectrum_ref[0] = to_kspace(maps, image_ref, fz_ref[...], fy_ref[...]) - data


def first_kernel(spectrum_ref, block_ref, mask_ref, gy_ref, gz_ref, dual_ref, out_ref, sums_ref):
    maps, _ = split_blocks(block_ref, mask_ref.shape[2] // mask_ref.shape[1])
    dual = (dual_step * masked(mask_ref, spectrum_ref[0])) * (1.0 / (1.0 + dual_step))
    dual_ref[0] = dual
    accumulate(sums_ref, out_ref, to_image(dual.astype(bf16), maps, gy_ref[...], gz_ref[...]))


def second_kernel(
    guess_ref, dual_ref, block_ref, mask_ref, fz_ref, fy_ref, gy_ref, gz_ref, out_ref, sums_ref
):
    maps, data = split_blocks(block_ref, mask_ref.shape[2] // mask_ref.shape[1])
    spectrum = to_kspace(maps, guess_ref, fz_ref[...], fy_ref[...])
    dual = (dual_ref[0] + dual_step * masked(mask_ref, spectrum - data)) * (1.0 / (1.0 + dual_step))
    accumulate(sums_ref, out_ref, to_image(dual.astype(bf16), maps, gy_ref[...], gz_ref[...]))


def last_kernel(edge_ref, start_ref, updated_ref, guess_ref, before_ref, after_ref, out_ref):
    old_before, old_here, old_after = read_start(edge_ref, start_ref)
    has_after = edge_ref[1]
    here = [guess_ref[p] for p in range(2)]
    before = [before_ref[p] for p in range(2)]
    after = [jnp.where(has_after > 0.0, after_ref[p], here[p]) for p in range(2)]
    duals = shrink(here, after, shrink(old_here, old_after, None))
    duals_before = shrink(before, here, shrink(old_before, old_here, None))
    spread = divergence(duals, duals_before, edge_ref[0])
    for p in range(2):
        out_ref[p] = updated_ref[p] - primal_step * spread[p]


def step_block(a):
    rest = (0,) * (a.ndim - 1)
    return pl.BlockSpec((1, *a.shape[1:]), lambda i: (i, *rest))


def whole_block(a):
    if a.ndim == 1:
        return pl.BlockSpec(memory_space=pltpu.SMEM)
    zeros = (0,) * a.ndim
    return pl.BlockSpec(a.shape, lambda i: zeros)


def call(kernel, outs, stepped, *operands, steps, scratch=()):
    specs = [step_block(a) if s else whole_block(a) for a, s in zip((*operands, *outs), stepped)]
    return pl.pallas_call(
        kernel,
        grid=(steps,),
        in_specs=specs[: len(operands)],
        out_specs=specs[len(operands) :],
        out_shape=outs,
        scratch_shapes=[pltpu.VMEM(shape, f32) for shape in scratch],
        compiler_params=pltpu.CompilerParams(vmem_limit_bytes=40 * 1024 * 1024),
    )(*operands)


def on_device(kspace_data, coil_maps, sample_mask, initial_image):
    coils, _, planes, ny, nx = coil_maps.shape
    nz, lines = kspace_data.shape[2:4]
    rows = initial_image.shape[2]
    sizes = [lax.axis_size(a) for a in COLUMN]
    zq, group = sizes[0], lax.axis_size(GROUP)
    count = math.prod(sizes)
    slabs = count // zq
    column_of = snake(*sizes)
    place_of = np.argsort(column_of)
    me = lax.axis_index(COLUMN)
    is_first, is_last = me == int(place_of[0]), me == int(place_of[-1])
    quarters = sizes[3]

    def spread(blocks):
        return lax.all_to_all(blocks, COLUMN, 0, 0, tiled=True)

    pick = np.eye(nx, dtype=np.float32)[column_of]
    near = [pick, np.roll(pick, -1, 1), np.roll(pick, 1, 1)]
    map_rows = jnp.einsum(
        "wx,iryx->wriy", pick.astype(ml_dtypes.bfloat16), coil_maps.reshape(coils * 2, planes, ny, nx),
        preferred_element_type=f32,
    ).astype(bf16)
    inv_x = table(nx, True)[:, column_of]
    turned = jnp.einsum(
        "ckzyw,jxkw->xycjz", kspace_data, inv_x, preferred_element_type=f32
    ).astype(bf16)
    high = initial_image.astype(bf16)
    low = (initial_image - high.astype(f32)).astype(bf16)
    image_rows = jnp.einsum(
        "wx,kx->wk",
        np.concatenate(near).astype(ml_dtypes.bfloat16),
        jnp.concatenate([high.reshape(-1, nx), low.reshape(-1, nx)]),
        preferred_element_type=f32,
    ).astype(bf16)
    half = image_rows.shape[1] // 2
    image_rows = jnp.concatenate(
        [image_rows[:nx], image_rows[nx : 2 * nx, :half], image_rows[2 * nx :, :half]], 1
    ).reshape(nx, 2, 2 * half)
    mask_rows = sample_mask.transpose(0, 2, 1).astype(bf16).reshape(quarters, -1, nz)
    mask_rows = jnp.broadcast_to(mask_rows[None], (count // quarters, *mask_rows.shape))
    extra = jnp.concatenate([image_rows, mask_rows.reshape(nx, -1, nz)], 1)
    lanes = coils * 2 * ny
    blocks = spread(
        jnp.concatenate([map_rows.reshape(nx, planes, lanes), turned.reshape(nx, lines, lanes), extra], 2)
    )
    extra = blocks[:, :, 2 * lanes :]
    blocks = blocks.reshape(zq, nz, -1)

    def gather(part, axis):
        copies = jnp.broadcast_to(part[None], (lax.axis_size(axis), *part.shape))
        return lax.all_to_all(copies, axis, 0, 0, tiled=True)

    start = extra[:, :2].reshape(zq, slabs, 4, 2, planes, rows)
    start = gather(start.transpose(2, 3, 1, 4, 0, 5).reshape(4, 2, nz, zq * rows), GROUP)
    mask = extra[:, 2:].reshape(zq, slabs, -1, nz)
    start, mask = lax.optimization_barrier((start, mask))
    mask = gather(mask, COLUMN[3])
    start = start.reshape(group, 4, 2, nz, zq, rows).transpose(1, 2, 3, 4, 0, 5).reshape(4, 2, nz, ny)
    mask = mask.reshape(coils, quarters // coils, zq, slabs, -1, nz)
    mask = mask.transpose(2, 3, 1, 4, 0, 5).reshape(zq, slabs * lines, coils * nz)
    edge = jnp.stack([1.0 - is_first.astype(f32), 1.0 - is_last.astype(f32)])

    fz, fy = (table(n, False).reshape(2 * n, 2 * n) for n in (nz, ny))
    gy, gz = (table(n, True).reshape(2 * n, 2 * n) for n in (ny, nz))
    dual_like = jax.ShapeDtypeStruct((zq, 2 * ny, coils * nz), f32)
    grad_like = jax.ShapeDtypeStruct((2, nz, ny), bf16)
    image_like = jax.ShapeDtypeStruct((2, nz, ny), f32)

    spectrum, settled, current = call(
        spectrum_kernel, (dual_like, image_like, image_like), (0, 0, 1, 0, 0, 1, 0, 0),
        edge, start, blocks, fz, fy, steps=zq,
    )
    dual, grad = call(
        first_kernel, (dual_like, grad_like), (1, 1, 1, 0, 0, 1, 0),
        spectrum, blocks, mask, gy, gz, steps=zq, scratch=[image_like.shape],
    )
    grad = lax.all_gather(grad, GROUP, axis=0).astype(f32).sum(0)
    updated = settled - primal_step * grad
    guess = 2.0 * updated - current

    forth = [(int(place_of[i]), int(place_of[i + 1])) for i in range(count - 1)]
    before = lax.ppermute(guess, COLUMN, forth)
    after = lax.ppermute(guess, COLUMN, [(b, a) for a, b in forth])
    (grad,) = call(
        second_kernel, (grad_like,), (0, 1, 1, 1, 0, 0, 0, 0, 0),
        guess, dual, blocks, mask, fz, fy, gy, gz, steps=zq, scratch=[image_like.shape],
    )
    grad = grad.reshape(2, nz, zq, group, rows).transpose(3, 0, 1, 2, 4)
    grad = lax.all_to_all(grad, GROUP, 0, 0, tiled=True).astype(f32).sum(0)

    (rest,) = call(
        last_kernel, (image_like,), (0,) * 7, edge, start, updated, guess, before, after, steps=1
    )
    rest = rest.reshape(2, nz, zq, group, rows)
    rest = lax.dynamic_index_in_dim(rest, lax.axis_index(GROUP), 3, keepdims=False)
    result = rest - primal_step * grad
    result = result.reshape(2, slabs, planes, zq, rows).transpose(3, 1, 0, 2, 4)
    result = spread(result.reshape(count, 2 * planes * rows))
    result = lax.dot_general(
        result, pick, (((0,), (0,)), ((), ())), precision=lax.Precision.HIGHEST, preferred_element_type=f32
    )
    return result.reshape(2, planes, rows, nx)


def solution(mesh):
    devices = mesh.devices.reshape(4, 2, 2, 4, 2, 4)
    split = Mesh(devices, ("zq", "zp", "core", "x", "zhi", "y"))
    coil, slab = ("zq", "zp", "core"), ("x", "zhi", "y")
    return jax.shard_map(
        on_device,
        mesh=split,
        in_specs=(
            P(coil, None, None, slab, None),
            P(coil, None, slab, None, None),
            P(coil, None, slab),
            P(None, slab, coil, None),
        ),
        out_specs=P(None, slab, coil, None),
        check_vma=False,
    )
```

```python
import math

import jax
import jax.numpy as jnp
import ml_dtypes
import numpy as np
from jax import lax
from jax.experimental import pallas as pl
from jax.experimental.pallas import tpu as pltpu
from jax.sharding import Mesh
from jax.sharding import PartitionSpec as P

dual_step = 0.25
primal_step = 0.25
tv_weight = 0.5

COLUMN = ("zq", "x", "zhi", "y")
GROUP = ("zp", "core")
bf16 = jnp.bfloat16
f32 = jnp.float32


def table(length, inverse):
    product = np.outer(np.arange(length), np.arange(length)) % length
    phase = (2.0 * math.pi / length) * product
    real = np.cos(phase) / math.sqrt(length)
    imag = np.sin(phase) / math.sqrt(length) * (1.0 if inverse else -1.0)
    whole = np.stack([np.stack([real, -imag], 1), np.stack([imag, real], 1)])
    return whole.astype(np.float32).astype(ml_dtypes.bfloat16)


def snake(zq, x, zhi, y):
    column = np.zeros((zq, x, zhi, y), np.int32)
    for a in range(zq):
        for h in range(zhi):
            turn = h * zq + a
            for i in range(x):
                for j in range(y):
                    step = i * y + (j if i % 2 == 0 else y - 1 - j)
                    column[a, i, h, j] = turn * x * y + (step if turn % 2 == 0 else x * y - 1 - step)
    return column.reshape(-1)


def dot(a, b):
    return lax.dot_general(a, b, (((1,), (0,)), ((), ())), preferred_element_type=f32)


def dot_t(a, b):
    return lax.dot_general(a, b, (((1,), (1,)), ((), ())), preferred_element_type=f32)


def lanes_to_rows(value, coils):
    n = value.shape[0] // 2
    m = value.shape[1] // coils
    return jnp.concatenate(
        [
            jnp.concatenate([value[p * n : (p + 1) * n, c * m : (c + 1) * m] for p in range(2)], 1)
            for c in range(coils)
        ],
        0,
    )


def to_kspace(maps, image, fz, fy):
    columns = []
    for real, imag in maps:
        columns.append(
            jnp.concatenate(
                [real * image[0] - imag * image[1], real * image[1] + imag * image[0]], 0
            ).astype(bf16)
        )
    half = dot(fz, jnp.concatenate(columns, 1)).astype(bf16)
    return dot_t(fy, lanes_to_rows(half, len(maps)))


def to_image(dual, maps, gy, gz):
    coils, n = len(maps), maps[0][0].shape[0]
    half = dot(gy, dual).astype(bf16)
    field = dot_t(gz, lanes_to_rows(half, coils))
    real_sum, imag_sum = 0.0, 0.0
    for c, (real, imag) in enumerate(maps):
        m = field.shape[1] // coils
        h_real, h_imag = field[:n, c * m : (c + 1) * m], field[n:, c * m : (c + 1) * m]
        real_sum += real * h_real + imag * h_imag
        imag_sum += real * h_imag - imag * h_real
    return real_sum, imag_sum


def accumulate(sums_ref, out_ref, parts):
    step = pl.program_id(0)

    @pl.when(step == 0)
    def _():
        sums_ref[...] = jnp.zeros_like(sums_ref)

    sums_ref[0] += parts[0]
    sums_ref[1] += parts[1]

    @pl.when(step == pl.num_programs(0) - 1)
    def _():
        out_ref[...] = sums_ref[...].astype(out_ref.dtype)


def lane_block(ref, i):
    n = ref.shape[1]
    return ref[0, :, i * n : (i + 1) * n].astype(f32)


def read_maps(maps_ref):
    coils = maps_ref.shape[2] // maps_ref.shape[1] // 2
    return [[lane_block(maps_ref, 2 * c + p) for p in range(2)] for c in range(coils)]


def read_data(data_ref):
    coils = data_ref.shape[2] // data_ref.shape[1] // 2
    return jnp.concatenate(
        [
            jnp.concatenate([lane_block(data_ref, 2 * c + p) for c in range(coils)], 1)
            for p in range(2)
        ],
        0,
    )


def masked(mask_ref, value):
    coils = value.shape[1] // mask_ref.shape[3]
    pieces = mask_ref.shape[0] // coils
    mask = jnp.concatenate(
        [
            jnp.concatenate([mask_ref[c * pieces + i, 0].astype(f32) for i in range(pieces)], 0)
            for c in range(coils)
        ],
        1,
    )
    return jnp.concatenate([mask, mask], 0) * value


def shifted(a, axis, step):
    n = a.shape[axis]
    if step > 0:
        pieces = (lax.slice_in_dim(a, 1, n, axis=axis), lax.slice_in_dim(a, 0, 1, axis=axis))
    else:
        pieces = (lax.slice_in_dim(a, n - 1, n, axis=axis), lax.slice_in_dim(a, 0, n - 1, axis=axis))
    return jnp.concatenate(pieces, axis)


def position(shape, axis):
    return lax.broadcasted_iota(jnp.int32, shape, axis)


def shrink(here, ahead, duals):
    moved = []
    for p in range(2):
        a = here[p]
        up_z = jnp.where(position(a.shape, 0) < a.shape[0] - 1, shifted(a, 0, 1) - a, 0.0)
        up_y = jnp.where(position(a.shape, 1) < a.shape[1] - 1, shifted(a, 1, 1) - a, 0.0)
        steps = [dual_step * up_z, dual_step * up_y, dual_step * (ahead[p] - a)]
        moved.append(steps if duals is None else [d + s for d, s in zip(duals[p], steps)])
    size = jnp.sqrt(sum(m * m for part in moved for m in part))
    factor = 1.0 / jnp.maximum(1.0, size / tv_weight)
    return [[m * factor for m in part] for part in moved]


def divergence(duals, duals_before, has_before):
    sums = []
    for p in range(2):
        d_z, d_y, d_x = duals[p]
        back_z = jnp.where(position(d_z.shape, 0) > 0, shifted(d_z, 0, -1), 0.0)
        back_y = jnp.where(position(d_y.shape, 1) > 0, shifted(d_y, 1, -1), 0.0)
        sums.append((back_z - d_z) + (back_y - d_y) + (has_before * duals_before[p][2] - d_x))
    return sums


def read_start(edge_ref, start_ref):
    here, before, after = [[start_ref[i, p].astype(f32) for p in range(2)] for i in range(3)]
    return before, here, [jnp.where(edge_ref[1] > 0.0, a, h) for a, h in zip(after, here)]


def first_kernel(
    edge_ref, start_ref, maps_ref, data_ref, mask_ref, fz_ref, fy_ref, gy_ref, gz_ref,
    dual_ref, out_ref, change_ref, image_ref, sums_ref,
):
    @pl.when(pl.program_id(0) == 0)
    def _():
        before, here, after = read_start(edge_ref, start_ref)
        spread = divergence(shrink(here, after, None), shrink(before, here, None), edge_ref[0])
        for p in range(2):
            image_ref[p] = here[p]
            change_ref[p] = spread[p]

    maps = read_maps(maps_ref)
    spectrum = to_kspace(maps, image_ref, fz_ref[...], fy_ref[...])
    dual = (dual_step * masked(mask_ref, spectrum - read_data(data_ref))) * (1.0 / (1.0 + dual_step))
    dual_ref[0] = dual
    accumulate(sums_ref, out_ref, to_image(dual.astype(bf16), maps, gy_ref[...], gz_ref[...]))


def second_kernel(
    guess_ref, dual_ref, maps_ref, data_ref, mask_ref, fz_ref, fy_ref, gy_ref, gz_ref, out_ref, sums_ref
):
    maps = read_maps(maps_ref)
    spectrum = to_kspace(maps, guess_ref, fz_ref[...], fy_ref[...])
    step = dual_step * masked(mask_ref, spectrum - read_data(data_ref))
    dual = (dual_ref[0] + step) * (1.0 / (1.0 + dual_step))
    accumulate(sums_ref, out_ref, to_image(dual.astype(bf16), maps, gy_ref[...], gz_ref[...]))


def last_kernel(edge_ref, start_ref, change_ref, guess_ref, before_ref, after_ref, out_ref):
    old_before, old_here, old_after = read_start(edge_ref, start_ref)
    has_after = edge_ref[1]
    here = [guess_ref[p] for p in range(2)]
    before = [before_ref[p] for p in range(2)]
    after = [jnp.where(has_after > 0.0, after_ref[p], here[p]) for p in range(2)]
    duals = shrink(here, after, shrink(old_here, old_after, None))
    duals_before = shrink(before, here, shrink(old_before, old_here, None))
    spread = divergence(duals, duals_before, edge_ref[0])
    for p in range(2):
        out_ref[p] = change_ref[p] + spread[p]


def step_block(a, dim):
    return pl.BlockSpec(
        tuple(1 if i == dim else n for i, n in enumerate(a.shape)),
        lambda i: tuple(i if k == dim else 0 for k in range(a.ndim)),
    )


def whole_block(a):
    if a.ndim == 1:
        return pl.BlockSpec(memory_space=pltpu.SMEM)
    zeros = (0,) * a.ndim
    return pl.BlockSpec(a.shape, lambda i: zeros)


def call(kernel, outs, stepped, *operands, steps, scratch=()):
    specs = [
        whole_block(a) if dim is None else step_block(a, dim)
        for a, dim in zip((*operands, *outs), stepped)
    ]
    return pl.pallas_call(
        kernel,
        grid=(steps,),
        in_specs=specs[: len(operands)],
        out_specs=specs[len(operands) :],
        out_shape=outs,
        scratch_shapes=[pltpu.VMEM(shape, f32) for shape in scratch],
        compiler_params=pltpu.CompilerParams(vmem_limit_bytes=40 * 1024 * 1024),
    )(*operands)


def on_device(kspace_data, coil_maps, sample_mask, initial_image):
    coils, _, planes, ny, nx = coil_maps.shape
    nz, lines = kspace_data.shape[2:4]
    rows = initial_image.shape[2]
    sizes = [lax.axis_size(a) for a in COLUMN]
    zq, group = sizes[0], lax.axis_size(GROUP)
    count = math.prod(sizes)
    slabs = count // zq
    column_of = snake(*sizes)
    place_of = np.argsort(column_of)
    me = lax.axis_index(COLUMN)
    is_first, is_last = me == int(place_of[0]), me == int(place_of[-1])
    quarters = sizes[3]

    def spread(blocks):
        return lax.all_to_all(blocks, COLUMN, 0, 0, tiled=True)

    pick = np.eye(nx, dtype=np.float32)[column_of]
    near = [pick, np.roll(pick, -1, 1), np.roll(pick, 1, 1)]
    map_rows = jnp.einsum(
        "wx,iryx->wriy", pick.astype(ml_dtypes.bfloat16), coil_maps.reshape(coils * 2, planes, ny, nx),
        preferred_element_type=f32,
    ).astype(bf16)
    inv_x = table(nx, True)[:, column_of]
    turned = jnp.einsum(
        "ckzyw,jxkw->xycjz", kspace_data, inv_x, preferred_element_type=f32
    ).astype(bf16)
    image_rows = jnp.einsum(
        "wx,kx->wk",
        np.concatenate(near).astype(ml_dtypes.bfloat16),
        initial_image.astype(bf16).reshape(-1, nx),
        preferred_element_type=f32,
    ).astype(bf16)
    image_rows = jnp.concatenate([image_rows[i * nx : (i + 1) * nx] for i in range(3)], 1)
    image_rows = jnp.pad(image_rows, ((0, 0), (0, -image_rows.shape[1] % nz))).reshape(nx, -1, nz)
    mask_rows = sample_mask.transpose(0, 2, 1).astype(bf16).reshape(quarters, -1, nz)
    mask_rows = jnp.broadcast_to(mask_rows[None], (count // quarters, *mask_rows.shape))
    extra = jnp.concatenate([image_rows, mask_rows.reshape(nx, -1, nz)], 1)
    lanes = coils * 2 * ny
    blocks = spread(
        jnp.concatenate([map_rows.reshape(nx, planes, lanes), turned.reshape(nx, lines, lanes), extra], 2)
    )
    extra = blocks[:, :, 2 * lanes :]
    pieces = quarters // coils

    mask = extra[:, 2:].reshape(zq, -1, nz)
    mask = jnp.broadcast_to(mask[None], (quarters, *mask.shape))
    mask = lax.all_to_all(mask, COLUMN[3], 0, 0, tiled=True)

    start = extra[:, :2].reshape(zq, slabs, -1)[:, :, : 3 * 2 * planes * rows]
    start = start.reshape(zq, slabs, 3, 2, planes, rows).transpose(2, 3, 1, 4, 0, 5)
    start = lax.all_gather(start.reshape(3, 2, nz, zq * rows), GROUP, axis=0)
    start = start.reshape(group, 3, 2, nz, zq, rows).transpose(1, 2, 3, 4, 0, 5).reshape(3, 2, nz, ny)

    maps = blocks[:, :, :lanes].reshape(zq, nz, lanes)
    data = blocks[:, :, lanes : 2 * lanes].reshape(zq, slabs, pieces, -1, lanes)
    data = data.transpose(0, 2, 1, 3, 4).reshape(zq, ny, lanes)
    edge = jnp.stack([1.0 - is_first.astype(f32), 1.0 - is_last.astype(f32)])

    ky_order = np.arange(ny).reshape(slabs, pieces, -1).transpose(1, 0, 2).reshape(-1)
    fz, gz = (table(nz, inverse).reshape(2 * nz, 2 * nz) for inverse in (False, True))
    fy = table(ny, False)[:, ky_order].reshape(2 * ny, 2 * ny)
    gy = table(ny, True)[..., ky_order].reshape(2 * ny, 2 * ny)
    dual_like = jax.ShapeDtypeStruct((zq, 2 * ny, coils * nz), f32)
    grad_like = jax.ShapeDtypeStruct((2, nz, ny), bf16)
    image_like = jax.ShapeDtypeStruct((2, nz, ny), f32)

    dual, grad, change, current = call(
        first_kernel, (dual_like, grad_like, image_like, image_like),
        (None, None, 0, 0, 1, None, None, None, None, 0, None, None, None),
        edge, start, maps, data, mask, fz, fy, gy, gz, steps=zq, scratch=[image_like.shape],
    )
    change = change + lax.all_gather(grad, GROUP, axis=0).astype(f32).sum(0)
    guess = current - (2.0 * primal_step) * change

    forth = [(int(place_of[i]), int(place_of[i + 1])) for i in range(count - 1)]
    before = lax.ppermute(guess, COLUMN, forth)
    after = lax.ppermute(guess, COLUMN, [(b, a) for a, b in forth])
    (grad,) = call(
        second_kernel, (grad_like,), (None, 0, 0, 0, 1, None, None, None, None, None),
        guess, dual, maps, data, mask, fz, fy, gy, gz, steps=zq, scratch=[image_like.shape],
    )
    grad = grad.reshape(2, nz, zq, group, rows).transpose(3, 0, 1, 2, 4)
    grad = lax.all_to_all(grad, GROUP, 0, 0, tiled=True).astype(f32).sum(0)

    (rest,) = call(
        last_kernel, (image_like,), (None,) * 7, edge, start, change, guess, before, after, steps=1
    )
    rest = rest.reshape(2, nz, zq, group, rows)
    rest = lax.dynamic_index_in_dim(rest, lax.axis_index(GROUP), 3, keepdims=False)
    result = rest + grad
    result = result.reshape(2, slabs, planes, zq, rows).transpose(3, 1, 0, 2, 4)
    result = spread(result.reshape(count, 2 * planes * rows))
    result = lax.dot_general(
        result, pick, (((0,), (0,)), ((), ())), precision=lax.Precision.HIGHEST, preferred_element_type=f32
    )
    return initial_image - primal_step * result.reshape(2, planes, rows, nx)


def solution(mesh):
    devices = mesh.devices.reshape(4, 2, 2, 4, 2, 4)
    split = Mesh(devices, ("zq", "zp", "core", "x", "zhi", "y"))
    coil, slab = ("zq", "zp", "core"), ("x", "zhi", "y")
    return jax.shard_map(
        on_device,
        mesh=split,
        in_specs=(
            P(coil, None, None, slab, None),
            P(coil, None, slab, None, None),
            P(coil, None, slab),
            P(None, slab, coil, None),
        ),
        out_specs=P(None, slab, coil, None),
        check_vma=False,
    )
```

```python
import math

import jax
import jax.numpy as jnp
import ml_dtypes
import numpy as np
from jax import lax
from jax.experimental import pallas as pl
from jax.experimental.pallas import tpu as pltpu
from jax.sharding import Mesh
from jax.sharding import PartitionSpec as P

dual_step = 0.25
primal_step = 0.25
tv_weight = 0.5

COLUMN = ("zq", "x", "zhi", "y")
GROUP = ("zp", "core")
bf16 = jnp.bfloat16
f32 = jnp.float32


def table(length, inverse):
    product = np.outer(np.arange(length), np.arange(length)) % length
    phase = (2.0 * math.pi / length) * product
    real = np.cos(phase) / math.sqrt(length)
    imag = np.sin(phase) / math.sqrt(length) * (1.0 if inverse else -1.0)
    whole = np.stack([np.stack([real, -imag], 1), np.stack([imag, real], 1)])
    return whole.astype(np.float32).astype(ml_dtypes.bfloat16)


def snake(zq, x, zhi, y):
    column = np.zeros((zq, x, zhi, y), np.int32)
    for a in range(zq):
        for h in range(zhi):
            turn = h * zq + a
            for i in range(x):
                for j in range(y):
                    step = i * y + (j if i % 2 == 0 else y - 1 - j)
                    column[a, i, h, j] = turn * x * y + (step if turn % 2 == 0 else x * y - 1 - step)
    return column.reshape(-1)


def dot(a, b):
    return lax.dot_general(a, b, (((1,), (0,)), ((), ())), preferred_element_type=f32)


def dot_t(a, b):
    return lax.dot_general(a, b, (((1,), (1,)), ((), ())), preferred_element_type=f32)


def lanes_to_rows(value, coils):
    n = value.shape[0] // 2
    m = value.shape[1] // coils
    return jnp.concatenate(
        [
            jnp.concatenate([value[p * n : (p + 1) * n, c * m : (c + 1) * m] for p in range(2)], 1)
            for c in range(coils)
        ],
        0,
    )


def to_kspace(maps, image, fz, fy):
    columns = []
    for real, imag in maps:
        columns.append(
            jnp.concatenate(
                [real * image[0] - imag * image[1], real * image[1] + imag * image[0]], 0
            ).astype(bf16)
        )
    half = dot(fz, jnp.concatenate(columns, 1)).astype(bf16)
    return dot_t(fy, lanes_to_rows(half, len(maps)))


def to_image(dual, maps, gy, gz):
    coils, n = len(maps), maps[0][0].shape[0]
    half = dot(gy, dual).astype(bf16)
    field = dot_t(gz, lanes_to_rows(half, coils))
    real_sum, imag_sum = 0.0, 0.0
    for c, (real, imag) in enumerate(maps):
        m = field.shape[1] // coils
        h_real, h_imag = field[:n, c * m : (c + 1) * m], field[n:, c * m : (c + 1) * m]
        real_sum += real * h_real + imag * h_imag
        imag_sum += real * h_imag - imag * h_real
    return real_sum, imag_sum


def accumulate(sums_ref, out_ref, parts):
    step = pl.program_id(0)

    @pl.when(step == 0)
    def _():
        sums_ref[...] = jnp.zeros_like(sums_ref)

    sums_ref[0] += parts[0]
    sums_ref[1] += parts[1]

    @pl.when(step == pl.num_programs(0) - 1)
    def _():
        out_ref[...] = sums_ref[...].astype(out_ref.dtype)


def lane_block(ref, i):
    n = ref.shape[0] * ref.shape[1]
    return ref[:, :, i * n : (i + 1) * n].astype(f32).reshape(n, n)


def read_maps(block_ref, coils):
    return [[lane_block(block_ref, 2 * c + p) for p in range(2)] for c in range(coils)]


def read_data(block_ref, coils):
    return jnp.concatenate(
        [
            jnp.concatenate([lane_block(block_ref, 2 * (coils + c) + p) for c in range(coils)], 1)
            for p in range(2)
        ],
        0,
    )


def masked(mask_ref, value):
    n = mask_ref.shape[3]
    coils = value.shape[1] // n
    late = pl.program_id(0) >= pl.num_programs(0) // 2
    left = position((n, n), 1) < n // 2
    columns = []
    for c in range(coils):
        low, high = (mask_ref[2 * c + h, 0].astype(f32) for h in range(2))
        low = jnp.where(late, pltpu.roll(low, n // 2, 1), low)
        high = jnp.where(late, high, pltpu.roll(high, n // 2, 1))
        columns.append(jnp.where(left, low, high))
    mask = jnp.concatenate(columns, 1)
    return jnp.concatenate([mask, mask], 0) * value


def pack_kernel(
    maps_ref, data_ref, mask_ref, image_ref, near_ref, inv_ref, sort_ref, choose_ref, out_ref
):
    coils, _, planes, n, _ = maps_ref.shape
    lines, rows = data_ref.shape[3], image_ref.shape[2]
    kinds = near_ref.shape[1] // n
    lanes = coils * 2 * n
    pick = near_ref[:, :n]
    sort = sort_ref[...]
    group = sort.shape[0]
    for t in range(planes):
        planes_t = jnp.concatenate([maps_ref[c, p, t] for c in range(coils) for p in range(2)], 0)
        out_ref[:, t, :lanes] = dot_t(pick, planes_t).astype(bf16)
    for c in range(coils):
        field = jnp.concatenate([data_ref[c, p].reshape(n * lines, n) for p in range(2)], 1)
        sorted_rows = [
            dot(sort, field[g * group : (g + 1) * group]).astype(bf16) for g in range(n * lines // group)
        ]
        part = group // lines
        for t in range(lines):
            line = jnp.concatenate([r[t * part : (t + 1) * part] for r in sorted_rows], 0)
            turned = dot_t(inv_ref[...], line)
            for p in range(2):
                start = lanes + (2 * c + p) * n
                out_ref[:, t, start : start + n] = turned[p * n : (p + 1) * n].astype(bf16)
    shape = (n, n)
    half = n // 2
    mask = jnp.concatenate([mask_ref[c].astype(f32) for c in range(coils)], 1).astype(bf16)
    chosen = dot_t(choose_ref[...], mask)
    for t in range(planes):
        value = jnp.concatenate([image_ref[p, t] for p in range(2)], 0)
        high = value.astype(bf16).astype(f32)
        parts = [high, value - high, high, high]
        none = jnp.zeros_like(value)
        spread = jnp.concatenate(
            [jnp.concatenate([parts[k] if k == i else none for i in range(kinds)], 1) for k in range(kinds)], 0
        )
        spread = jnp.concatenate([spread, jnp.zeros_like(spread)], 0).astype(bf16)
        image = dot_t(near_ref[...], spread)
        line = chosen[t * n : (t + 1) * n]
        odd = lax.rem(position(shape, 0), 2) == 1
        line = jnp.where(odd, line, pltpu.roll(line, half, 1))
        out_ref[:, t, 2 * lanes :] = jnp.where(position(shape, 1) < half, image, line).astype(bf16)


def shifted(a, axis, step):
    n = a.shape[axis]
    if step > 0:
        pieces = (lax.slice_in_dim(a, 1, n, axis=axis), lax.slice_in_dim(a, 0, 1, axis=axis))
    else:
        pieces = (lax.slice_in_dim(a, n - 1, n, axis=axis), lax.slice_in_dim(a, 0, n - 1, axis=axis))
    return jnp.concatenate(pieces, axis)


def position(shape, axis):
    return lax.broadcasted_iota(jnp.int32, shape, axis)


def shrink(here, ahead, duals):
    moved = []
    for p in range(2):
        a = here[p]
        up_z = jnp.where(position(a.shape, 0) < a.shape[0] - 1, shifted(a, 0, 1) - a, 0.0)
        up_y = jnp.where(position(a.shape, 1) < a.shape[1] - 1, shifted(a, 1, 1) - a, 0.0)
        steps = [dual_step * up_z, dual_step * up_y, dual_step * (ahead[p] - a)]
        moved.append(steps if duals is None else [d + s for d, s in zip(duals[p], steps)])
    size = jnp.sqrt(sum(m * m for part in moved for m in part))
    factor = 1.0 / jnp.maximum(1.0, size / tv_weight)
    return [[m * factor for m in part] for part in moved]


def divergence(duals, duals_before, has_before):
    sums = []
    for p in range(2):
        d_z, d_y, d_x = duals[p]
        back_z = jnp.where(position(d_z.shape, 0) > 0, shifted(d_z, 0, -1), 0.0)
        back_y = jnp.where(position(d_y.shape, 1) > 0, shifted(d_y, 1, -1), 0.0)
        sums.append((back_z - d_z) + (back_y - d_y) + (has_before * duals_before[p][2] - d_x))
    return sums


def first_kernel(
    edge_ref, start_ref, place_ref, block_ref, mask_ref, fz_ref, fy_ref, gy_ref, gz_ref,
    dual_ref, out_ref, change_ref, image_ref, sums_ref,
):
    coils = dual_ref.shape[2] // start_ref.shape[2]

    @pl.when(pl.program_id(0) == 0)
    def _():
        pieces = [start_ref[r, h] for r in range(start_ref.shape[0]) for h in range(start_ref.shape[1])]
        planes = dot(jnp.concatenate(pieces, 1), place_ref[...])
        n = planes.shape[0]
        here, before, after = [
            [planes[:, (2 * k + p) * n : (2 * k + p + 1) * n] for p in range(2)] for k in range(3)
        ]
        after = [jnp.where(edge_ref[1] > 0.0, a, h) for a, h in zip(after, here)]
        spread = divergence(shrink(here, after, None), shrink(before, here, None), edge_ref[0])
        for p in range(2):
            image_ref[0, p] = here[p]
            image_ref[1, p] = before[p]
            image_ref[2, p] = after[p]
            change_ref[p] = spread[p]

    maps = read_maps(block_ref, coils)
    spectrum = to_kspace(maps, image_ref.at[0], fz_ref[...], fy_ref[...])
    dual = (dual_step * masked(mask_ref, spectrum - read_data(block_ref, coils))) * (1.0 / (1.0 + dual_step))
    dual_ref[0] = dual
    accumulate(sums_ref, out_ref, to_image(dual.astype(bf16), maps, gy_ref[...], gz_ref[...]))


def second_kernel(
    guess_ref, dual_ref, block_ref, mask_ref, fz_ref, fy_ref, gy_ref, gz_ref, out_ref, sums_ref
):
    coils = dual_ref.shape[2] // guess_ref.shape[1]
    maps = read_maps(block_ref, coils)
    spectrum = to_kspace(maps, guess_ref, fz_ref[...], fy_ref[...])
    step = dual_step * masked(mask_ref, spectrum - read_data(block_ref, coils))
    dual = (dual_ref[0] + step) * (1.0 / (1.0 + dual_step))
    accumulate(sums_ref, out_ref, to_image(dual.astype(bf16), maps, gy_ref[...], gz_ref[...]))


def last_kernel(edge_ref, image_ref, change_ref, guess_ref, before_ref, after_ref, out_ref):
    old_here, old_before, old_after = [[image_ref[k, p] for p in range(2)] for k in range(3)]
    here = [guess_ref[p] for p in range(2)]
    before = [before_ref[p] for p in range(2)]
    after = [jnp.where(edge_ref[1] > 0.0, after_ref[p], here[p]) for p in range(2)]
    duals = shrink(here, after, shrink(old_here, old_after, None))
    duals_before = shrink(before, here, shrink(old_before, old_here, None))
    spread = divergence(duals, duals_before, edge_ref[0])
    for p in range(2):
        out_ref[p] = change_ref[p] + spread[p]


def step_block(a, dim, count, steps):
    return pl.BlockSpec(
        tuple(n // count if i == dim else n for i, n in enumerate(a.shape)),
        lambda i: tuple(lax.rem(i, count) if k == dim else 0 for k in range(a.ndim)),
    )


def whole_block(a):
    if a.ndim == 1:
        return pl.BlockSpec(memory_space=pltpu.SMEM)
    zeros = (0,) * a.ndim
    return pl.BlockSpec(a.shape, lambda i: zeros)


def call(kernel, outs, stepped, *operands, steps, scratch=()):
    specs = [
        whole_block(a) if cut is None else step_block(a, *cut, steps)
        for a, cut in zip((*operands, *outs), stepped)
    ]
    return pl.pallas_call(
        kernel,
        grid=(steps,),
        in_specs=specs[: len(operands)],
        out_specs=specs[len(operands) :],
        out_shape=outs,
        scratch_shapes=[pltpu.VMEM(shape, f32) for shape in scratch],
        compiler_params=pltpu.CompilerParams(vmem_limit_bytes=40 * 1024 * 1024),
    )(*operands)


def on_device(kspace_data, coil_maps, sample_mask, initial_image):
    coils, _, planes, ny, nx = coil_maps.shape
    nz, lines = kspace_data.shape[2:4]
    rows = initial_image.shape[2]
    sizes = [lax.axis_size(a) for a in COLUMN]
    zq, group = sizes[0], lax.axis_size(GROUP)
    count = math.prod(sizes)
    slabs = count // zq
    column_of = snake(*sizes)
    place_of = np.argsort(column_of)
    me = lax.axis_index(COLUMN)
    is_first, is_last = me == int(place_of[0]), me == int(place_of[-1])
    quarters = sizes[3]

    def spread(blocks):
        return lax.all_to_all(blocks, COLUMN, 0, 0, tiled=True)

    pick = np.eye(nx, dtype=np.float32)[column_of]
    near = np.concatenate([pick, pick, np.roll(pick, -1, 1), np.roll(pick, 1, 1)], 1)
    inv_x = table(nx, True)[:, column_of].reshape(2 * nx, 2 * nx)
    sort = np.eye(nx, dtype=np.float32).reshape(nx // lines, lines, nx).transpose(1, 0, 2).reshape(nx, nx)
    quarter = np.arange(count) % quarters
    choose = np.zeros((lines, count, coils, lines), np.float32)
    for t in range(lines):
        choose[t, np.arange(count), quarter // 2, t] = 1.0
    lanes = coils * 2 * ny
    half = nz // 2
    packed = jax.ShapeDtypeStruct((nx, planes, 2 * lanes + nz), bf16)
    (blocks,) = call(
        pack_kernel, (packed,), (None,) * 9, coil_maps, kspace_data, sample_mask, initial_image,
        near.astype(bf16), inv_x, sort.astype(bf16), choose.reshape(lines * count, -1).astype(bf16), steps=1,
    )
    blocks = spread(blocks)
    extra = blocks[:, :, 2 * lanes :].reshape(zq, nz, nz)

    def pairs(part):
        return jnp.concatenate([part[: zq // 2], part[zq // 2 :]], 2)

    mask = pairs(extra[:, :, half:])
    mask = jnp.broadcast_to(mask[None], (quarters, *mask.shape))
    mask = lax.all_to_all(mask, COLUMN[3], 0, 0, tiled=True)
    start = lax.all_gather(pairs(extra[:, :, :half]), GROUP, axis=0)

    place = np.zeros((group, zq // 2, 2, 4, 2, rows, 3, 2, zq, group, rows), np.float32)
    for r in range(group):
        for a in range(zq):
            for kind, plane in enumerate((0, 0, 1, 2)):
                for p in range(2):
                    for j in range(rows):
                        place[r, a % (zq // 2), a // (zq // 2), kind, p, j, plane, p, a, r, j] = 1.0
    place = place.reshape(group * zq // 2 * nz, 3 * 2 * ny).astype(bf16)
    edge = jnp.stack([1.0 - is_first.astype(f32), 1.0 - is_last.astype(f32)])

    fz, gz = (table(nz, inverse).reshape(2 * nz, 2 * nz) for inverse in (False, True))
    fy, gy = (table(ny, inverse).reshape(2 * ny, 2 * ny) for inverse in (False, True))
    dual_like = jax.ShapeDtypeStruct((zq, 2 * ny, coils * nz), f32)
    grad_like = jax.ShapeDtypeStruct((2, nz, ny), bf16)
    image_like = jax.ShapeDtypeStruct((2, nz, ny), f32)

    images_like = jax.ShapeDtypeStruct((3, 2, nz, ny), f32)
    whole, step, step_mask = None, (0, zq), (1, zq // 2)

    dual, grad, change, images = call(
        first_kernel, (dual_like, grad_like, image_like, images_like),
        (whole, whole, whole, step, step_mask, whole, whole, whole, whole, step, whole, whole, whole),
        edge, start, place, blocks, mask, fz, fy, gy, gz, steps=zq, scratch=[image_like.shape],
    )
    change = change + lax.all_gather(grad, GROUP, axis=0).astype(f32).sum(0)
    guess = images[0] - (2.0 * primal_step) * change

    forth = [(int(place_of[i]), int(place_of[i + 1])) for i in range(count - 1)]
    before = lax.ppermute(guess, COLUMN, forth)
    after = lax.ppermute(guess, COLUMN, [(b, a) for a, b in forth])
    (grad,) = call(
        second_kernel, (grad_like,),
        (whole, step, step, step_mask, whole, whole, whole, whole, whole),
        guess, dual, blocks, mask, fz, fy, gy, gz, steps=zq, scratch=[image_like.shape],
    )
    grad = grad.reshape(2, nz, zq, group, rows).transpose(3, 0, 1, 2, 4)
    grad = lax.all_to_all(grad, GROUP, 0, 0, tiled=True).astype(f32).sum(0)

    (rest,) = call(
        last_kernel, (image_like,), (whole,) * 7, edge, images, change, guess, before, after, steps=1
    )
    rest = rest.reshape(2, nz, zq, group, rows)
    rest = lax.dynamic_index_in_dim(rest, lax.axis_index(GROUP), 3, keepdims=False)
    result = rest + grad
    result = result.reshape(2, slabs, planes, zq, rows).transpose(3, 1, 0, 2, 4)
    result = spread(result.reshape(count, 2 * planes * rows))
    result = lax.dot_general(
        result, pick, (((0,), (0,)), ((), ())), precision=lax.Precision.HIGHEST, preferred_element_type=f32
    )
    return initial_image - primal_step * result.reshape(2, planes, rows, nx)


def solution(mesh):
    devices = mesh.devices.reshape(4, 2, 2, 4, 2, 4)
    split = Mesh(devices, ("zq", "zp", "core", "x", "zhi", "y"))
    coil, slab = ("zq", "zp", "core"), ("x", "zhi", "y")
    return jax.shard_map(
        on_device,
        mesh=split,
        in_specs=(
            P(coil, None, None, slab, None),
            P(coil, None, slab, None, None),
            P(coil, None, slab),
            P(None, slab, coil, None),
        ),
        out_specs=P(None, slab, coil, None),
        check_vma=False,
    )
```

```python
import math

import jax
import jax.numpy as jnp
import ml_dtypes
import numpy as np
from jax import lax
from jax.experimental import pallas as pl
from jax.experimental.pallas import tpu as pltpu
from jax.sharding import Mesh
from jax.sharding import PartitionSpec as P

dual_step = 0.25
primal_step = 0.25
tv_weight = 0.5

COLUMN = ("zq", "x", "zhi", "y")
GROUP = ("zp", "core")
bf16 = jnp.bfloat16
f32 = jnp.float32


def table(length, inverse):
    product = np.outer(np.arange(length), np.arange(length)) % length
    phase = (2.0 * math.pi / length) * product
    real = np.cos(phase) / math.sqrt(length)
    imag = np.sin(phase) / math.sqrt(length) * (1.0 if inverse else -1.0)
    whole = np.stack([np.stack([real, -imag], 1), np.stack([imag, real], 1)])
    return whole.astype(np.float32).astype(ml_dtypes.bfloat16)


def snake(zq, x, zhi, y):
    column = np.zeros((zq, x, zhi, y), np.int32)
    for a in range(zq):
        for h in range(zhi):
            turn = h * zq + a
            for i in range(x):
                for j in range(y):
                    step = i * y + (j if i % 2 == 0 else y - 1 - j)
                    column[a, i, h, j] = turn * x * y + (step if turn % 2 == 0 else x * y - 1 - step)
    return column.reshape(-1)


def dot(a, b):
    return lax.dot_general(a, b, (((1,), (0,)), ((), ())), preferred_element_type=f32)


def dot_t(a, b):
    return lax.dot_general(a, b, (((1,), (1,)), ((), ())), preferred_element_type=f32)


def lanes_to_rows(value, coils):
    n = value.shape[0] // 2
    m = value.shape[1] // coils
    return jnp.concatenate(
        [
            jnp.concatenate([value[p * n : (p + 1) * n, c * m : (c + 1) * m] for p in range(2)], 1)
            for c in range(coils)
        ],
        0,
    )


def to_kspace(maps, image, fz, fy):
    columns = []
    for real, imag in maps:
        columns.append(
            jnp.concatenate(
                [real * image[0] - imag * image[1], real * image[1] + imag * image[0]], 0
            ).astype(bf16)
        )
    half = dot(fz, jnp.concatenate(columns, 1)).astype(bf16)
    return dot_t(fy, lanes_to_rows(half, len(maps)))


def to_image(dual, maps, gy, gz):
    coils, n = len(maps), maps[0][0].shape[0]
    half = dot(gy, dual).astype(bf16)
    field = dot_t(gz, lanes_to_rows(half, coils))
    real_sum, imag_sum = 0.0, 0.0
    for c, (real, imag) in enumerate(maps):
        m = field.shape[1] // coils
        h_real, h_imag = field[:n, c * m : (c + 1) * m], field[n:, c * m : (c + 1) * m]
        real_sum += real * h_real + imag * h_imag
        imag_sum += real * h_imag - imag * h_real
    return real_sum, imag_sum


def lane_block(block_ref, a, i):
    n = block_ref.shape[0]
    slabs = n // block_ref.shape[1]
    return block_ref[a * slabs : (a + 1) * slabs, :, i * n : (i + 1) * n].astype(f32).reshape(n, n)


def read_maps(block_ref, a, coils):
    return [[lane_block(block_ref, a, 2 * c + p) for p in range(2)] for c in range(coils)]


def read_data(block_ref, a, coils):
    return jnp.concatenate(
        [
            jnp.concatenate([lane_block(block_ref, a, 2 * (coils + c) + p) for c in range(coils)], 1)
            for p in range(2)
        ],
        0,
    )


def masked(mask_ref, a, coils, value):
    n = mask_ref.shape[3]
    late, pair = divmod(a, mask_ref.shape[1])
    left = position((n, n), 1) < n // 2
    columns = []
    for c in range(coils):
        halves = [mask_ref[2 * c + h, pair].astype(f32) for h in range(2)]
        halves[1 - late] = pltpu.roll(halves[1 - late], n // 2, 1)
        columns.append(jnp.where(left, halves[0], halves[1]))
    mask = jnp.concatenate(columns, 1)
    return jnp.concatenate([mask, mask], 0) * value


def pack_kernel(maps_ref, data_ref, mask_ref, image_ref, near_ref, inv_ref, sort_ref, choose_ref, out_ref):
    coils, _, planes, n, _ = maps_ref.shape
    lines, rows = data_ref.shape[3], image_ref.shape[2]
    kinds = near_ref.shape[1] // n
    pick = near_ref[:, :n]
    sort, mix = sort_ref[0], sort_ref[1]
    part = n // lines
    half = n // 2
    shape = (n, n)

    field = [jnp.concatenate([data_ref[c, p].reshape(n * lines, n) for p in range(2)], 1) for c in range(coils)]
    field = jnp.concatenate(field, 1)
    field = [dot(sort, field[g * n : (g + 1) * n]).astype(bf16) for g in range(lines)]
    mask = jnp.concatenate([mask_ref[c] for c in range(coils)], 0).astype(f32).astype(bf16)
    odd = lax.rem(position(shape, 0), 2) == 1

    packed = []
    for t in range(planes):
        planes_t = jnp.concatenate([maps_ref[c, p, t] for c in range(coils) for p in range(2)], 0)
        pieces = [dot_t(pick, planes_t)]
        line = jnp.concatenate([f[t * part : (t + 1) * part] for f in field], 0)
        line = jnp.concatenate([line[:, c * 2 * n : (c + 1) * 2 * n] for c in range(coils)], 0)
        turned = dot_t(inv_ref[...], line)
        pieces += [
            turned[p * n : (p + 1) * n, c * n : (c + 1) * n] for c in range(coils) for p in range(2)
        ]
        value = jnp.concatenate([image_ref[p, t] for p in range(2)], 0)
        high = value.astype(bf16).astype(f32)
        parts = [high, value - high, high, high]
        none = jnp.zeros_like(value)
        spread = jnp.concatenate(
            [jnp.concatenate([parts[k] if k == i else none for i in range(kinds)], 1) for k in range(kinds)], 0
        )
        image = dot_t(near_ref[...], jnp.concatenate([spread, jnp.zeros_like(spread)], 0).astype(bf16))
        chosen = dot(choose_ref[t * n : (t + 1) * n], mask)
        chosen = jnp.where(odd, chosen, pltpu.roll(chosen, half, 1))
        pieces.append(jnp.where(position(shape, 1) < half, image, chosen))
        packed.append(jnp.concatenate(pieces, 1).astype(bf16))
    for g in range(lines):
        together = jnp.concatenate([v[g * part : (g + 1) * part] for v in packed], 0)
        mixed = dot(mix, together).astype(bf16)
        out_ref[g * part : (g + 1) * part] = mixed.reshape(part, planes, mixed.shape[1])


def shifted(a, axis, step):
    n = a.shape[axis]
    if step > 0:
        pieces = (lax.slice_in_dim(a, 1, n, axis=axis), lax.slice_in_dim(a, 0, 1, axis=axis))
    else:
        pieces = (lax.slice_in_dim(a, n - 1, n, axis=axis), lax.slice_in_dim(a, 0, n - 1, axis=axis))
    return jnp.concatenate(pieces, axis)


def position(shape, axis):
    return lax.broadcasted_iota(jnp.int32, shape, axis)


def shrink(here, ahead, duals):
    moved = []
    for p in range(2):
        a = here[p]
        up_z = jnp.where(position(a.shape, 0) < a.shape[0] - 1, shifted(a, 0, 1) - a, 0.0)
        up_y = jnp.where(position(a.shape, 1) < a.shape[1] - 1, shifted(a, 1, 1) - a, 0.0)
        steps = [dual_step * up_z, dual_step * up_y, dual_step * (ahead[p] - a)]
        moved.append(steps if duals is None else [d + s for d, s in zip(duals[p], steps)])
    size = jnp.sqrt(sum(m * m for part in moved for m in part))
    factor = 1.0 / jnp.maximum(1.0, size / tv_weight)
    return [[m * factor for m in part] for part in moved]


def divergence(duals, duals_before, has_before):
    sums = []
    for p in range(2):
        d_z, d_y, d_x = duals[p]
        back_z = jnp.where(position(d_z.shape, 0) > 0, shifted(d_z, 0, -1), 0.0)
        back_y = jnp.where(position(d_y.shape, 1) > 0, shifted(d_y, 1, -1), 0.0)
        sums.append((back_z - d_z) + (back_y - d_y) + (has_before * duals_before[p][2] - d_x))
    return sums


def first_kernel(
    edge_ref, start_ref, place_ref, block_ref, mask_ref, fz_ref, fy_ref, gy_ref, gz_ref,
    dual_ref, out_ref, change_ref, image_ref,
):
    pairs = dual_ref.shape[0]
    coils = dual_ref.shape[2] // start_ref.shape[2]
    pieces = [start_ref[r, h] for r in range(start_ref.shape[0]) for h in range(start_ref.shape[1])]
    planes = dot(jnp.concatenate(pieces, 1), place_ref[...])
    n = planes.shape[0]
    here, before, after = [
        [planes[:, (2 * k + p) * n : (2 * k + p + 1) * n] for p in range(2)] for k in range(3)
    ]
    after = [jnp.where(edge_ref[1] > 0.0, a, h) for a, h in zip(after, here)]
    sums = [0.0, 0.0]
    for a in range(pairs):
        maps = read_maps(block_ref, a, coils)
        spectrum = to_kspace(maps, here, fz_ref[...], fy_ref[...])
        dual = dual_step * masked(mask_ref, a, coils, spectrum - read_data(block_ref, a, coils))
        dual = dual * (1.0 / (1.0 + dual_step))
        dual_ref[a] = dual
        sums = [s + t for s, t in zip(sums, to_image(dual.astype(bf16), maps, gy_ref[...], gz_ref[...]))]
    spread = divergence(shrink(here, after, None), shrink(before, here, None), edge_ref[0])
    for p in range(2):
        out_ref[p] = sums[p].astype(bf16)
        image_ref[0, p] = here[p]
        image_ref[1, p] = before[p]
        image_ref[2, p] = after[p]
        change_ref[p] = spread[p]


def second_kernel(guess_ref, dual_ref, block_ref, mask_ref, fz_ref, fy_ref, gy_ref, gz_ref, out_ref):
    pairs = dual_ref.shape[0]
    coils = dual_ref.shape[2] // guess_ref.shape[1]
    guess = [guess_ref[p] for p in range(2)]
    sums = [0.0, 0.0]
    for a in range(pairs):
        maps = read_maps(block_ref, a, coils)
        spectrum = to_kspace(maps, guess, fz_ref[...], fy_ref[...])
        step = dual_step * masked(mask_ref, a, coils, spectrum - read_data(block_ref, a, coils))
        dual = (dual_ref[a] + step) * (1.0 / (1.0 + dual_step))
        sums = [s + t for s, t in zip(sums, to_image(dual.astype(bf16), maps, gy_ref[...], gz_ref[...]))]
    for p in range(2):
        out_ref[p] = sums[p].astype(bf16)


def last_kernel(edge_ref, image_ref, change_ref, guess_ref, before_ref, after_ref, out_ref):
    old_here, old_before, old_after = [[image_ref[k, p] for p in range(2)] for k in range(3)]
    here = [guess_ref[p] for p in range(2)]
    before = [before_ref[p] for p in range(2)]
    after = [jnp.where(edge_ref[1] > 0.0, after_ref[p], here[p]) for p in range(2)]
    duals = shrink(here, after, shrink(old_here, old_after, None))
    duals_before = shrink(before, here, shrink(old_before, old_here, None))
    spread = divergence(duals, duals_before, edge_ref[0])
    for p in range(2):
        out_ref[p] = change_ref[p] + spread[p]


def call(kernel, outs, *operands, vmem=40):
    def place(a):
        return pl.BlockSpec(memory_space=pltpu.SMEM if a.ndim == 1 else pltpu.VMEM)

    return pl.pallas_call(
        kernel,
        in_specs=[place(a) for a in operands],
        out_specs=[place(a) for a in outs],
        out_shape=outs,
        compiler_params=pltpu.CompilerParams(vmem_limit_bytes=vmem * 1024 * 1024),
    )(*operands)


def on_device(kspace_data, coil_maps, sample_mask, initial_image):
    coils, _, planes, ny, nx = coil_maps.shape
    nz, lines = kspace_data.shape[2:4]
    rows = initial_image.shape[2]
    sizes = [lax.axis_size(a) for a in COLUMN]
    zq, group = sizes[0], lax.axis_size(GROUP)
    count = math.prod(sizes)
    slabs = count // zq
    column_of = snake(*sizes)
    place_of = np.argsort(column_of)
    me = lax.axis_index(COLUMN)
    is_first, is_last = me == int(place_of[0]), me == int(place_of[-1])
    quarters = sizes[3]

    def spread(blocks):
        return lax.all_to_all(blocks, COLUMN, 0, 0, tiled=True)

    pick = np.eye(nx, dtype=np.float32)[column_of]
    near = np.concatenate([pick, pick, np.roll(pick, -1, 1), np.roll(pick, 1, 1)], 1)
    inv_x = table(nx, True)[:, column_of].reshape(2 * nx, 2 * nx)
    sort = np.eye(nx, dtype=np.float32).reshape(nx // lines, lines, nx).transpose(1, 0, 2).reshape(nx, nx)
    quarter = np.arange(count) % quarters
    choose = np.zeros((lines, count, coils, lines), np.float32)
    for t in range(lines):
        choose[t, np.arange(count), quarter // 2, t] = 1.0
    lanes = coils * 2 * ny
    half = nz // 2
    packed = jax.ShapeDtypeStruct((nx, planes, 2 * lanes + nz), bf16)
    (blocks,) = call(
        pack_kernel, (packed,), coil_maps, kspace_data, sample_mask.transpose(0, 2, 1), initial_image,
        near.astype(bf16), inv_x, np.stack([sort, sort.T]).astype(bf16),
        choose.reshape(lines * count, -1).astype(bf16), vmem=60,
    )
    blocks = spread(blocks)
    extra = blocks[:, :, 2 * lanes :].reshape(zq, nz, nz)

    def pairs(part):
        return jnp.concatenate([part[: zq // 2], part[zq // 2 :]], 2)

    mask = pairs(extra[:, :, half:])
    mask = jnp.broadcast_to(mask[None], (quarters, *mask.shape))
    mask = lax.all_to_all(mask, COLUMN[3], 0, 0, tiled=True)
    start = lax.all_gather(pairs(extra[:, :, :half]), GROUP, axis=0)

    place = np.zeros((group, zq // 2, 2, 4, 2, rows, 3, 2, zq, group, rows), np.float32)
    for r in range(group):
        for a in range(zq):
            for kind, plane in enumerate((0, 0, 1, 2)):
                for p in range(2):
                    for j in range(rows):
                        place[r, a % (zq // 2), a // (zq // 2), kind, p, j, plane, p, a, r, j] = 1.0
    place = place.reshape(group * zq // 2 * nz, 3 * 2 * ny).astype(bf16)
    edge = jnp.stack([1.0 - is_first.astype(f32), 1.0 - is_last.astype(f32)])

    fz, gz = (table(nz, inverse).reshape(2 * nz, 2 * nz) for inverse in (False, True))
    fy, gy = (table(ny, inverse).reshape(2 * ny, 2 * ny) for inverse in (False, True))
    dual_like = jax.ShapeDtypeStruct((zq, 2 * ny, coils * nz), f32)
    grad_like = jax.ShapeDtypeStruct((2, nz, ny), bf16)
    image_like = jax.ShapeDtypeStruct((2, nz, ny), f32)

    images_like = jax.ShapeDtypeStruct((3, 2, nz, ny), f32)
    dual, grad, change, images = call(
        first_kernel, (dual_like, grad_like, image_like, images_like),
        edge, start, place, blocks, mask, fz, fy, gy, gz,
    )
    change = change + lax.all_gather(grad, GROUP, axis=0).astype(f32).sum(0)
    guess = images[0] - (2.0 * primal_step) * change

    forth = [(int(place_of[i]), int(place_of[i + 1])) for i in range(count - 1)]
    before = lax.ppermute(guess, COLUMN, forth)
    after = lax.ppermute(guess, COLUMN, [(b, a) for a, b in forth])
    (grad,) = call(second_kernel, (grad_like,), guess, dual, blocks, mask, fz, fy, gy, gz)
    grad = grad.reshape(2, nz, zq, group, rows).transpose(3, 0, 1, 2, 4)
    grad = lax.all_to_all(grad, GROUP, 0, 0, tiled=True).astype(f32).sum(0)

    (rest,) = call(last_kernel, (image_like,), edge, images, change, guess, before, after)
    rest = rest.reshape(2, nz, zq, group, rows)
    rest = lax.dynamic_index_in_dim(rest, lax.axis_index(GROUP), 3, keepdims=False)
    result = rest + grad
    result = result.reshape(2, slabs, planes, zq, rows).transpose(3, 1, 0, 2, 4)
    result = spread(result.reshape(count, 2 * planes * rows))
    result = lax.dot_general(
        result, pick, (((0,), (0,)), ((), ())), precision=lax.Precision.HIGHEST, preferred_element_type=f32
    )
    return initial_image - primal_step * result.reshape(2, planes, rows, nx)


def solution(mesh):
    devices = mesh.devices.reshape(4, 2, 2, 4, 2, 4)
    split = Mesh(devices, ("zq", "zp", "core", "x", "zhi", "y"))
    coil, slab = ("zq", "zp", "core"), ("x", "zhi", "y")
    return jax.shard_map(
        on_device,
        mesh=split,
        in_specs=(
            P(coil, None, None, slab, None),
            P(coil, None, slab, None, None),
            P(coil, None, slab),
            P(None, slab, coil, None),
        ),
        out_specs=P(None, slab, coil, None),
        check_vma=False,
    )
```

```python
import math

import jax
import jax.numpy as jnp
import ml_dtypes
import numpy as np
from jax import lax
from jax.experimental import pallas as pl
from jax.experimental.pallas import tpu as pltpu
from jax.sharding import Mesh
from jax.sharding import PartitionSpec as P

dual_step = 0.25
primal_step = 0.25
tv_weight = 0.5

COLUMN = ("zq", "x", "zhi", "y")
GROUP = ("zp", "core")
bf16 = jnp.bfloat16
f32 = jnp.float32


def table(length, inverse):
    product = np.outer(np.arange(length), np.arange(length)) % length
    phase = (2.0 * math.pi / length) * product
    real = np.cos(phase) / math.sqrt(length)
    imag = np.sin(phase) / math.sqrt(length) * (1.0 if inverse else -1.0)
    whole = np.stack([np.stack([real, -imag], 1), np.stack([imag, real], 1)])
    return whole.astype(np.float32).astype(ml_dtypes.bfloat16)


def snake(zq, x, zhi, y):
    column = np.zeros((zq, x, zhi, y), np.int32)
    for a in range(zq):
        for h in range(zhi):
            turn = h * zq + a
            for i in range(x):
                for j in range(y):
                    step = i * y + (j if i % 2 == 0 else y - 1 - j)
                    column[a, i, h, j] = turn * x * y + (step if turn % 2 == 0 else x * y - 1 - step)
    return column.reshape(-1)


def dot(a, b):
    return lax.dot_general(a, b, (((1,), (0,)), ((), ())), preferred_element_type=f32)


def dot_t(a, b):
    return lax.dot_general(a, b, (((1,), (1,)), ((), ())), preferred_element_type=f32)


def lanes_to_rows(value, coils):
    n = value.shape[0] // 2
    m = value.shape[1] // coils
    return jnp.concatenate(
        [
            jnp.concatenate([value[p * n : (p + 1) * n, c * m : (c + 1) * m] for p in range(2)], 1)
            for c in range(coils)
        ],
        0,
    )


def to_kspace(maps, image, fz, fy):
    columns = []
    for real, imag in maps:
        columns.append(
            jnp.concatenate(
                [real * image[0] - imag * image[1], real * image[1] + imag * image[0]], 0
            ).astype(bf16)
        )
    half = dot(fz, jnp.concatenate(columns, 1)).astype(bf16)
    return dot_t(fy, lanes_to_rows(half, len(maps)))


def to_image(dual, maps, gy, gz):
    coils, n = len(maps), maps[0][0].shape[0]
    half = dot(gy, dual).astype(bf16)
    field = dot_t(gz, lanes_to_rows(half, coils))
    real_sum, imag_sum = 0.0, 0.0
    for c, (real, imag) in enumerate(maps):
        m = field.shape[1] // coils
        h_real, h_imag = field[:n, c * m : (c + 1) * m], field[n:, c * m : (c + 1) * m]
        real_sum += real * h_real + imag * h_imag
        imag_sum += real * h_imag - imag * h_real
    return real_sum, imag_sum


def lane_block(block_ref, a, i):
    n = block_ref.shape[0]
    slabs = n // block_ref.shape[1]
    return block_ref[a * slabs : (a + 1) * slabs, :, i * n : (i + 1) * n].astype(f32).reshape(n, n)


def read_maps(block_ref, a, coils):
    return [[lane_block(block_ref, a, 2 * c + p) for p in range(2)] for c in range(coils)]


def read_data(block_ref, a, coils):
    return jnp.concatenate(
        [
            jnp.concatenate([lane_block(block_ref, a, 2 * (coils + c) + p) for c in range(coils)], 1)
            for p in range(2)
        ],
        0,
    )


def masked(mask_ref, a, coils, value):
    n = mask_ref.shape[3]
    late, pair = divmod(a, mask_ref.shape[1])
    left = position((n, n), 1) < n // 2
    columns = []
    for c in range(coils):
        halves = [mask_ref[2 * c + h, pair].astype(f32) for h in range(2)]
        halves[1 - late] = pltpu.roll(halves[1 - late], n // 2, 1)
        columns.append(jnp.where(left, halves[0], halves[1]))
    mask = jnp.concatenate(columns, 1)
    return jnp.concatenate([mask, mask], 0) * value


def pack_kernel(maps_ref, data_ref, mask_ref, image_ref, near_ref, inv_ref, sort_ref, choose_ref, out_ref):
    coils, _, planes, n, _ = maps_ref.shape
    lines, rows = data_ref.shape[3], image_ref.shape[2]
    kinds = near_ref.shape[1] // n
    pick = near_ref[:, :n]
    sort, mix = sort_ref[0], sort_ref[1]
    part = n // lines
    half = n // 2
    shape = (n, n)

    field = [jnp.concatenate([data_ref[c, p].reshape(n * lines, n) for p in range(2)], 1) for c in range(coils)]
    field = jnp.concatenate(field, 1)
    field = [dot(sort, field[g * n : (g + 1) * n]).astype(bf16) for g in range(lines)]
    mask = jnp.concatenate([mask_ref[c] for c in range(coils)], 0).astype(f32).astype(bf16)
    odd = lax.rem(position(shape, 0), 2) == 1

    packed = []
    for t in range(planes):
        planes_t = jnp.concatenate([maps_ref[c, p, t] for c in range(coils) for p in range(2)], 0)
        pieces = [dot_t(pick, planes_t)]
        line = jnp.concatenate([f[t * part : (t + 1) * part] for f in field], 0)
        line = jnp.concatenate([line[:, c * 2 * n : (c + 1) * 2 * n] for c in range(coils)], 0)
        turned = dot_t(inv_ref[...], line)
        pieces += [
            turned[p * n : (p + 1) * n, c * n : (c + 1) * n] for c in range(coils) for p in range(2)
        ]
        value = jnp.concatenate([image_ref[p, t] for p in range(2)], 0)
        high = value.astype(bf16).astype(f32)
        parts = [high, value - high, high, high]
        none = jnp.zeros_like(value)
        spread = jnp.concatenate(
            [jnp.concatenate([parts[k] if k == i else none for i in range(kinds)], 1) for k in range(kinds)], 0
        )
        image = dot_t(near_ref[...], jnp.concatenate([spread, jnp.zeros_like(spread)], 0).astype(bf16))
        chosen = dot(choose_ref[t * n : (t + 1) * n], mask)
        chosen = jnp.where(odd, chosen, pltpu.roll(chosen, half, 1))
        pieces.append(jnp.where(position(shape, 1) < half, image, chosen))
        packed.append(jnp.concatenate(pieces, 1).astype(bf16))
    for g in range(lines):
        together = jnp.concatenate([v[g * part : (g + 1) * part] for v in packed], 0)
        mixed = dot(mix, together).astype(bf16)
        out_ref[g * part : (g + 1) * part] = mixed.reshape(part, planes, mixed.shape[1])


def shifted(a, axis, step):
    n = a.shape[axis]
    if step > 0:
        pieces = (lax.slice_in_dim(a, 1, n, axis=axis), lax.slice_in_dim(a, 0, 1, axis=axis))
    else:
        pieces = (lax.slice_in_dim(a, n - 1, n, axis=axis), lax.slice_in_dim(a, 0, n - 1, axis=axis))
    return jnp.concatenate(pieces, axis)


def position(shape, axis):
    return lax.broadcasted_iota(jnp.int32, shape, axis)


def shrink(here, ahead, duals):
    moved = []
    for p in range(2):
        a = here[p]
        up_z = jnp.where(position(a.shape, 0) < a.shape[0] - 1, shifted(a, 0, 1) - a, 0.0)
        up_y = jnp.where(position(a.shape, 1) < a.shape[1] - 1, shifted(a, 1, 1) - a, 0.0)
        steps = [dual_step * up_z, dual_step * up_y, dual_step * (ahead[p] - a)]
        moved.append(steps if duals is None else [d + s for d, s in zip(duals[p], steps)])
    size = jnp.sqrt(sum(m * m for part in moved for m in part))
    factor = 1.0 / jnp.maximum(1.0, size / tv_weight)
    return [[m * factor for m in part] for part in moved]


def divergence(duals):
    sums = []
    for d_z, d_y, d_x in duals:
        back_z = jnp.where(position(d_z.shape, 0) > 0, shifted(d_z, 0, -1), 0.0)
        back_y = jnp.where(position(d_y.shape, 1) > 0, shifted(d_y, 1, -1), 0.0)
        sums.append((back_z - d_z) + (back_y - d_y) - d_x)
    return sums


def first_kernel(
    edge_ref, start_ref, place_ref, block_ref, mask_ref, fz_ref, fy_ref, gy_ref, gz_ref,
    dual_ref, out_ref, change_ref, image_ref,
):
    pairs = dual_ref.shape[0]
    coils = dual_ref.shape[2] // start_ref.shape[2]
    pieces = [start_ref[r, h] for r in range(start_ref.shape[0]) for h in range(start_ref.shape[1])]
    planes = dot(jnp.concatenate(pieces, 1), place_ref[...])
    n = planes.shape[0]
    here, before, after = [
        [planes[:, (2 * k + p) * n : (2 * k + p + 1) * n] for p in range(2)] for k in range(3)
    ]
    after = [jnp.where(edge_ref[1] > 0.0, a, h) for a, h in zip(after, here)]
    sums = [0.0, 0.0]
    for a in range(pairs):
        maps = read_maps(block_ref, a, coils)
        spectrum = to_kspace(maps, here, fz_ref[...], fy_ref[...])
        dual = dual_step * masked(mask_ref, a, coils, spectrum - read_data(block_ref, a, coils))
        dual = dual * (1.0 / (1.0 + dual_step))
        dual_ref[a] = dual
        sums = [s + t for s, t in zip(sums, to_image(dual.astype(bf16), maps, gy_ref[...], gz_ref[...]))]
    spread = divergence(shrink(here, after, None))
    duals_before = shrink(before, here, None)
    for p in range(2):
        out_ref[p] = sums[p].astype(bf16)
        image_ref[0, p] = here[p]
        image_ref[1, p] = before[p]
        change_ref[p] = spread[p] + edge_ref[0] * duals_before[p][2]


def second_kernel(
    parts_ref, spread_ref, image_ref, dual_ref, block_ref, mask_ref, fz_ref, fy_ref, gy_ref, gz_ref,
    out_ref, change_ref, guess_ref,
):
    pairs = dual_ref.shape[0]
    coils = dual_ref.shape[2] // parts_ref.shape[2]
    guess = []
    for p in range(2):
        change = spread_ref[p] + sum(parts_ref[r, p].astype(f32) for r in range(parts_ref.shape[0]))
        guess.append(image_ref[0, p] - (2.0 * primal_step) * change)
        change_ref[p] = change
        guess_ref[p] = guess[p]
    sums = [0.0, 0.0]
    for a in range(pairs):
        maps = read_maps(block_ref, a, coils)
        spectrum = to_kspace(maps, guess, fz_ref[...], fy_ref[...])
        step = dual_step * masked(mask_ref, a, coils, spectrum - read_data(block_ref, a, coils))
        dual = (dual_ref[a] + step) * (1.0 / (1.0 + dual_step))
        sums = [s + t for s, t in zip(sums, to_image(dual.astype(bf16), maps, gy_ref[...], gz_ref[...]))]
    for p in range(2):
        out_ref[p] = sums[p].astype(bf16)


def last_kernel(edge_ref, image_ref, change_ref, guess_ref, before_ref, out_ref):
    old_here, old_before = [[image_ref[k, p] for p in range(2)] for k in range(2)]
    here = [guess_ref[p] for p in range(2)]
    before = [before_ref[p] for p in range(2)]
    duals = shrink(before, here, shrink(old_before, old_here, None))
    spread = divergence(duals)
    last = divergence(shrink(here, here, shrink(old_here, old_here, None)))
    for p in range(2):
        out_ref[0, p] = change_ref[p] + edge_ref[0] * duals[p][2] + (1.0 - edge_ref[1]) * last[p]
        out_ref[1, p] = spread[p]


def call(kernel, outs, *operands, vmem=40):
    def place(a):
        return pl.BlockSpec(memory_space=pltpu.SMEM if a.ndim == 1 else pltpu.VMEM)

    return pl.pallas_call(
        kernel,
        in_specs=[place(a) for a in operands],
        out_specs=[place(a) for a in outs],
        out_shape=outs,
        compiler_params=pltpu.CompilerParams(vmem_limit_bytes=vmem * 1024 * 1024),
    )(*operands)


def on_device(kspace_data, coil_maps, sample_mask, initial_image):
    coils, _, planes, ny, nx = coil_maps.shape
    nz, lines = kspace_data.shape[2:4]
    rows = initial_image.shape[2]
    sizes = [lax.axis_size(a) for a in COLUMN]
    zq, group = sizes[0], lax.axis_size(GROUP)
    count = math.prod(sizes)
    slabs = count // zq
    column_of = snake(*sizes)
    place_of = np.argsort(column_of)
    me = lax.axis_index(COLUMN)
    is_first, is_last = me == int(place_of[0]), me == int(place_of[-1])
    quarters = sizes[3]

    def spread(blocks):
        return lax.all_to_all(blocks, COLUMN, 0, 0, tiled=True)

    pick = np.eye(nx, dtype=np.float32)[column_of]
    near = np.concatenate([pick, pick, np.roll(pick, -1, 1), np.roll(pick, 1, 1)], 1)
    inv_x = table(nx, True)[:, column_of].reshape(2 * nx, 2 * nx)
    sort = np.eye(nx, dtype=np.float32).reshape(nx // lines, lines, nx).transpose(1, 0, 2).reshape(nx, nx)
    quarter = np.arange(count) % quarters
    choose = np.zeros((lines, count, coils, lines), np.float32)
    for t in range(lines):
        choose[t, np.arange(count), quarter // 2, t] = 1.0
    lanes = coils * 2 * ny
    half = nz // 2
    packed = jax.ShapeDtypeStruct((nx, planes, 2 * lanes + nz), bf16)
    (blocks,) = call(
        pack_kernel, (packed,), coil_maps, kspace_data, sample_mask.transpose(0, 2, 1), initial_image,
        near.astype(bf16), inv_x, np.stack([sort, sort.T]).astype(bf16),
        choose.reshape(lines * count, -1).astype(bf16), vmem=60,
    )
    blocks = spread(blocks)
    extra = blocks[:, :, 2 * lanes :].reshape(zq, nz, nz)

    def pairs(part):
        return jnp.concatenate([part[: zq // 2], part[zq // 2 :]], 2)

    mask = pairs(extra[:, :, half:])
    mask = jnp.broadcast_to(mask[None], (quarters, *mask.shape))
    mask = lax.all_to_all(mask, COLUMN[3], 0, 0, tiled=True)
    start = lax.all_gather(pairs(extra[:, :, :half]), GROUP, axis=0)

    place = np.zeros((group, zq // 2, 2, 4, 2, rows, 3, 2, zq, group, rows), np.float32)
    for r in range(group):
        for a in range(zq):
            for kind, plane in enumerate((0, 0, 1, 2)):
                for p in range(2):
                    for j in range(rows):
                        place[r, a % (zq // 2), a // (zq // 2), kind, p, j, plane, p, a, r, j] = 1.0
    place = place.reshape(group * zq // 2 * nz, 3 * 2 * ny).astype(bf16)
    edge = jnp.stack([1.0 - is_first.astype(f32), 1.0 - is_last.astype(f32)])

    fz, gz = (table(nz, inverse).reshape(2 * nz, 2 * nz) for inverse in (False, True))
    fy, gy = (table(ny, inverse).reshape(2 * ny, 2 * ny) for inverse in (False, True))
    dual_like = jax.ShapeDtypeStruct((zq, 2 * ny, coils * nz), f32)
    grad_like = jax.ShapeDtypeStruct((2, nz, ny), bf16)
    image_like = jax.ShapeDtypeStruct((2, nz, ny), f32)

    images_like = jax.ShapeDtypeStruct((2, 2, nz, ny), f32)
    dual, grad, spread_sum, images = call(
        first_kernel, (dual_like, grad_like, image_like, images_like),
        edge, start, place, blocks, mask, fz, fy, gy, gz,
    )
    parts = lax.all_gather(grad, GROUP, axis=0)
    grad, change, guess = call(
        second_kernel, (grad_like, image_like, image_like),
        parts, spread_sum, images, dual, blocks, mask, fz, fy, gy, gz,
    )
    forth = [(int(place_of[i]), int(place_of[i + 1])) for i in range(count - 1)]
    before = lax.ppermute(guess, COLUMN, forth)
    grad = grad.reshape(2, nz, zq, group, rows).transpose(3, 0, 1, 2, 4)
    grad = lax.all_to_all(grad, GROUP, 0, 0, tiled=True).astype(f32).sum(0)

    (rest,) = call(last_kernel, (images_like,), edge, images, change, guess, before)
    rest = rest.reshape(2, 2, nz, zq, group, rows)
    rest = lax.dynamic_index_in_dim(rest, lax.axis_index(GROUP), 4, keepdims=False)
    result = jnp.concatenate([rest[:1] + grad[None], rest[1:]], 0)
    result = result.reshape(2, 2, slabs, planes, zq, rows).transpose(4, 2, 0, 1, 3, 5)
    result = spread(result.reshape(count, 2, 2 * planes * rows))
    targets = np.stack([pick, np.concatenate([pick[:, 1:], np.zeros_like(pick[:, :1])], 1)], 1)
    result = lax.dot_general(
        result.reshape(2 * count, -1), targets.reshape(2 * count, nx), (((0,), (0,)), ((), ())),
        precision=lax.Precision.HIGHEST, preferred_element_type=f32,
    )
    return initial_image - primal_step * result.reshape(2, planes, rows, nx)


def solution(mesh):
    devices = mesh.devices.reshape(4, 2, 2, 4, 2, 4)
    split = Mesh(devices, ("zq", "zp", "core", "x", "zhi", "y"))
    coil, slab = ("zq", "zp", "core"), ("x", "zhi", "y")
    return jax.shard_map(
        on_device,
        mesh=split,
        in_specs=(
            P(coil, None, None, slab, None),
            P(coil, None, slab, None, None),
            P(coil, None, slab),
            P(None, slab, coil, None),
        ),
        out_specs=P(None, slab, coil, None),
        check_vma=False,
    )
```

```python
import math

import jax
import jax.numpy as jnp
import ml_dtypes
import numpy as np
from jax import lax
from jax.experimental import pallas as pl
from jax.experimental.pallas import tpu as pltpu
from jax.sharding import Mesh
from jax.sharding import PartitionSpec as P

dual_step = 0.25
primal_step = 0.25
tv_weight = 0.5

COLUMN = ("zq", "x", "zhi", "y")
GROUP = ("zp", "core")
bf16 = jnp.bfloat16
f32 = jnp.float32


def table(length, inverse):
    product = np.outer(np.arange(length), np.arange(length)) % length
    phase = (2.0 * math.pi / length) * product
    real = np.cos(phase) / math.sqrt(length)
    imag = np.sin(phase) / math.sqrt(length) * (1.0 if inverse else -1.0)
    whole = np.stack([np.stack([real, -imag], 1), np.stack([imag, real], 1)])
    return whole.astype(np.float32).astype(ml_dtypes.bfloat16)


def snake(zq, x, zhi, y):
    column = np.zeros((zq, x, zhi, y), np.int32)
    for a in range(zq):
        for h in range(zhi):
            turn = h * zq + a
            for i in range(x):
                for j in range(y):
                    step = i * y + (j if i % 2 == 0 else y - 1 - j)
                    column[a, i, h, j] = turn * x * y + (step if turn % 2 == 0 else x * y - 1 - step)
    return column.reshape(-1)


def dot(a, b):
    return lax.dot_general(a, b, (((1,), (0,)), ((), ())), preferred_element_type=f32)


def dot_t(a, b):
    return lax.dot_general(a, b, (((1,), (1,)), ((), ())), preferred_element_type=f32)


def lanes_to_rows(value, coils):
    n = value.shape[0] // 2
    m = value.shape[1] // coils
    return jnp.concatenate(
        [
            jnp.concatenate([value[p * n : (p + 1) * n, c * m : (c + 1) * m] for p in range(2)], 1)
            for c in range(coils)
        ],
        0,
    )


def to_kspace(maps, image, fz, fy):
    columns = []
    for real, imag in maps:
        columns.append(
            jnp.concatenate(
                [real * image[0] - imag * image[1], real * image[1] + imag * image[0]], 0
            ).astype(bf16)
        )
    half = dot(fz, jnp.concatenate(columns, 1)).astype(bf16)
    return dot_t(fy, lanes_to_rows(half, len(maps)))


def to_image(dual, maps, gy, gz):
    coils, n = len(maps), maps[0][0].shape[0]
    half = dot(gy, dual).astype(bf16)
    field = dot_t(gz, lanes_to_rows(half, coils))
    real_sum, imag_sum = 0.0, 0.0
    for c, (real, imag) in enumerate(maps):
        m = field.shape[1] // coils
        h_real, h_imag = field[:n, c * m : (c + 1) * m], field[n:, c * m : (c + 1) * m]
        real_sum += real * h_real + imag * h_imag
        imag_sum += real * h_imag - imag * h_real
    return real_sum, imag_sum


def lane_block(block_ref, a, i):
    n = block_ref.shape[0]
    slabs = n // block_ref.shape[1]
    return block_ref[a * slabs : (a + 1) * slabs, :, i * n : (i + 1) * n].astype(f32).reshape(n, n)


def read_maps(block_ref, a, coils):
    return [[lane_block(block_ref, a, 2 * c + p) for p in range(2)] for c in range(coils)]


def read_data(block_ref, a, coils):
    return jnp.concatenate(
        [
            jnp.concatenate([lane_block(block_ref, a, 2 * (coils + c) + p) for c in range(coils)], 1)
            for p in range(2)
        ],
        0,
    )


def masked(mask_ref, a, coils, value):
    n = mask_ref.shape[3]
    late, pair = divmod(a, mask_ref.shape[1])
    left = position((n, n), 1) < n // 2
    columns = []
    for c in range(coils):
        halves = [mask_ref[2 * c + h, pair].astype(f32) for h in range(2)]
        halves[1 - late] = pltpu.roll(halves[1 - late], n // 2, 1)
        columns.append(jnp.where(left, halves[0], halves[1]))
    mask = jnp.concatenate(columns, 1)
    return jnp.concatenate([mask, mask], 0) * value


def pack_kernel(maps_ref, data_ref, mask_ref, image_ref, near_ref, inv_ref, sort_ref, choose_ref, out_ref):
    coils, _, planes, n, _ = maps_ref.shape
    lines, rows = data_ref.shape[3], image_ref.shape[2]
    kinds = near_ref.shape[1] // n
    pick = near_ref[:, :n]
    sort, mix = sort_ref[0], sort_ref[1]
    part = n // lines
    half = n // 2
    shape = (n, n)

    field = [jnp.concatenate([data_ref[c, p].reshape(n * lines, n) for p in range(2)], 1) for c in range(coils)]
    field = jnp.concatenate(field, 1)
    field = [dot(sort, field[g * n : (g + 1) * n]).astype(bf16) for g in range(lines)]
    mask = jnp.concatenate([mask_ref[c] for c in range(coils)], 0).astype(f32).astype(bf16)
    odd = lax.rem(position(shape, 0), 2) == 1

    packed = []
    for t in range(planes):
        planes_t = jnp.concatenate([maps_ref[c, p, t] for c in range(coils) for p in range(2)], 0)
        pieces = [dot_t(pick, planes_t)]
        line = jnp.concatenate([f[t * part : (t + 1) * part] for f in field], 0)
        line = jnp.concatenate([line[:, c * 2 * n : (c + 1) * 2 * n] for c in range(coils)], 0)
        turned = dot_t(inv_ref[...], line)
        pieces += [
            turned[p * n : (p + 1) * n, c * n : (c + 1) * n] for c in range(coils) for p in range(2)
        ]
        value = jnp.concatenate([image_ref[p, t] for p in range(2)], 0)
        high = value.astype(bf16).astype(f32)
        parts = [high, value - high, high, high]
        none = jnp.zeros_like(value)
        spread = jnp.concatenate(
            [jnp.concatenate([parts[k] if k == i else none for i in range(kinds)], 1) for k in range(kinds)], 0
        )
        image = dot_t(near_ref[...], jnp.concatenate([spread, jnp.zeros_like(spread)], 0).astype(bf16))
        chosen = dot(choose_ref[t * n : (t + 1) * n], mask)
        chosen = jnp.where(odd, chosen, pltpu.roll(chosen, half, 1))
        pieces.append(jnp.where(position(shape, 1) < half, image, chosen))
        packed.append(jnp.concatenate(pieces, 1).astype(bf16))
    for g in range(lines):
        together = jnp.concatenate([v[g * part : (g + 1) * part] for v in packed], 0)
        mixed = dot(mix, together).astype(bf16)
        out_ref[g * part : (g + 1) * part] = mixed.reshape(part, planes, mixed.shape[1])


def shifted(a, axis, step):
    n = a.shape[axis]
    if step > 0:
        pieces = (lax.slice_in_dim(a, 1, n, axis=axis), lax.slice_in_dim(a, 0, 1, axis=axis))
    else:
        pieces = (lax.slice_in_dim(a, n - 1, n, axis=axis), lax.slice_in_dim(a, 0, n - 1, axis=axis))
    return jnp.concatenate(pieces, axis)


def position(shape, axis):
    return lax.broadcasted_iota(jnp.int32, shape, axis)


def shrink(here, ahead, duals):
    moved = []
    for p in range(2):
        a = here[p]
        up_z = jnp.where(position(a.shape, 0) < a.shape[0] - 1, shifted(a, 0, 1) - a, 0.0)
        up_y = jnp.where(position(a.shape, 1) < a.shape[1] - 1, shifted(a, 1, 1) - a, 0.0)
        steps = [dual_step * up_z, dual_step * up_y, dual_step * (ahead[p] - a)]
        moved.append(steps if duals is None else [d + s for d, s in zip(duals[p], steps)])
    size = jnp.sqrt(sum(m * m for part in moved for m in part))
    factor = 1.0 / jnp.maximum(1.0, size / tv_weight)
    return [[m * factor for m in part] for part in moved]


def divergence(duals):
    sums = []
    for d_z, d_y, d_x in duals:
        back_z = jnp.where(position(d_z.shape, 0) > 0, shifted(d_z, 0, -1), 0.0)
        back_y = jnp.where(position(d_y.shape, 1) > 0, shifted(d_y, 1, -1), 0.0)
        sums.append((back_z - d_z) + (back_y - d_y) - d_x)
    return sums


def first_kernel(
    edge_ref, start_ref, place_ref, block_ref, mask_ref, fz_ref, fy_ref, gy_ref, gz_ref,
    dual_ref, out_ref, change_ref, image_ref,
):
    pairs = dual_ref.shape[0]
    coils = dual_ref.shape[2] // start_ref.shape[2]
    pieces = [start_ref[r, h] for r in range(start_ref.shape[0]) for h in range(start_ref.shape[1])]
    planes = dot(jnp.concatenate(pieces, 1), place_ref[...])
    n = planes.shape[0]
    here, before, after = [
        [planes[:, (2 * k + p) * n : (2 * k + p + 1) * n] for p in range(2)] for k in range(3)
    ]
    after = [jnp.where(edge_ref[1] > 0.0, a, h) for a, h in zip(after, here)]
    sums = [0.0, 0.0]
    for a in range(pairs):
        maps = read_maps(block_ref, a, coils)
        spectrum = to_kspace(maps, here, fz_ref[...], fy_ref[...])
        dual = dual_step * masked(mask_ref, a, coils, spectrum - read_data(block_ref, a, coils))
        dual = dual * (1.0 / (1.0 + dual_step))
        dual_ref[a] = dual
        sums = [s + t for s, t in zip(sums, to_image(dual.astype(bf16), maps, gy_ref[...], gz_ref[...]))]
    spread = divergence(shrink(here, after, None))
    duals_before = shrink(before, here, None)
    for p in range(2):
        out_ref[p] = sums[p].astype(bf16)
        image_ref[0, p] = here[p]
        image_ref[1, p] = before[p]
        change_ref[p] = spread[p] + edge_ref[0] * duals_before[p][2]


def second_kernel(
    parts_ref, spread_ref, image_ref, dual_ref, block_ref, mask_ref, fz_ref, fy_ref, gy_ref, gz_ref,
    out_ref, change_ref, guess_ref,
):
    pairs = dual_ref.shape[0]
    coils = dual_ref.shape[2] // parts_ref.shape[2]
    guess = []
    for p in range(2):
        change = spread_ref[p] + sum(parts_ref[r, p].astype(f32) for r in range(parts_ref.shape[0]))
        guess.append(image_ref[0, p] - (2.0 * primal_step) * change)
        change_ref[p] = change
        guess_ref[p] = guess[p]
    sums = [0.0, 0.0]
    for a in range(pairs):
        maps = read_maps(block_ref, a, coils)
        spectrum = to_kspace(maps, guess, fz_ref[...], fy_ref[...])
        step = dual_step * masked(mask_ref, a, coils, spectrum - read_data(block_ref, a, coils))
        dual = (dual_ref[a] + step) * (1.0 / (1.0 + dual_step))
        sums = [s + t for s, t in zip(sums, to_image(dual.astype(bf16), maps, gy_ref[...], gz_ref[...]))]
    for p in range(2):
        out_ref[p] = sums[p].astype(bf16)


def last_kernel(edge_ref, place_ref, image_ref, change_ref, guess_ref, before_ref, parts_ref, out_ref, plane_ref):
    old_here, old_before = [[image_ref[k, p] for p in range(2)] for k in range(2)]
    here = [guess_ref[p] for p in range(2)]
    before = [before_ref[p] for p in range(2)]
    duals = shrink(before, here, shrink(old_before, old_here, None))
    spread = divergence(duals)
    last = divergence(shrink(here, here, shrink(old_here, old_here, None)))
    group = parts_ref.shape[0]
    n = here[0].shape[1]
    rows = n // group // group
    back = lax.rem(n - rows * place_ref[0], n)
    for p in range(2):
        own = change_ref[p] + sum(parts_ref[r, p].astype(f32) for r in range(group))
        own = own + edge_ref[0] * duals[p][2] + (1.0 - edge_ref[1]) * last[p]
        plane_ref[p] = pltpu.roll(own, back, 1)
        plane_ref[2 + p] = pltpu.roll(spread[p], back, 1)
    slabs = out_ref.shape[0] // group
    planes = n // slabs
    lane = position((slabs, n), 1)
    packed = [jnp.zeros((slabs, n), f32) for _ in range(group)]
    for k in range(4):
        for z in range(planes):
            value = plane_ref[k, pl.ds(z, slabs, stride=planes), :]
            target = (k * planes + z) * rows
            chosen = (lane >= target) & (lane < target + rows)
            for a in range(group):
                moved = pltpu.roll(value, (target - a * group * rows) % n, 1)
                packed[a] = jnp.where(chosen, moved, packed[a])
    for a in range(group):
        out_ref[a * slabs : (a + 1) * slabs] = packed[a]


def result_kernel(packed_ref, target_ref, image_ref, out_ref):
    n = packed_ref.shape[0]
    half = n // 2
    value = packed_ref[...].T
    high = value.astype(bf16)
    low = (value - high.astype(f32)).astype(bf16)
    spread = dot(high, target_ref[...]) + dot(low, target_ref[...])
    change = spread[:half, :n] + spread[half:, n:]
    out_ref[...] = image_ref[...] - primal_step * change.reshape(out_ref.shape)


def call(kernel, outs, *operands, vmem=24, scratch=()):
    def place(a):
        return pl.BlockSpec(memory_space=pltpu.SMEM if a.ndim == 1 else pltpu.VMEM)

    return pl.pallas_call(
        kernel,
        in_specs=[place(a) for a in operands],
        out_specs=[place(a) for a in outs],
        out_shape=outs,
        scratch_shapes=[pltpu.VMEM(shape, f32) for shape in scratch],
        compiler_params=pltpu.CompilerParams(vmem_limit_bytes=vmem * 1024 * 1024),
    )(*operands)


def on_device(kspace_data, coil_maps, sample_mask, initial_image):
    coils, _, planes, ny, nx = coil_maps.shape
    nz, lines = kspace_data.shape[2:4]
    rows = initial_image.shape[2]
    sizes = [lax.axis_size(a) for a in COLUMN]
    zq, group = sizes[0], lax.axis_size(GROUP)
    count = math.prod(sizes)
    slabs = count // zq
    column_of = snake(*sizes)
    place_of = np.argsort(column_of)
    me = lax.axis_index(COLUMN)
    is_first, is_last = me == int(place_of[0]), me == int(place_of[-1])
    quarters = sizes[3]

    def spread(blocks):
        return lax.all_to_all(blocks, COLUMN, 0, 0, tiled=True)

    pick = np.eye(nx, dtype=np.float32)[column_of]
    near = np.concatenate([pick, pick, np.roll(pick, -1, 1), np.roll(pick, 1, 1)], 1)
    inv_x = table(nx, True)[:, column_of].reshape(2 * nx, 2 * nx)
    sort = np.eye(nx, dtype=np.float32).reshape(nx // lines, lines, nx).transpose(1, 0, 2).reshape(nx, nx)
    quarter = np.arange(count) % quarters
    choose = np.zeros((lines, count, coils, lines), np.float32)
    for t in range(lines):
        choose[t, np.arange(count), quarter // 2, t] = 1.0
    lanes = coils * 2 * ny
    half = nz // 2
    packed = jax.ShapeDtypeStruct((nx, planes, 2 * lanes + nz), bf16)
    (blocks,) = call(
        pack_kernel, (packed,), coil_maps, kspace_data, sample_mask.transpose(0, 2, 1), initial_image,
        near.astype(bf16), inv_x, np.stack([sort, sort.T]).astype(bf16),
        choose.reshape(lines * count, -1).astype(bf16), vmem=60,
    )
    blocks = spread(blocks)
    extra = blocks[:, :, 2 * lanes :].reshape(zq, nz, nz)

    def pairs(part):
        return jnp.concatenate([part[: zq // 2], part[zq // 2 :]], 2)

    mask = pairs(extra[:, :, half:])
    mask = jnp.broadcast_to(mask[None], (quarters, *mask.shape))
    mask = lax.all_to_all(mask, COLUMN[3], 0, 0, tiled=True)
    start = lax.all_gather(pairs(extra[:, :, :half]), GROUP, axis=0)

    place = np.zeros((group, zq // 2, 2, 4, 2, rows, 3, 2, zq, group, rows), np.float32)
    for r in range(group):
        for a in range(zq):
            for kind, plane in enumerate((0, 0, 1, 2)):
                for p in range(2):
                    for j in range(rows):
                        place[r, a % (zq // 2), a // (zq // 2), kind, p, j, plane, p, a, r, j] = 1.0
    place = place.reshape(group * zq // 2 * nz, 3 * 2 * ny).astype(bf16)
    edge = jnp.stack([1.0 - is_first.astype(f32), 1.0 - is_last.astype(f32)])

    fz, gz = (table(nz, inverse).reshape(2 * nz, 2 * nz) for inverse in (False, True))
    fy, gy = (table(ny, inverse).reshape(2 * ny, 2 * ny) for inverse in (False, True))
    dual_like = jax.ShapeDtypeStruct((zq, 2 * ny, coils * nz), f32)
    grad_like = jax.ShapeDtypeStruct((2, nz, ny), bf16)
    image_like = jax.ShapeDtypeStruct((2, nz, ny), f32)

    images_like = jax.ShapeDtypeStruct((2, 2, nz, ny), f32)
    dual, grad, spread_sum, images = call(
        first_kernel, (dual_like, grad_like, image_like, images_like),
        edge, start, place, blocks, mask, fz, fy, gy, gz,
    )
    parts = lax.all_gather(grad, GROUP, axis=0)
    grad, change, guess = call(
        second_kernel, (grad_like, image_like, image_like),
        parts, spread_sum, images, dual, blocks, mask, fz, fy, gy, gz,
    )
    forth = [(int(place_of[i]), int(place_of[i + 1])) for i in range(count - 1)]
    before = lax.ppermute(guess, COLUMN, forth)
    parts = lax.all_gather(grad, GROUP, axis=0)
    place_in_group = lax.axis_index(GROUP).astype(jnp.int32)[None]
    (packed,) = call(
        last_kernel, (jax.ShapeDtypeStruct((count, nx), f32),),
        edge, place_in_group, images, change, guess, before, parts, scratch=[(4, nz, ny)],
    )
    packed = spread(packed)
    targets = np.concatenate([pick, pick[:, 1:], np.zeros_like(pick[:, :1])], 1).astype(bf16)
    (image,) = call(
        result_kernel, (jax.ShapeDtypeStruct(initial_image.shape, f32),), packed, targets, initial_image
    )
    return image


def solution(mesh):
    devices = mesh.devices.reshape(4, 2, 2, 4, 2, 4)
    split = Mesh(devices, ("zq", "zp", "core", "x", "zhi", "y"))
    coil, slab = ("zq", "zp", "core"), ("x", "zhi", "y")
    return jax.shard_map(
        on_device,
        mesh=split,
        in_specs=(
            P(coil, None, None, slab, None),
            P(coil, None, slab, None, None),
            P(coil, None, slab),
            P(None, slab, coil, None),
        ),
        out_specs=P(None, slab, coil, None),
        check_vma=False,
    )
```

```python
import math

import jax
import jax.numpy as jnp
import ml_dtypes
import numpy as np
from jax import lax
from jax.experimental import pallas as pl
from jax.experimental.pallas import tpu as pltpu
from jax.sharding import Mesh
from jax.sharding import PartitionSpec as P

dual_step = 0.25
primal_step = 0.25
tv_weight = 0.5

COLUMN = ("zq", "x", "zhi", "y")
GROUP = ("zp", "core")
bf16 = jnp.bfloat16
f32 = jnp.float32


def table(length, inverse):
    product = np.outer(np.arange(length), np.arange(length)) % length
    phase = (2.0 * math.pi / length) * product
    real = np.cos(phase) / math.sqrt(length)
    imag = np.sin(phase) / math.sqrt(length) * (1.0 if inverse else -1.0)
    whole = np.stack([np.stack([real, -imag], 1), np.stack([imag, real], 1)])
    return whole.astype(np.float32).astype(ml_dtypes.bfloat16)


def snake(zq, x, zhi, y):
    column = np.zeros((zq, x, zhi, y), np.int32)
    for a in range(zq):
        for h in range(zhi):
            turn = h * zq + a
            for i in range(x):
                for j in range(y):
                    step = i * y + (j if i % 2 == 0 else y - 1 - j)
                    column[a, i, h, j] = turn * x * y + (step if turn % 2 == 0 else x * y - 1 - step)
    return column.reshape(-1)


def dot(a, b):
    return lax.dot_general(a, b, (((1,), (0,)), ((), ())), preferred_element_type=f32)


def dot_t(a, b):
    return lax.dot_general(a, b, (((1,), (1,)), ((), ())), preferred_element_type=f32)


def lanes_to_rows(value, coils):
    n = value.shape[0] // 2
    m = value.shape[1] // coils
    return jnp.concatenate(
        [
            jnp.concatenate([value[p * n : (p + 1) * n, c * m : (c + 1) * m] for p in range(2)], 1)
            for c in range(coils)
        ],
        0,
    )


def to_kspace(maps, image, fz, fy):
    columns = []
    for real, imag in maps:
        columns.append(
            jnp.concatenate(
                [real * image[0] - imag * image[1], real * image[1] + imag * image[0]], 0
            ).astype(bf16)
        )
    half = dot(fz, jnp.concatenate(columns, 1)).astype(bf16)
    return dot_t(fy, lanes_to_rows(half, len(maps)))


def to_image(dual, maps, gy, gz):
    coils, n = len(maps), maps[0][0].shape[0]
    half = dot(gy, dual).astype(bf16)
    field = dot_t(gz, lanes_to_rows(half, coils))
    real_sum, imag_sum = 0.0, 0.0
    for c, (real, imag) in enumerate(maps):
        m = field.shape[1] // coils
        h_real, h_imag = field[:n, c * m : (c + 1) * m], field[n:, c * m : (c + 1) * m]
        real_sum += real * h_real + imag * h_imag
        imag_sum += real * h_imag - imag * h_real
    return real_sum, imag_sum


def lane_block(block_ref, a, i):
    n = block_ref.shape[0]
    slabs = n // block_ref.shape[1]
    return block_ref[a * slabs : (a + 1) * slabs, :, i * n : (i + 1) * n].astype(f32).reshape(n, n)


def read_maps(block_ref, a, coils):
    return [[lane_block(block_ref, a, 2 * c + p) for p in range(2)] for c in range(coils)]


def read_data(block_ref, a, coils):
    return jnp.concatenate(
        [
            jnp.concatenate([lane_block(block_ref, a, 2 * (coils + c) + p) for c in range(coils)], 1)
            for p in range(2)
        ],
        0,
    )


def read_mask(mask_ref, coils):
    n = mask_ref.shape[3]
    left = position((n, n), 1) < n // 2
    columns = []
    for a in range(2 * mask_ref.shape[1]):
        late, pair = divmod(a, mask_ref.shape[1])
        for c in range(coils):
            halves = [mask_ref[2 * c + h, pair].astype(f32) for h in range(2)]
            halves[1 - late] = pltpu.roll(halves[1 - late], n // 2, 1)
            columns.append(jnp.where(left, halves[0], halves[1]))
    return jnp.concatenate(columns, 1)


def read_coils(block_ref, mask_ref):
    coils = block_ref.shape[2] // block_ref.shape[0] // 4
    pairs = range(2 * mask_ref.shape[1])
    maps = [m for a in pairs for m in read_maps(block_ref, a, coils)]
    data = jnp.concatenate([read_data(block_ref, a, coils) for a in pairs], 1)
    mask = read_mask(mask_ref, coils)
    return maps, data, jnp.concatenate([mask, mask], 0)


def pack_kernel(maps_ref, data_ref, mask_ref, image_ref, near_ref, inv_ref, sort_ref, choose_ref, out_ref):
    coils, _, planes, n, _ = maps_ref.shape
    lines, rows = data_ref.shape[3], image_ref.shape[2]
    kinds = near_ref.shape[1] // n
    pick = near_ref[:, :n]
    sort, mix = sort_ref[0], sort_ref[1]
    part = n // lines
    half = n // 2
    shape = (n, n)

    field = [jnp.concatenate([data_ref[c, p].reshape(n * lines, n) for p in range(2)], 1) for c in range(coils)]
    field = jnp.concatenate(field, 1)
    field = [dot(sort, field[g * n : (g + 1) * n]).astype(bf16) for g in range(lines)]
    mask = jnp.concatenate([mask_ref[c] for c in range(coils)], 0).astype(f32).astype(bf16)
    odd = lax.rem(position(shape, 0), 2) == 1

    packed = []
    for t in range(planes):
        planes_t = jnp.concatenate([maps_ref[c, p, t] for c in range(coils) for p in range(2)], 0)
        pieces = [dot_t(pick, planes_t)]
        line = jnp.concatenate([f[t * part : (t + 1) * part] for f in field], 0)
        line = jnp.concatenate([line[:, c * 2 * n : (c + 1) * 2 * n] for c in range(coils)], 0)
        turned = dot_t(inv_ref[...], line)
        pieces += [
            turned[p * n : (p + 1) * n, c * n : (c + 1) * n] for c in range(coils) for p in range(2)
        ]
        value = jnp.concatenate([image_ref[p, t] for p in range(2)], 0)
        high = value.astype(bf16).astype(f32)
        parts = [high, value - high, high, high]
        none = jnp.zeros_like(value)
        spread = jnp.concatenate(
            [jnp.concatenate([parts[k] if k == i else none for i in range(kinds)], 1) for k in range(kinds)], 0
        )
        image = dot_t(near_ref[...], jnp.concatenate([spread, jnp.zeros_like(spread)], 0).astype(bf16))
        chosen = dot(choose_ref[t * n : (t + 1) * n], mask)
        chosen = jnp.where(odd, chosen, pltpu.roll(chosen, half, 1))
        pieces.append(jnp.where(position(shape, 1) < half, image, chosen))
        packed.append(jnp.concatenate(pieces, 1).astype(bf16))
    for g in range(lines):
        together = jnp.concatenate([v[g * part : (g + 1) * part] for v in packed], 0)
        mixed = dot(mix, together).astype(bf16)
        out_ref[g * part : (g + 1) * part] = mixed.reshape(part, planes, mixed.shape[1])


def shifted(a, axis, step):
    n = a.shape[axis]
    if step > 0:
        pieces = (lax.slice_in_dim(a, 1, n, axis=axis), lax.slice_in_dim(a, 0, 1, axis=axis))
    else:
        pieces = (lax.slice_in_dim(a, n - 1, n, axis=axis), lax.slice_in_dim(a, 0, n - 1, axis=axis))
    return jnp.concatenate(pieces, axis)


def position(shape, axis):
    return lax.broadcasted_iota(jnp.int32, shape, axis)


def shrink(here, ahead, duals):
    moved = []
    for p in range(2):
        a = here[p]
        up_z = jnp.where(position(a.shape, 0) < a.shape[0] - 1, shifted(a, 0, 1) - a, 0.0)
        up_y = jnp.where(position(a.shape, 1) < a.shape[1] - 1, shifted(a, 1, 1) - a, 0.0)
        steps = [dual_step * up_z, dual_step * up_y, dual_step * (ahead[p] - a)]
        moved.append(steps if duals is None else [d + s for d, s in zip(duals[p], steps)])
    size = jnp.sqrt(sum(m * m for part in moved for m in part))
    factor = 1.0 / jnp.maximum(1.0, size / tv_weight)
    return [[m * factor for m in part] for part in moved]


def divergence(duals):
    sums = []
    for d_z, d_y, d_x in duals:
        back_z = jnp.where(position(d_z.shape, 0) > 0, shifted(d_z, 0, -1), 0.0)
        back_y = jnp.where(position(d_y.shape, 1) > 0, shifted(d_y, 1, -1), 0.0)
        sums.append((back_z - d_z) + (back_y - d_y) - d_x)
    return sums


def first_kernel(
    edge_ref, start_ref, place_ref, block_ref, mask_ref, fz_ref, fy_ref, gy_ref, gz_ref,
    dual_ref, out_ref, change_ref, image_ref,
):
    maps, data, mask = read_coils(block_ref, mask_ref)
    pieces = [start_ref[h, r] for r in range(start_ref.shape[1]) for h in range(start_ref.shape[0])]
    planes = dot(jnp.concatenate(pieces, 1), place_ref[...])
    n = planes.shape[0]
    here, before, after = [
        [planes[:, (2 * k + p) * n : (2 * k + p + 1) * n] for p in range(2)] for k in range(3)
    ]
    after = [jnp.where(edge_ref[1] > 0.0, a, h) for a, h in zip(after, here)]
    spectrum = to_kspace(maps, here, fz_ref[...], fy_ref[...])
    dual = dual_step * (mask * (spectrum - data)) * (1.0 / (1.0 + dual_step))
    dual_ref[...] = dual
    sums = to_image(dual.astype(bf16), maps, gy_ref[...], gz_ref[...])
    spread = divergence(shrink(here, after, None))
    duals_before = shrink(before, here, None)
    for p in range(2):
        out_ref[p] = sums[p].astype(bf16)
        image_ref[0, p] = here[p]
        image_ref[1, p] = before[p]
        change_ref[p] = spread[p] + edge_ref[0] * duals_before[p][2]


def second_kernel(
    parts_ref, spread_ref, image_ref, dual_ref, block_ref, mask_ref, fz_ref, fy_ref, gy_ref, gz_ref,
    out_ref, change_ref, guess_ref,
):
    guess = []
    for p in range(2):
        change = spread_ref[p] + sum(parts_ref[r, p].astype(f32) for r in range(parts_ref.shape[0]))
        guess.append(image_ref[0, p] - (2.0 * primal_step) * change)
        change_ref[p] = change
        guess_ref[p] = guess[p]
    maps, data, mask = read_coils(block_ref, mask_ref)
    spectrum = to_kspace(maps, guess, fz_ref[...], fy_ref[...])
    dual = (dual_ref[...] + dual_step * (mask * (spectrum - data))) * (1.0 / (1.0 + dual_step))
    sums = to_image(dual.astype(bf16), maps, gy_ref[...], gz_ref[...])
    for p in range(2):
        out_ref[p] = sums[p].astype(bf16)


def last_kernel(edge_ref, place_ref, image_ref, change_ref, guess_ref, before_ref, parts_ref, out_ref, plane_ref):
    old_here, old_before = [[image_ref[k, p] for p in range(2)] for k in range(2)]
    here = [guess_ref[p] for p in range(2)]
    before = [before_ref[p] for p in range(2)]
    duals = shrink(before, here, shrink(old_before, old_here, None))
    spread = divergence(duals)
    last = divergence(shrink(here, here, shrink(old_here, old_here, None)))
    group = parts_ref.shape[0]
    n = here[0].shape[1]
    rows = n // group // group
    back = lax.rem(n - rows * place_ref[0], n)
    for p in range(2):
        own = change_ref[p] + sum(parts_ref[r, p].astype(f32) for r in range(group))
        own = own + edge_ref[0] * duals[p][2] + (1.0 - edge_ref[1]) * last[p]
        plane_ref[p] = pltpu.roll(own, back, 1)
        plane_ref[2 + p] = pltpu.roll(spread[p], back, 1)
    slabs = out_ref.shape[0] // group
    planes = n // slabs
    lane = position((slabs, n), 1)
    packed = [jnp.zeros((slabs, n), f32) for _ in range(group)]
    for k in range(4):
        for z in range(planes):
            value = plane_ref[k, pl.ds(z, slabs, stride=planes), :]
            target = (k * planes + z) * rows
            chosen = (lane >= target) & (lane < target + rows)
            for a in range(group):
                moved = pltpu.roll(value, (target - a * group * rows) % n, 1)
                packed[a] = jnp.where(chosen, moved, packed[a])
    for a in range(group):
        out_ref[a * slabs : (a + 1) * slabs] = packed[a]


def result_kernel(packed_ref, target_ref, image_ref, out_ref):
    n = packed_ref.shape[0]
    half = n // 2
    value = packed_ref[...].T
    high = value.astype(bf16)
    low = (value - high.astype(f32)).astype(bf16)
    spread = dot(high, target_ref[...]) + dot(low, target_ref[...])
    change = spread[:half, :n] + spread[half:, n:]
    out_ref[...] = image_ref[...] - primal_step * change.reshape(out_ref.shape)


def call(kernel, outs, *operands, vmem=24, scratch=()):
    def place(a):
        return pl.BlockSpec(memory_space=pltpu.SMEM if a.ndim == 1 else pltpu.VMEM)

    return pl.pallas_call(
        kernel,
        in_specs=[place(a) for a in operands],
        out_specs=[place(a) for a in outs],
        out_shape=outs,
        scratch_shapes=scratch,
        compiler_params=pltpu.CompilerParams(vmem_limit_bytes=vmem * 1024 * 1024),
    )(*operands)


def on_device(kspace_data, coil_maps, sample_mask, initial_image):
    coils, _, planes, ny, nx = coil_maps.shape
    nz, lines = kspace_data.shape[2:4]
    rows = initial_image.shape[2]
    sizes = [lax.axis_size(a) for a in COLUMN]
    zq, group = sizes[0], lax.axis_size(GROUP)
    count = math.prod(sizes)
    slabs = count // zq
    column_of = snake(*sizes)
    place_of = np.argsort(column_of)
    me = lax.axis_index(COLUMN)
    is_first, is_last = me == int(place_of[0]), me == int(place_of[-1])
    quarters = sizes[3]

    def spread(blocks):
        return lax.all_to_all(blocks, COLUMN, 0, 0, tiled=True)

    pick = np.eye(nx, dtype=np.float32)[column_of]
    near = np.concatenate([pick, pick, np.roll(pick, -1, 1), np.roll(pick, 1, 1)], 1)
    inv_x = table(nx, True)[:, column_of].reshape(2 * nx, 2 * nx)
    sort = np.eye(nx, dtype=np.float32).reshape(nx // lines, lines, nx).transpose(1, 0, 2).reshape(nx, nx)
    quarter = np.arange(count) % quarters
    choose = np.zeros((lines, count, coils, lines), np.float32)
    for t in range(lines):
        choose[t, np.arange(count), quarter // 2, t] = 1.0
    lanes = coils * 2 * ny
    half = nz // 2
    packed = jax.ShapeDtypeStruct((nx, planes, 2 * lanes + nz), bf16)
    (blocks,) = call(
        pack_kernel, (packed,), coil_maps, kspace_data, sample_mask.transpose(0, 2, 1), initial_image,
        near.astype(bf16), inv_x, np.stack([sort, sort.T]).astype(bf16),
        choose.reshape(lines * count, -1).astype(bf16), vmem=60,
    )
    blocks = spread(blocks)
    extra = blocks[:, :, 2 * lanes :].reshape(zq, nz, nz)

    def pairs(part):
        return jnp.concatenate([part[: zq // 2], part[zq // 2 :]], 2)

    mask = pairs(extra[:, :, half:])
    mask = jnp.broadcast_to(mask[None], (quarters, *mask.shape))
    mask = lax.all_to_all(mask, COLUMN[3], 0, 0, tiled=True)
    start = lax.all_gather(pairs(extra[:, :, :half]), GROUP, axis=1)

    place = np.zeros((group, zq // 2, 2, 4, 2, rows, 3, 2, zq, group, rows), np.float32)
    for r in range(group):
        for a in range(zq):
            for kind, plane in enumerate((0, 0, 1, 2)):
                for p in range(2):
                    for j in range(rows):
                        place[r, a % (zq // 2), a // (zq // 2), kind, p, j, plane, p, a, r, j] = 1.0
    place = place.reshape(group * zq // 2 * nz, 3 * 2 * ny).astype(bf16)
    edge = jnp.stack([1.0 - is_first.astype(f32), 1.0 - is_last.astype(f32)])

    fz, gz = (table(nz, inverse).reshape(2 * nz, 2 * nz) for inverse in (False, True))
    fy, gy = (table(ny, inverse).reshape(2 * ny, 2 * ny) for inverse in (False, True))
    dual_like = jax.ShapeDtypeStruct((2 * ny, zq * coils * nz), f32)
    grad_like = jax.ShapeDtypeStruct((2, nz, ny), bf16)
    image_like = jax.ShapeDtypeStruct((2, nz, ny), f32)

    images_like = jax.ShapeDtypeStruct((2, 2, nz, ny), f32)
    dual, grad, spread_sum, images = call(
        first_kernel, (dual_like, grad_like, image_like, images_like),
        edge, start, place, blocks, mask, fz, fy, gy, gz,
    )
    parts = lax.all_gather(grad, GROUP, axis=0)
    grad, change, guess = call(
        second_kernel, (grad_like, image_like, image_like),
        parts, spread_sum, images, dual, blocks, mask, fz, fy, gy, gz,
    )
    forth = [(int(place_of[i]), int(place_of[i + 1])) for i in range(count - 1)]
    before = lax.ppermute(guess, COLUMN, forth)
    parts = lax.all_gather(grad, GROUP, axis=0)
    place_in_group = lax.axis_index(GROUP).astype(jnp.int32)[None]
    (packed,) = call(
        last_kernel, (jax.ShapeDtypeStruct((count, nx), f32),),
        edge, place_in_group, images, change, guess, before, parts, scratch=[pltpu.VMEM((4, nz, ny), f32)],
    )
    packed = spread(packed)
    targets = np.concatenate([pick, pick[:, 1:], np.zeros_like(pick[:, :1])], 1).astype(bf16)
    (image,) = call(
        result_kernel, (jax.ShapeDtypeStruct(initial_image.shape, f32),), packed, targets, initial_image
    )
    return image


def solution(mesh):
    devices = mesh.devices.reshape(4, 2, 2, 4, 2, 4)
    split = Mesh(devices, ("zq", "zp", "core", "x", "zhi", "y"))
    coil, slab = ("zq", "zp", "core"), ("x", "zhi", "y")
    return jax.shard_map(
        on_device,
        mesh=split,
        in_specs=(
            P(coil, None, None, slab, None),
            P(coil, None, slab, None, None),
            P(coil, None, slab),
            P(None, slab, coil, None),
        ),
        out_specs=P(None, slab, coil, None),
        check_vma=False,
    )
```

```python
import math

import jax
import jax.numpy as jnp
import ml_dtypes
import numpy as np
from jax import lax
from jax.experimental import pallas as pl
from jax.experimental.pallas import tpu as pltpu
from jax.sharding import Mesh
from jax.sharding import PartitionSpec as P

dual_step = 0.25
primal_step = 0.25
tv_weight = 0.5

COLUMN = ("zq", "x", "zhi", "y")
GROUP = ("zp", "core")
bf16 = jnp.bfloat16
f32 = jnp.float32


def table(length, inverse):
    product = np.outer(np.arange(length), np.arange(length)) % length
    phase = (2.0 * math.pi / length) * product
    real = np.cos(phase) / math.sqrt(length)
    imag = np.sin(phase) / math.sqrt(length) * (1.0 if inverse else -1.0)
    whole = np.stack([np.stack([real, -imag], 1), np.stack([imag, real], 1)])
    return whole.astype(np.float32).astype(ml_dtypes.bfloat16)


def snake(zq, x, zhi, y):
    column = np.zeros((zq, x, zhi, y), np.int32)
    for a in range(zq):
        for h in range(zhi):
            turn = h * zq + a
            for i in range(x):
                for j in range(y):
                    step = i * y + (j if i % 2 == 0 else y - 1 - j)
                    column[a, i, h, j] = turn * x * y + (step if turn % 2 == 0 else x * y - 1 - step)
    return column.reshape(-1)


def dot(a, b):
    return lax.dot_general(a, b, (((1,), (0,)), ((), ())), preferred_element_type=f32)


def dot_t(a, b):
    return lax.dot_general(a, b, (((1,), (1,)), ((), ())), preferred_element_type=f32)


def lanes_to_rows(value, coils):
    n = value.shape[0] // 2
    m = value.shape[1] // coils
    return jnp.concatenate(
        [
            jnp.concatenate([value[p * n : (p + 1) * n, c * m : (c + 1) * m] for p in range(2)], 1)
            for c in range(coils)
        ],
        0,
    )


def to_kspace(maps, image, fz, fy):
    columns = []
    for real, imag in maps:
        columns.append(
            jnp.concatenate(
                [real * image[0] - imag * image[1], real * image[1] + imag * image[0]], 0
            ).astype(bf16)
        )
    half = dot(fz, jnp.concatenate(columns, 1)).astype(bf16)
    return dot_t(fy, lanes_to_rows(half, len(maps)))


def to_image(dual, maps, gy, gz):
    coils, n = len(maps), maps[0][0].shape[0]
    half = dot(gy, dual).astype(bf16)
    field = dot_t(gz, lanes_to_rows(half, coils))
    real_sum, imag_sum = 0.0, 0.0
    for c, (real, imag) in enumerate(maps):
        m = field.shape[1] // coils
        h_real, h_imag = field[:n, c * m : (c + 1) * m], field[n:, c * m : (c + 1) * m]
        real_sum += real * h_real + imag * h_imag
        imag_sum += real * h_imag - imag * h_real
    return real_sum, imag_sum


def lane_block(block_ref, a, i):
    n = block_ref.shape[0]
    slabs = n // block_ref.shape[1]
    return block_ref[a * slabs : (a + 1) * slabs, :, i * n : (i + 1) * n].astype(f32).reshape(n, n)


def read_maps(block_ref, a, coils):
    return [[lane_block(block_ref, a, 2 * c + p) for p in range(2)] for c in range(coils)]


def read_data(block_ref, a, coils):
    return jnp.concatenate(
        [
            jnp.concatenate([lane_block(block_ref, a, 2 * (coils + c) + p) for c in range(coils)], 1)
            for p in range(2)
        ],
        0,
    )


def read_mask(mask_ref, coils):
    n = mask_ref.shape[3]
    left = position((n, n), 1) < n // 2
    columns = []
    for a in range(2 * mask_ref.shape[1]):
        late, pair = divmod(a, mask_ref.shape[1])
        for c in range(coils):
            halves = [mask_ref[2 * c + h, pair].astype(f32) for h in range(2)]
            halves[1 - late] = pltpu.roll(halves[1 - late], n // 2, 1)
            columns.append(jnp.where(left, halves[0], halves[1]))
    return jnp.concatenate(columns, 1)


def read_coils(block_ref, mask_ref):
    coils = block_ref.shape[2] // block_ref.shape[0] // 4
    pairs = range(2 * mask_ref.shape[1])
    maps = [m for a in pairs for m in read_maps(block_ref, a, coils)]
    data = jnp.concatenate([read_data(block_ref, a, coils) for a in pairs], 1)
    mask = read_mask(mask_ref, coils)
    return maps, data, jnp.concatenate([mask, mask], 0)


def pack_kernel(*refs):
    sources, out_hbm = refs[:8], refs[8]
    held, out_ref, arrived, left = refs[9:17], refs[17], refs[18], refs[19]
    loads = [pltpu.make_async_copy(a, b, arrived.at[i]) for i, (a, b) in enumerate(zip(sources, held))]
    for load in loads:
        load.start()
    near_ref, maps_ref, sort_ref, data_ref, inv_ref, mask_ref, image_ref, choose_ref = held
    coils, _, planes, n, _ = maps_ref.shape
    lines = data_ref.shape[3]
    kinds = near_ref.shape[1] // n
    lanes = coils * 2 * n
    part = n // lines
    half = n // 2
    shape = (n, n)

    def place(rows, start, stop):
        for g in range(lines):
            together = jnp.concatenate([v[g * part : (g + 1) * part] for v in rows], 0)
            mixed = dot(sort_ref[1], together).astype(bf16)
            out_ref[g * part : (g + 1) * part, :, start:stop] = mixed.reshape(part, planes, stop - start)
        return pltpu.make_async_copy(
            out_ref.at[:, :, start:stop], out_hbm.at[:, :, start:stop], left.at[start // lanes]
        )

    for load in loads[:3]:
        load.wait()
    pick = near_ref[:, :n]
    rows = []
    for t in range(planes):
        planes_t = jnp.concatenate([maps_ref[c, p, t] for c in range(coils) for p in range(2)], 0)
        rows.append(dot_t(pick, planes_t).astype(bf16))
    first = place(rows, 0, lanes)
    first.start()

    for load in loads[3:]:
        load.wait()
    field = [jnp.concatenate([data_ref[c, p].reshape(n * lines, n) for p in range(2)], 1) for c in range(coils)]
    field = jnp.concatenate(field, 1)
    field = [dot(sort_ref[0], field[g * n : (g + 1) * n]).astype(bf16) for g in range(lines)]
    mask = jnp.concatenate([mask_ref[c] for c in range(coils)], 0).astype(f32).astype(bf16)
    odd = lax.rem(position(shape, 0), 2) == 1
    rows = []
    for t in range(planes):
        line = jnp.concatenate([f[t * part : (t + 1) * part] for f in field], 0)
        line = jnp.concatenate([line[:, c * 2 * n : (c + 1) * 2 * n] for c in range(coils)], 0)
        turned = dot_t(inv_ref[...], line)
        pieces = [turned[p * n : (p + 1) * n, c * n : (c + 1) * n] for c in range(coils) for p in range(2)]
        value = jnp.concatenate([image_ref[p, t] for p in range(2)], 0)
        high = value.astype(bf16).astype(f32)
        parts = [high, value - high, high, high]
        none = jnp.zeros_like(value)
        spread = jnp.concatenate(
            [jnp.concatenate([parts[k] if k == i else none for i in range(kinds)], 1) for k in range(kinds)], 0
        )
        image = dot_t(near_ref[...], jnp.concatenate([spread, jnp.zeros_like(spread)], 0).astype(bf16))
        chosen = dot(choose_ref[t * n : (t + 1) * n], mask)
        chosen = jnp.where(odd, chosen, pltpu.roll(chosen, half, 1))
        pieces.append(jnp.where(position(shape, 1) < half, image, chosen))
        rows.append(jnp.concatenate(pieces, 1).astype(bf16))
    second = place(rows, lanes, 2 * lanes + n)
    second.start()
    first.wait()
    second.wait()


def shifted(a, axis, step):
    n = a.shape[axis]
    if step > 0:
        pieces = (lax.slice_in_dim(a, 1, n, axis=axis), lax.slice_in_dim(a, 0, 1, axis=axis))
    else:
        pieces = (lax.slice_in_dim(a, n - 1, n, axis=axis), lax.slice_in_dim(a, 0, n - 1, axis=axis))
    return jnp.concatenate(pieces, axis)


def position(shape, axis):
    return lax.broadcasted_iota(jnp.int32, shape, axis)


def shrink(here, ahead, duals):
    moved = []
    for p in range(2):
        a = here[p]
        up_z = jnp.where(position(a.shape, 0) < a.shape[0] - 1, shifted(a, 0, 1) - a, 0.0)
        up_y = jnp.where(position(a.shape, 1) < a.shape[1] - 1, shifted(a, 1, 1) - a, 0.0)
        steps = [dual_step * up_z, dual_step * up_y, dual_step * (ahead[p] - a)]
        moved.append(steps if duals is None else [d + s for d, s in zip(duals[p], steps)])
    size = jnp.sqrt(sum(m * m for part in moved for m in part))
    factor = 1.0 / jnp.maximum(1.0, size / tv_weight)
    return [[m * factor for m in part] for part in moved]


def divergence(duals):
    sums = []
    for d_z, d_y, d_x in duals:
        back_z = jnp.where(position(d_z.shape, 0) > 0, shifted(d_z, 0, -1), 0.0)
        back_y = jnp.where(position(d_y.shape, 1) > 0, shifted(d_y, 1, -1), 0.0)
        sums.append((back_z - d_z) + (back_y - d_y) - d_x)
    return sums


def first_kernel(
    edge_ref, start_ref, block_ref, mask_ref, fz_ref, fy_ref, gy_ref, gz_ref,
    dual_ref, out_ref, change_ref, image_ref,
):
    maps, data, mask = read_coils(block_ref, mask_ref)
    planes = start_ref[...]
    n = planes.shape[0]
    here, before, after = [
        [planes[:, (2 * k + p) * n : (2 * k + p + 1) * n] for p in range(2)] for k in range(3)
    ]
    after = [jnp.where(edge_ref[1] > 0.0, a, h) for a, h in zip(after, here)]
    spectrum = to_kspace(maps, here, fz_ref[...], fy_ref[...])
    dual = dual_step * (mask * (spectrum - data)) * (1.0 / (1.0 + dual_step))
    dual_ref[...] = dual
    sums = to_image(dual.astype(bf16), maps, gy_ref[...], gz_ref[...])
    spread = divergence(shrink(here, after, None))
    duals_before = shrink(before, here, None)
    for p in range(2):
        out_ref[p] = sums[p].astype(bf16)
        image_ref[0, p] = here[p]
        image_ref[1, p] = before[p]
        change_ref[p] = spread[p] + edge_ref[0] * duals_before[p][2]


def second_kernel(
    parts_ref, spread_ref, image_ref, dual_ref, block_ref, mask_ref, fz_ref, fy_ref, gy_ref, gz_ref,
    out_ref, change_ref, guess_ref,
):
    guess = []
    for p in range(2):
        change = spread_ref[p] + sum(parts_ref[r, p].astype(f32) for r in range(parts_ref.shape[0]))
        guess.append(image_ref[0, p] - (2.0 * primal_step) * change)
        change_ref[p] = change
        guess_ref[p] = guess[p]
    maps, data, mask = read_coils(block_ref, mask_ref)
    spectrum = to_kspace(maps, guess, fz_ref[...], fy_ref[...])
    dual = (dual_ref[...] + dual_step * (mask * (spectrum - data))) * (1.0 / (1.0 + dual_step))
    sums = to_image(dual.astype(bf16), maps, gy_ref[...], gz_ref[...])
    for p in range(2):
        out_ref[p] = sums[p].astype(bf16)


def last_kernel(edge_ref, place_ref, image_ref, change_ref, guess_ref, before_ref, parts_ref, out_ref, plane_ref):
    old_here, old_before = [[image_ref[k, p] for p in range(2)] for k in range(2)]
    here = [guess_ref[p] for p in range(2)]
    before = [before_ref[p] for p in range(2)]
    duals = shrink(before, here, shrink(old_before, old_here, None))
    spread = divergence(duals)
    last = divergence(shrink(here, here, shrink(old_here, old_here, None)))
    group = parts_ref.shape[0]
    n = here[0].shape[1]
    rows = n // group // group
    back = lax.rem(n - rows * place_ref[0], n)
    for p in range(2):
        own = change_ref[p] + sum(parts_ref[r, p].astype(f32) for r in range(group))
        own = own + edge_ref[0] * duals[p][2] + (1.0 - edge_ref[1]) * last[p]
        plane_ref[p] = pltpu.roll(own, back, 1)
        plane_ref[2 + p] = pltpu.roll(spread[p], back, 1)
    slabs = out_ref.shape[0] // group
    planes = n // slabs
    lane = position((slabs, n), 1)
    packed = [jnp.zeros((slabs, n), f32) for _ in range(group)]
    for k in range(4):
        for z in range(planes):
            value = plane_ref[k, pl.ds(z, slabs, stride=planes), :]
            target = (k * planes + z) * rows
            chosen = (lane >= target) & (lane < target + rows)
            for a in range(group):
                moved = pltpu.roll(value, (target - a * group * rows) % n, 1)
                packed[a] = jnp.where(chosen, moved, packed[a])
    for a in range(group):
        out_ref[a * slabs : (a + 1) * slabs] = packed[a]


def result_kernel(packed_ref, target_ref, image_ref, out_ref):
    n = packed_ref.shape[0]
    half = n // 2
    value = packed_ref[...].T
    high = value.astype(bf16)
    low = (value - high.astype(f32)).astype(bf16)
    spread = dot(high, target_ref[...]) + dot(low, target_ref[...])
    change = spread[:half, :n] + spread[half:, n:]
    out_ref[...] = image_ref[...] - primal_step * change.reshape(out_ref.shape)


def call(kernel, outs, *operands, vmem=24, scratch=()):
    def place(a):
        return pl.BlockSpec(memory_space=pltpu.SMEM if a.ndim == 1 else pltpu.VMEM)

    return pl.pallas_call(
        kernel,
        in_specs=[place(a) for a in operands],
        out_specs=[place(a) for a in outs],
        out_shape=outs,
        scratch_shapes=scratch,
        compiler_params=pltpu.CompilerParams(vmem_limit_bytes=vmem * 1024 * 1024),
    )(*operands)


def on_device(kspace_data, coil_maps, sample_mask, initial_image):
    coils, _, planes, ny, nx = coil_maps.shape
    nz, lines = kspace_data.shape[2:4]
    rows = initial_image.shape[2]
    sizes = [lax.axis_size(a) for a in COLUMN]
    zq, group = sizes[0], lax.axis_size(GROUP)
    count = math.prod(sizes)
    slabs = count // zq
    column_of = snake(*sizes)
    place_of = np.argsort(column_of)
    me = lax.axis_index(COLUMN)
    is_first, is_last = me == int(place_of[0]), me == int(place_of[-1])
    quarters = sizes[3]

    def spread(blocks):
        return lax.all_to_all(blocks, COLUMN, 0, 0, tiled=True)

    pick = np.eye(nx, dtype=np.float32)[column_of]
    near = np.concatenate([pick, pick, np.roll(pick, -1, 1), np.roll(pick, 1, 1)], 1)
    inv_x = table(nx, True)[:, column_of].reshape(2 * nx, 2 * nx)
    sort = np.eye(nx, dtype=np.float32).reshape(nx // lines, lines, nx).transpose(1, 0, 2).reshape(nx, nx)
    quarter = np.arange(count) % quarters
    choose = np.zeros((lines, count, coils, lines), np.float32)
    for t in range(lines):
        choose[t, np.arange(count), quarter // 2, t] = 1.0
    lanes = coils * 2 * ny
    half = nz // 2
    packed = jax.ShapeDtypeStruct((nx, planes, 2 * lanes + nz), bf16)
    sources = (
        near.astype(bf16), coil_maps, np.stack([sort, sort.T]).astype(bf16), kspace_data, inv_x,
        sample_mask.transpose(0, 2, 1), initial_image, choose.reshape(lines * count, -1).astype(bf16),
    )
    blocks = pl.pallas_call(
        pack_kernel,
        in_specs=[pl.BlockSpec(memory_space=pl.ANY)] * len(sources),
        out_specs=pl.BlockSpec(memory_space=pl.ANY),
        out_shape=packed,
        scratch_shapes=[pltpu.VMEM(a.shape, a.dtype) for a in (*sources, packed)]
        + [pltpu.SemaphoreType.DMA((len(sources),)), pltpu.SemaphoreType.DMA((2,))],
        compiler_params=pltpu.CompilerParams(vmem_limit_bytes=60 * 1024 * 1024),
    )(*sources)
    blocks = spread(blocks)
    extra = blocks[:, :, 2 * lanes :].reshape(zq, nz, nz)

    def pairs(part):
        return jnp.concatenate([part[: zq // 2], part[zq // 2 :]], 2)

    mask = pairs(extra[:, :, half:])
    mask = jnp.broadcast_to(mask[None], (quarters, *mask.shape))
    mask, start = lax.optimization_barrier((mask, pairs(extra[:, :, :half])))
    mask = lax.all_to_all(mask, COLUMN[3], 0, 0, tiled=True)
    start = lax.all_gather(start, GROUP, axis=1)

    place = np.zeros((group, zq // 2, 2, 4, 2, rows, 3, 2, zq, group, rows), np.float32)
    for r in range(group):
        for a in range(zq):
            for kind, plane in enumerate((0, 0, 1, 2)):
                for p in range(2):
                    for j in range(rows):
                        place[r, a % (zq // 2), a // (zq // 2), kind, p, j, plane, p, a, r, j] = 1.0
    place = place.reshape(group * zq // 2 * nz, 3 * 2 * ny).astype(bf16)
    place = place.reshape(group, zq // 2, nz, -1)
    start = jnp.einsum("hrzl,rhlk->zk", start, place, preferred_element_type=f32)
    edge = jnp.stack([1.0 - is_first.astype(f32), 1.0 - is_last.astype(f32)])

    fz, gz = (table(nz, inverse).reshape(2 * nz, 2 * nz) for inverse in (False, True))
    fy, gy = (table(ny, inverse).reshape(2 * ny, 2 * ny) for inverse in (False, True))
    dual_like = jax.ShapeDtypeStruct((2 * ny, zq * coils * nz), f32)
    grad_like = jax.ShapeDtypeStruct((2, nz, ny), bf16)
    image_like = jax.ShapeDtypeStruct((2, nz, ny), f32)

    images_like = jax.ShapeDtypeStruct((2, 2, nz, ny), f32)
    dual, grad, spread_sum, images = call(
        first_kernel, (dual_like, grad_like, image_like, images_like),
        edge, start, blocks, mask, fz, fy, gy, gz,
    )
    parts = lax.all_gather(grad, GROUP, axis=0)
    grad, change, guess = call(
        second_kernel, (grad_like, image_like, image_like),
        parts, spread_sum, images, dual, blocks, mask, fz, fy, gy, gz,
    )
    forth = [(int(place_of[i]), int(place_of[i + 1])) for i in range(count - 1)]
    before = lax.ppermute(guess, COLUMN, forth)
    parts = lax.all_gather(grad, GROUP, axis=0)
    place_in_group = lax.axis_index(GROUP).astype(jnp.int32)[None]
    (packed,) = call(
        last_kernel, (jax.ShapeDtypeStruct((count, nx), f32),),
        edge, place_in_group, images, change, guess, before, parts, scratch=[pltpu.VMEM((4, nz, ny), f32)],
    )
    packed = spread(packed)
    targets = np.concatenate([pick, pick[:, 1:], np.zeros_like(pick[:, :1])], 1).astype(bf16)
    (image,) = call(
        result_kernel, (jax.ShapeDtypeStruct(initial_image.shape, f32),), packed, targets, initial_image
    )
    return image


def solution(mesh):
    devices = mesh.devices.reshape(4, 2, 2, 4, 2, 4)
    split = Mesh(devices, ("zq", "zp", "core", "x", "zhi", "y"))
    coil, slab = ("zq", "zp", "core"), ("x", "zhi", "y")
    return jax.shard_map(
        on_device,
        mesh=split,
        in_specs=(
            P(coil, None, None, slab, None),
            P(coil, None, slab, None, None),
            P(coil, None, slab),
            P(None, slab, coil, None),
        ),
        out_specs=P(None, slab, coil, None),
        check_vma=False,
    )
```

```python
import math

import jax
import jax.numpy as jnp
import ml_dtypes
import numpy as np
from jax import lax
from jax.experimental import pallas as pl
from jax.experimental.pallas import tpu as pltpu
from jax.sharding import Mesh
from jax.sharding import PartitionSpec as P

dual_step = 0.25
primal_step = 0.25
tv_weight = 0.5

COLUMN = ("zq", "x", "zhi", "y")
GROUP = ("zp", "core")
bf16 = jnp.bfloat16
f32 = jnp.float32


def table(length, inverse):
    product = np.outer(np.arange(length), np.arange(length)) % length
    phase = (2.0 * math.pi / length) * product
    real = np.cos(phase) / math.sqrt(length)
    imag = np.sin(phase) / math.sqrt(length) * (1.0 if inverse else -1.0)
    whole = np.stack([np.stack([real, -imag], 1), np.stack([imag, real], 1)])
    return whole.astype(np.float32).astype(ml_dtypes.bfloat16)


def snake(zq, x, zhi, y):
    column = np.zeros((zq, x, zhi, y), np.int32)
    for a in range(zq):
        for h in range(zhi):
            turn = h * zq + a
            for i in range(x):
                for j in range(y):
                    step = i * y + (j if i % 2 == 0 else y - 1 - j)
                    column[a, i, h, j] = turn * x * y + (step if turn % 2 == 0 else x * y - 1 - step)
    return column.reshape(-1)


def dot(a, b):
    return lax.dot_general(a, b, (((1,), (0,)), ((), ())), preferred_element_type=f32)


def dot_t(a, b):
    return lax.dot_general(a, b, (((1,), (1,)), ((), ())), preferred_element_type=f32)


def lanes_to_rows(value, coils):
    n = value.shape[0] // 2
    m = value.shape[1] // coils
    return jnp.concatenate(
        [
            jnp.concatenate([value[p * n : (p + 1) * n, c * m : (c + 1) * m] for p in range(2)], 1)
            for c in range(coils)
        ],
        0,
    )


def to_kspace(maps, image, fz, fy):
    columns = []
    for real, imag in maps:
        columns.append(
            jnp.concatenate(
                [real * image[0] - imag * image[1], real * image[1] + imag * image[0]], 0
            ).astype(bf16)
        )
    half = dot(fz, jnp.concatenate(columns, 1)).astype(bf16)
    return dot_t(fy, lanes_to_rows(half, len(maps)))


def to_image(dual, maps, gy, gz):
    coils, n = len(maps), maps[0][0].shape[0]
    half = dot(gy, dual).astype(bf16)
    field = dot_t(gz, lanes_to_rows(half, coils))
    real_sum, imag_sum = 0.0, 0.0
    for c, (real, imag) in enumerate(maps):
        m = field.shape[1] // coils
        h_real, h_imag = field[:n, c * m : (c + 1) * m], field[n:, c * m : (c + 1) * m]
        real_sum += real * h_real + imag * h_imag
        imag_sum += real * h_imag - imag * h_real
    return real_sum, imag_sum


def lane_block(block_ref, a, i):
    n = block_ref.shape[0]
    slabs = n // block_ref.shape[1]
    return block_ref[a * slabs : (a + 1) * slabs, :, i * n : (i + 1) * n].astype(f32).reshape(n, n)


def read_maps(block_ref, a, coils):
    return [[lane_block(block_ref, a, 2 * c + p) for p in range(2)] for c in range(coils)]


def read_data(block_ref, a, coils):
    return jnp.concatenate(
        [
            jnp.concatenate([lane_block(block_ref, a, 2 * (coils + c) + p) for c in range(coils)], 1)
            for p in range(2)
        ],
        0,
    )


def read_mask(mask_ref, coils):
    n = mask_ref.shape[3]
    left = position((n, n), 1) < n // 2
    columns = []
    for a in range(2 * mask_ref.shape[1]):
        late, pair = divmod(a, mask_ref.shape[1])
        for c in range(coils):
            halves = [mask_ref[2 * c + h, pair].astype(f32) for h in range(2)]
            halves[1 - late] = pltpu.roll(halves[1 - late], n // 2, 1)
            columns.append(jnp.where(left, halves[0], halves[1]))
    return jnp.concatenate(columns, 1)


def read_coils(block_ref, mask_ref):
    coils = block_ref.shape[2] // block_ref.shape[0] // 4
    pairs = range(2 * mask_ref.shape[1])
    maps = [m for a in pairs for m in read_maps(block_ref, a, coils)]
    data = jnp.concatenate([read_data(block_ref, a, coils) for a in pairs], 1)
    mask = read_mask(mask_ref, coils)
    return maps, data, jnp.concatenate([mask, mask], 0)


def pack_kernel(maps_ref, data_ref, mask_ref, image_ref, near_ref, inv_ref, sort_ref, choose_ref, out_ref):
    coils, _, planes, n, _ = maps_ref.shape
    lines, rows = data_ref.shape[3], image_ref.shape[2]
    kinds = near_ref.shape[1] // n
    pick = near_ref[:, :n]
    sort, mix = sort_ref[0], sort_ref[1]
    part = n // lines
    half = n // 2
    shape = (n, n)

    field = [jnp.concatenate([data_ref[c, p].reshape(n * lines, n) for p in range(2)], 1) for c in range(coils)]
    field = jnp.concatenate(field, 1)
    field = [dot(sort, field[g * n : (g + 1) * n]).astype(bf16) for g in range(lines)]
    mask = jnp.concatenate([mask_ref[c] for c in range(coils)], 0).astype(f32).astype(bf16)
    odd = lax.rem(position(shape, 0), 2) == 1

    packed = []
    for t in range(planes):
        planes_t = jnp.concatenate([maps_ref[c, p, t] for c in range(coils) for p in range(2)], 0)
        pieces = [dot_t(pick, planes_t)]
        line = jnp.concatenate([f[t * part : (t + 1) * part] for f in field], 0)
        line = jnp.concatenate([line[:, c * 2 * n : (c + 1) * 2 * n] for c in range(coils)], 0)
        turned = dot_t(inv_ref[...], line)
        pieces += [
            turned[p * n : (p + 1) * n, c * n : (c + 1) * n] for c in range(coils) for p in range(2)
        ]
        value = jnp.concatenate([image_ref[p, t] for p in range(2)], 0)
        high = value.astype(bf16).astype(f32)
        parts = [high, value - high, high, high]
        none = jnp.zeros_like(value)
        spread = jnp.concatenate(
            [jnp.concatenate([parts[k] if k == i else none for i in range(kinds)], 1) for k in range(kinds)], 0
        )
        image = dot_t(near_ref[...], jnp.concatenate([spread, jnp.zeros_like(spread)], 0).astype(bf16))
        chosen = dot(choose_ref[t * n : (t + 1) * n], mask)
        chosen = jnp.where(odd, chosen, pltpu.roll(chosen, half, 1))
        pieces.append(jnp.where(position(shape, 1) < half, image, chosen))
        packed.append(jnp.concatenate(pieces, 1).astype(bf16))
    for g in range(lines):
        together = jnp.concatenate([v[g * part : (g + 1) * part] for v in packed], 0)
        mixed = dot(mix, together).astype(bf16)
        out_ref[g * part : (g + 1) * part] = mixed.reshape(part, planes, mixed.shape[1])


def shifted(a, axis, step):
    n = a.shape[axis]
    if step > 0:
        pieces = (lax.slice_in_dim(a, 1, n, axis=axis), lax.slice_in_dim(a, 0, 1, axis=axis))
    else:
        pieces = (lax.slice_in_dim(a, n - 1, n, axis=axis), lax.slice_in_dim(a, 0, n - 1, axis=axis))
    return jnp.concatenate(pieces, axis)


def position(shape, axis):
    return lax.broadcasted_iota(jnp.int32, shape, axis)


def shrink(here, ahead, duals):
    moved = []
    for p in range(2):
        a = here[p]
        up_z = jnp.where(position(a.shape, 0) < a.shape[0] - 1, shifted(a, 0, 1) - a, 0.0)
        up_y = jnp.where(position(a.shape, 1) < a.shape[1] - 1, shifted(a, 1, 1) - a, 0.0)
        steps = [dual_step * up_z, dual_step * up_y, dual_step * (ahead[p] - a)]
        moved.append(steps if duals is None else [d + s for d, s in zip(duals[p], steps)])
    size = jnp.sqrt(sum(m * m for part in moved for m in part))
    factor = 1.0 / jnp.maximum(1.0, size / tv_weight)
    return [[m * factor for m in part] for part in moved]


def divergence(duals):
    sums = []
    for d_z, d_y, d_x in duals:
        back_z = jnp.where(position(d_z.shape, 0) > 0, shifted(d_z, 0, -1), 0.0)
        back_y = jnp.where(position(d_y.shape, 1) > 0, shifted(d_y, 1, -1), 0.0)
        sums.append((back_z - d_z) + (back_y - d_y) - d_x)
    return sums


def share_kernel(extra_ref, mask_ref, start_ref):
    pairs, n, _ = start_ref.shape
    left = position((n, n), 1) < n // 2
    for h in range(pairs):
        low, high = (extra_ref[h + k * pairs].astype(f32) for k in range(2))
        start_ref[h] = jnp.where(left, low, pltpu.roll(high, n // 2, 1)).astype(bf16)
        mask = jnp.where(left, pltpu.roll(low, n // 2, 1), high).astype(bf16)
        for q in range(mask_ref.shape[0]):
            mask_ref[q, h] = mask


def first_kernel(
    edge_ref, start_ref, place_ref, block_ref, mask_ref, fz_ref, fy_ref, gy_ref, gz_ref,
    dual_ref, out_ref, change_ref, image_ref,
):
    maps, data, mask = read_coils(block_ref, mask_ref)
    pieces = [start_ref[h, r] for r in range(start_ref.shape[1]) for h in range(start_ref.shape[0])]
    planes = dot(jnp.concatenate(pieces, 1), place_ref[...])
    n = planes.shape[0]
    here, before, after = [
        [planes[:, (2 * k + p) * n : (2 * k + p + 1) * n] for p in range(2)] for k in range(3)
    ]
    after = [jnp.where(edge_ref[1] > 0.0, a, h) for a, h in zip(after, here)]
    spectrum = to_kspace(maps, here, fz_ref[...], fy_ref[...])
    dual = dual_step * (mask * (spectrum - data)) * (1.0 / (1.0 + dual_step))
    dual_ref[...] = dual
    sums = to_image(dual.astype(bf16), maps, gy_ref[...], gz_ref[...])
    spread = divergence(shrink(here, after, None))
    duals_before = shrink(before, here, None)
    for p in range(2):
        out_ref[p] = sums[p].astype(bf16)
        image_ref[0, p] = here[p]
        image_ref[1, p] = before[p]
        change_ref[p] = spread[p] + edge_ref[0] * duals_before[p][2]


def second_kernel(
    parts_ref, spread_ref, image_ref, dual_ref, block_ref, mask_ref, fz_ref, fy_ref, gy_ref, gz_ref,
    out_ref, change_ref, guess_ref,
):
    guess = []
    for p in range(2):
        change = spread_ref[p] + sum(parts_ref[r, p].astype(f32) for r in range(parts_ref.shape[0]))
        guess.append(image_ref[0, p] - (2.0 * primal_step) * change)
        change_ref[p] = change
        guess_ref[p] = guess[p]
    maps, data, mask = read_coils(block_ref, mask_ref)
    spectrum = to_kspace(maps, guess, fz_ref[...], fy_ref[...])
    dual = (dual_ref[...] + dual_step * (mask * (spectrum - data))) * (1.0 / (1.0 + dual_step))
    sums = to_image(dual.astype(bf16), maps, gy_ref[...], gz_ref[...])
    for p in range(2):
        out_ref[p] = sums[p].astype(bf16)


def last_kernel(edge_ref, place_ref, image_ref, change_ref, guess_ref, before_ref, parts_ref, out_ref, plane_ref):
    old_here, old_before = [[image_ref[k, p] for p in range(2)] for k in range(2)]
    here = [guess_ref[p] for p in range(2)]
    before = [before_ref[p] for p in range(2)]
    duals = shrink(before, here, shrink(old_before, old_here, None))
    spread = divergence(duals)
    last = divergence(shrink(here, here, shrink(old_here, old_here, None)))
    group = parts_ref.shape[0]
    n = here[0].shape[1]
    rows = n // group // group
    back = lax.rem(n - rows * place_ref[0], n)
    for p in range(2):
        own = change_ref[p] + sum(parts_ref[r, p].astype(f32) for r in range(group))
        own = own + edge_ref[0] * duals[p][2] + (1.0 - edge_ref[1]) * last[p]
        plane_ref[p] = pltpu.roll(own, back, 1)
        plane_ref[2 + p] = pltpu.roll(spread[p], back, 1)
    slabs = out_ref.shape[0] // group
    planes = n // slabs
    lane = position((slabs, n), 1)
    packed = [jnp.zeros((slabs, n), f32) for _ in range(group)]
    for k in range(4):
        for z in range(planes):
            value = plane_ref[k, pl.ds(z, slabs, stride=planes), :]
            target = (k * planes + z) * rows
            chosen = (lane >= target) & (lane < target + rows)
            for a in range(group):
                moved = pltpu.roll(value, (target - a * group * rows) % n, 1)
                packed[a] = jnp.where(chosen, moved, packed[a])
    for a in range(group):
        out_ref[a * slabs : (a + 1) * slabs] = packed[a]


def result_kernel(packed_ref, target_ref, image_ref, out_ref):
    n = packed_ref.shape[0]
    half = n // 2
    value = packed_ref[...].T
    high = value.astype(bf16)
    low = (value - high.astype(f32)).astype(bf16)
    spread = dot(high, target_ref[...]) + dot(low, target_ref[...])
    change = spread[:half, :n] + spread[half:, n:]
    out_ref[...] = image_ref[...] - primal_step * change.reshape(out_ref.shape)


def call(kernel, outs, *operands, vmem=24, scratch=()):
    def place(a):
        return pl.BlockSpec(memory_space=pltpu.SMEM if a.ndim == 1 else pltpu.VMEM)

    return pl.pallas_call(
        kernel,
        in_specs=[place(a) for a in operands],
        out_specs=[place(a) for a in outs],
        out_shape=outs,
        scratch_shapes=scratch,
        compiler_params=pltpu.CompilerParams(vmem_limit_bytes=vmem * 1024 * 1024),
    )(*operands)


def on_device(kspace_data, coil_maps, sample_mask, initial_image):
    coils, _, planes, ny, nx = coil_maps.shape
    nz, lines = kspace_data.shape[2:4]
    rows = initial_image.shape[2]
    sizes = [lax.axis_size(a) for a in COLUMN]
    zq, group = sizes[0], lax.axis_size(GROUP)
    count = math.prod(sizes)
    slabs = count // zq
    column_of = snake(*sizes)
    place_of = np.argsort(column_of)
    me = lax.axis_index(COLUMN)
    is_first, is_last = me == int(place_of[0]), me == int(place_of[-1])
    quarters = sizes[3]

    def spread(blocks):
        return lax.all_to_all(blocks, COLUMN, 0, 0, tiled=True)

    pick = np.eye(nx, dtype=np.float32)[column_of]
    near = np.concatenate([pick, pick, np.roll(pick, -1, 1), np.roll(pick, 1, 1)], 1)
    inv_x = table(nx, True)[:, column_of].reshape(2 * nx, 2 * nx)
    sort = np.eye(nx, dtype=np.float32).reshape(nx // lines, lines, nx).transpose(1, 0, 2).reshape(nx, nx)
    quarter = np.arange(count) % quarters
    choose = np.zeros((lines, count, coils, lines), np.float32)
    for t in range(lines):
        choose[t, np.arange(count), quarter // 2, t] = 1.0
    lanes = coils * 2 * ny
    packed = jax.ShapeDtypeStruct((nx, planes, 2 * lanes + nz), bf16)
    (blocks,) = call(
        pack_kernel, (packed,), coil_maps, kspace_data, sample_mask.transpose(0, 2, 1), initial_image,
        near.astype(bf16), inv_x, np.stack([sort, sort.T]).astype(bf16),
        choose.reshape(lines * count, -1).astype(bf16), vmem=60,
    )
    blocks = spread(blocks)
    extra = blocks[:, :, 2 * lanes :].reshape(zq, nz, nz)

    mask, start = call(
        share_kernel,
        (jax.ShapeDtypeStruct((quarters, zq // 2, nz, nz), bf16), jax.ShapeDtypeStruct((zq // 2, nz, nz), bf16)),
        extra,
    )
    mask = lax.all_to_all(mask, COLUMN[3], 0, 0, tiled=True)
    start = lax.all_gather(start, GROUP, axis=1)

    place = np.zeros((group, zq // 2, 2, 4, 2, rows, 3, 2, zq, group, rows), np.float32)
    for r in range(group):
        for a in range(zq):
            for kind, plane in enumerate((0, 0, 1, 2)):
                for p in range(2):
                    for j in range(rows):
                        place[r, a % (zq // 2), a // (zq // 2), kind, p, j, plane, p, a, r, j] = 1.0
    place = place.reshape(group * zq // 2 * nz, 3 * 2 * ny).astype(bf16)
    edge = jnp.stack([1.0 - is_first.astype(f32), 1.0 - is_last.astype(f32)])

    fz, gz = (table(nz, inverse).reshape(2 * nz, 2 * nz) for inverse in (False, True))
    fy, gy = (table(ny, inverse).reshape(2 * ny, 2 * ny) for inverse in (False, True))
    dual_like = jax.ShapeDtypeStruct((2 * ny, zq * coils * nz), f32)
    grad_like = jax.ShapeDtypeStruct((2, nz, ny), bf16)
    image_like = jax.ShapeDtypeStruct((2, nz, ny), f32)

    images_like = jax.ShapeDtypeStruct((2, 2, nz, ny), f32)
    dual, grad, spread_sum, images = call(
        first_kernel, (dual_like, grad_like, image_like, images_like),
        edge, start, place, blocks, mask, fz, fy, gy, gz,
    )
    parts = lax.all_gather(grad, GROUP, axis=0)
    grad, change, guess = call(
        second_kernel, (grad_like, image_like, image_like),
        parts, spread_sum, images, dual, blocks, mask, fz, fy, gy, gz,
    )
    forth = [(int(place_of[i]), int(place_of[i + 1])) for i in range(count - 1)]
    before = lax.ppermute(guess, COLUMN, forth)
    parts = lax.all_gather(grad, GROUP, axis=0)
    place_in_group = lax.axis_index(GROUP).astype(jnp.int32)[None]
    (packed,) = call(
        last_kernel, (jax.ShapeDtypeStruct((count, nx), f32),),
        edge, place_in_group, images, change, guess, before, parts, scratch=[pltpu.VMEM((4, nz, ny), f32)],
    )
    packed = spread(packed)
    targets = np.concatenate([pick, pick[:, 1:], np.zeros_like(pick[:, :1])], 1).astype(bf16)
    (image,) = call(
        result_kernel, (jax.ShapeDtypeStruct(initial_image.shape, f32),), packed, targets, initial_image
    )
    return image


def solution(mesh):
    devices = mesh.devices.reshape(4, 2, 2, 4, 2, 4)
    split = Mesh(devices, ("zq", "zp", "core", "x", "zhi", "y"))
    coil, slab = ("zq", "zp", "core"), ("x", "zhi", "y")
    return jax.shard_map(
        on_device,
        mesh=split,
        in_specs=(
            P(coil, None, None, slab, None),
            P(coil, None, slab, None, None),
            P(coil, None, slab),
            P(None, slab, coil, None),
        ),
        out_specs=P(None, slab, coil, None),
        check_vma=False,
    )
```

```python
import math

import jax
import jax.numpy as jnp
import ml_dtypes
import numpy as np
from jax import lax
from jax.experimental import pallas as pl
from jax.experimental.pallas import tpu as pltpu
from jax.sharding import Mesh
from jax.sharding import PartitionSpec as P

dual_step = 0.25
primal_step = 0.25
tv_weight = 0.5

COLUMN = ("zq", "x", "zhi", "y")
GROUP = ("zp", "core")
bf16 = jnp.bfloat16
f32 = jnp.float32


def table(length, inverse):
    product = np.outer(np.arange(length), np.arange(length)) % length
    phase = (2.0 * math.pi / length) * product
    real = np.cos(phase) / math.sqrt(length)
    imag = np.sin(phase) / math.sqrt(length) * (1.0 if inverse else -1.0)
    whole = np.stack([np.stack([real, -imag], 1), np.stack([imag, real], 1)])
    return whole.astype(np.float32).astype(ml_dtypes.bfloat16)


def snake(zq, x, zhi, y):
    column = np.zeros((zq, x, zhi, y), np.int32)
    for a in range(zq):
        for h in range(zhi):
            turn = h * zq + a
            for i in range(x):
                for j in range(y):
                    step = i * y + (j if i % 2 == 0 else y - 1 - j)
                    column[a, i, h, j] = turn * x * y + (step if turn % 2 == 0 else x * y - 1 - step)
    return column.reshape(-1)


def dot(a, b):
    return lax.dot_general(a, b, (((1,), (0,)), ((), ())), preferred_element_type=f32)


def dot_t(a, b):
    return lax.dot_general(a, b, (((1,), (1,)), ((), ())), preferred_element_type=f32)


def lanes_to_rows(value, coils):
    n = value.shape[0] // 2
    m = value.shape[1] // coils
    return jnp.concatenate(
        [
            jnp.concatenate([value[p * n : (p + 1) * n, c * m : (c + 1) * m] for p in range(2)], 1)
            for c in range(coils)
        ],
        0,
    )


def to_kspace(maps, image, fz, fy):
    columns = []
    for real, imag in maps:
        columns.append(
            jnp.concatenate(
                [real * image[0] - imag * image[1], real * image[1] + imag * image[0]], 0
            ).astype(bf16)
        )
    half = dot(fz, jnp.concatenate(columns, 1)).astype(bf16)
    return dot_t(fy, lanes_to_rows(half, len(maps)))


def to_image(dual, maps, gy, gz):
    coils, n = len(maps), maps[0][0].shape[0]
    half = dot(gy, dual).astype(bf16)
    field = dot_t(gz, lanes_to_rows(half, coils))
    real_sum, imag_sum = 0.0, 0.0
    for c, (real, imag) in enumerate(maps):
        m = field.shape[1] // coils
        h_real, h_imag = field[:n, c * m : (c + 1) * m], field[n:, c * m : (c + 1) * m]
        real_sum += real * h_real + imag * h_imag
        imag_sum += real * h_imag - imag * h_real
    return real_sum, imag_sum


def lane_block(block_ref, a, i):
    n = block_ref.shape[0]
    slabs = n // block_ref.shape[1]
    return block_ref[a * slabs : (a + 1) * slabs, :, i * n : (i + 1) * n].astype(f32).reshape(n, n)


def read_maps(block_ref, a, coils):
    return [[lane_block(block_ref, a, 2 * c + p) for p in range(2)] for c in range(coils)]


def read_data(block_ref, a, coils):
    return jnp.concatenate(
        [
            jnp.concatenate([lane_block(block_ref, a, 2 * (coils + c) + p) for c in range(coils)], 1)
            for p in range(2)
        ],
        0,
    )


def read_mask(mask_ref, coils):
    n = mask_ref.shape[3]
    left = position((n, n), 1) < n // 2
    columns = []
    for a in range(2 * mask_ref.shape[1]):
        late, pair = divmod(a, mask_ref.shape[1])
        for c in range(coils):
            halves = [mask_ref[2 * c + h, pair].astype(f32) for h in range(2)]
            halves[1 - late] = pltpu.roll(halves[1 - late], n // 2, 1)
            columns.append(jnp.where(left, halves[0], halves[1]))
    return jnp.concatenate(columns, 1)


def read_coils(block_ref, mask_ref):
    coils = block_ref.shape[2] // block_ref.shape[0] // 4
    pairs = range(2 * mask_ref.shape[1])
    maps = [m for a in pairs for m in read_maps(block_ref, a, coils)]
    data = jnp.concatenate([read_data(block_ref, a, coils) for a in pairs], 1)
    mask = read_mask(mask_ref, coils)
    return maps, data, jnp.concatenate([mask, mask], 0)


def pack_kernel(maps_ref, data_ref, mask_ref, image_ref, near_ref, inv_ref, sort_ref, choose_ref, out_ref):
    coils, _, planes, n, _ = maps_ref.shape
    lines, rows = data_ref.shape[3], image_ref.shape[2]
    kinds = near_ref.shape[1] // n
    pick = near_ref[:, :n]
    sort, mix = sort_ref[0], sort_ref[1]
    part = n // lines
    half = n // 2
    shape = (n, n)

    field = [jnp.concatenate([data_ref[c, p].reshape(n * lines, n) for p in range(2)], 1) for c in range(coils)]
    field = jnp.concatenate(field, 1)
    field = [dot(sort, field[g * n : (g + 1) * n]).astype(bf16) for g in range(lines)]
    mask = jnp.concatenate([mask_ref[c] for c in range(coils)], 0).astype(f32).astype(bf16)
    odd = lax.rem(position(shape, 0), 2) == 1

    packed = []
    for t in range(planes):
        planes_t = jnp.concatenate([maps_ref[c, p, t] for c in range(coils) for p in range(2)], 0)
        pieces = [dot_t(pick, planes_t)]
        line = jnp.concatenate([f[t * part : (t + 1) * part] for f in field], 0)
        line = jnp.concatenate([line[:, c * 2 * n : (c + 1) * 2 * n] for c in range(coils)], 0)
        turned = dot_t(inv_ref[...], line)
        pieces += [
            turned[p * n : (p + 1) * n, c * n : (c + 1) * n] for c in range(coils) for p in range(2)
        ]
        value = jnp.concatenate([image_ref[p, t] for p in range(2)], 0)
        high = value.astype(bf16).astype(f32)
        parts = [high, value - high, high, high]
        none = jnp.zeros_like(value)
        spread = jnp.concatenate(
            [jnp.concatenate([parts[k] if k == i else none for i in range(kinds)], 1) for k in range(kinds)], 0
        )
        image = dot_t(near_ref[...], jnp.concatenate([spread, jnp.zeros_like(spread)], 0).astype(bf16))
        chosen = dot(choose_ref[t * n : (t + 1) * n], mask)
        chosen = jnp.where(odd, chosen, pltpu.roll(chosen, half, 1))
        pieces.append(jnp.where(position(shape, 1) < half, image, chosen))
        packed.append(jnp.concatenate(pieces, 1).astype(bf16))
    for g in range(lines):
        together = jnp.concatenate([v[g * part : (g + 1) * part] for v in packed], 0)
        mixed = dot(mix, together).astype(bf16)
        out_ref[g * part : (g + 1) * part] = mixed.reshape(part, planes, mixed.shape[1])


def shifted(a, axis, step):
    n = a.shape[axis]
    if step > 0:
        pieces = (lax.slice_in_dim(a, 1, n, axis=axis), lax.slice_in_dim(a, 0, 1, axis=axis))
    else:
        pieces = (lax.slice_in_dim(a, n - 1, n, axis=axis), lax.slice_in_dim(a, 0, n - 1, axis=axis))
    return jnp.concatenate(pieces, axis)


def position(shape, axis):
    return lax.broadcasted_iota(jnp.int32, shape, axis)


def shrink(here, ahead, duals):
    moved = []
    for p in range(2):
        a = here[p]
        up_z = jnp.where(position(a.shape, 0) < a.shape[0] - 1, shifted(a, 0, 1) - a, 0.0)
        up_y = jnp.where(position(a.shape, 1) < a.shape[1] - 1, shifted(a, 1, 1) - a, 0.0)
        steps = [dual_step * up_z, dual_step * up_y, dual_step * (ahead[p] - a)]
        moved.append(steps if duals is None else [d + s for d, s in zip(duals[p], steps)])
    size = jnp.sqrt(sum(m * m for part in moved for m in part))
    factor = 1.0 / jnp.maximum(1.0, size / tv_weight)
    return [[m * factor for m in part] for part in moved]


def divergence(duals):
    sums = []
    for d_z, d_y, d_x in duals:
        back_z = jnp.where(position(d_z.shape, 0) > 0, shifted(d_z, 0, -1), 0.0)
        back_y = jnp.where(position(d_y.shape, 1) > 0, shifted(d_y, 1, -1), 0.0)
        sums.append((back_z - d_z) + (back_y - d_y) - d_x)
    return sums


def share_kernel(block_ref, mask_ref, start_ref):
    pairs, n, _ = start_ref.shape
    left = position((n, n), 1) < n // 2
    for h in range(pairs):
        low, high = (lane_block(block_ref, h + k * pairs, block_ref.shape[2] // n - 1) for k in range(2))
        start_ref[h] = jnp.where(left, low, pltpu.roll(high, n // 2, 1)).astype(bf16)
        mask = jnp.where(left, pltpu.roll(low, n // 2, 1), high).astype(bf16)
        for q in range(mask_ref.shape[0]):
            mask_ref[q, h] = mask


def first_kernel(
    edge_ref, start_ref, place_ref, block_ref, mask_ref, fz_ref, fy_ref, gy_ref, gz_ref,
    dual_ref, out_ref, change_ref, image_ref,
):
    maps, data, mask = read_coils(block_ref, mask_ref)
    pieces = [start_ref[h, r] for r in range(start_ref.shape[1]) for h in range(start_ref.shape[0])]
    planes = dot(jnp.concatenate(pieces, 1), place_ref[...])
    n = planes.shape[0]
    here, before, after = [
        [planes[:, (2 * k + p) * n : (2 * k + p + 1) * n] for p in range(2)] for k in range(3)
    ]
    after = [jnp.where(edge_ref[1] > 0.0, a, h) for a, h in zip(after, here)]
    spectrum = to_kspace(maps, here, fz_ref[...], fy_ref[...])
    dual = dual_step * (mask * (spectrum - data)) * (1.0 / (1.0 + dual_step))
    dual_ref[...] = dual
    sums = to_image(dual.astype(bf16), maps, gy_ref[...], gz_ref[...])
    spread = divergence(shrink(here, after, None))
    duals_before = shrink(before, here, None)
    for p in range(2):
        out_ref[p] = sums[p].astype(bf16)
        image_ref[0, p] = here[p]
        image_ref[1, p] = before[p]
        change_ref[p] = spread[p] + edge_ref[0] * duals_before[p][2]


def second_kernel(
    parts_ref, spread_ref, image_ref, dual_ref, block_ref, mask_ref, fz_ref, fy_ref, gy_ref, gz_ref,
    out_ref, change_ref, guess_ref,
):
    guess = []
    for p in range(2):
        change = spread_ref[p] + sum(parts_ref[r, p].astype(f32) for r in range(parts_ref.shape[0]))
        guess.append(image_ref[0, p] - (2.0 * primal_step) * change)
        change_ref[p] = change
        guess_ref[p] = guess[p]
    maps, data, mask = read_coils(block_ref, mask_ref)
    spectrum = to_kspace(maps, guess, fz_ref[...], fy_ref[...])
    dual = (dual_ref[...] + dual_step * (mask * (spectrum - data))) * (1.0 / (1.0 + dual_step))
    sums = to_image(dual.astype(bf16), maps, gy_ref[...], gz_ref[...])
    for p in range(2):
        out_ref[p] = sums[p].astype(bf16)


def last_kernel(edge_ref, place_ref, image_ref, change_ref, guess_ref, before_ref, parts_ref, out_ref, plane_ref):
    old_here, old_before = [[image_ref[k, p] for p in range(2)] for k in range(2)]
    here = [guess_ref[p] for p in range(2)]
    before = [before_ref[p] for p in range(2)]
    duals = shrink(before, here, shrink(old_before, old_here, None))
    spread = divergence(duals)
    last = divergence(shrink(here, here, shrink(old_here, old_here, None)))
    group = parts_ref.shape[0]
    n = here[0].shape[1]
    rows = n // group // group
    back = lax.rem(n - rows * place_ref[0], n)
    for p in range(2):
        own = change_ref[p] + sum(parts_ref[r, p].astype(f32) for r in range(group))
        own = own + edge_ref[0] * duals[p][2] + (1.0 - edge_ref[1]) * last[p]
        plane_ref[p] = pltpu.roll(own, back, 1)
        plane_ref[2 + p] = pltpu.roll(spread[p], back, 1)
    slabs = out_ref.shape[0] // group
    planes = n // slabs
    lane = position((slabs, n), 1)
    packed = [jnp.zeros((slabs, n), f32) for _ in range(group)]
    for k in range(4):
        for z in range(planes):
            value = plane_ref[k, pl.ds(z, slabs, stride=planes), :]
            target = (k * planes + z) * rows
            chosen = (lane >= target) & (lane < target + rows)
            for a in range(group):
                moved = pltpu.roll(value, (target - a * group * rows) % n, 1)
                packed[a] = jnp.where(chosen, moved, packed[a])
    for a in range(group):
        out_ref[a * slabs : (a + 1) * slabs] = packed[a]


def result_kernel(packed_ref, target_ref, image_ref, out_ref):
    n = packed_ref.shape[0]
    half = n // 2
    value = packed_ref[...].T
    high = value.astype(bf16)
    low = (value - high.astype(f32)).astype(bf16)
    spread = dot(high, target_ref[...]) + dot(low, target_ref[...])
    change = spread[:half, :n] + spread[half:, n:]
    out_ref[...] = image_ref[...] - primal_step * change.reshape(out_ref.shape)


def call(kernel, outs, *operands, vmem=24, scratch=()):
    def place(a):
        return pl.BlockSpec(memory_space=pltpu.SMEM if a.ndim == 1 else pltpu.VMEM)

    return pl.pallas_call(
        kernel,
        in_specs=[place(a) for a in operands],
        out_specs=[place(a) for a in outs],
        out_shape=outs,
        scratch_shapes=scratch,
        compiler_params=pltpu.CompilerParams(vmem_limit_bytes=vmem * 1024 * 1024),
    )(*operands)


def on_device(kspace_data, coil_maps, sample_mask, initial_image):
    coils, _, planes, ny, nx = coil_maps.shape
    nz, lines = kspace_data.shape[2:4]
    rows = initial_image.shape[2]
    sizes = [lax.axis_size(a) for a in COLUMN]
    zq, group = sizes[0], lax.axis_size(GROUP)
    count = math.prod(sizes)
    slabs = count // zq
    column_of = snake(*sizes)
    place_of = np.argsort(column_of)
    me = lax.axis_index(COLUMN)
    is_first, is_last = me == int(place_of[0]), me == int(place_of[-1])
    quarters = sizes[3]

    def spread(blocks):
        return lax.all_to_all(blocks, COLUMN, 0, 0, tiled=True)

    pick = np.eye(nx, dtype=np.float32)[column_of]
    near = np.concatenate([pick, pick, np.roll(pick, -1, 1), np.roll(pick, 1, 1)], 1)
    inv_x = table(nx, True)[:, column_of].reshape(2 * nx, 2 * nx)
    sort = np.eye(nx, dtype=np.float32).reshape(nx // lines, lines, nx).transpose(1, 0, 2).reshape(nx, nx)
    quarter = np.arange(count) % quarters
    choose = np.zeros((lines, count, coils, lines), np.float32)
    for t in range(lines):
        choose[t, np.arange(count), quarter // 2, t] = 1.0
    lanes = coils * 2 * ny
    packed = jax.ShapeDtypeStruct((nx, planes, 2 * lanes + nz), bf16)
    (blocks,) = call(
        pack_kernel, (packed,), coil_maps, kspace_data, sample_mask.transpose(0, 2, 1), initial_image,
        near.astype(bf16), inv_x, np.stack([sort, sort.T]).astype(bf16),
        choose.reshape(lines * count, -1).astype(bf16), vmem=60,
    )
    blocks = spread(blocks)

    mask, start = call(
        share_kernel,
        (jax.ShapeDtypeStruct((quarters, zq // 2, nz, nz), bf16), jax.ShapeDtypeStruct((zq // 2, nz, nz), bf16)),
        blocks,
    )
    mask = lax.all_to_all(mask, COLUMN[3], 0, 0, tiled=True)
    start = lax.all_gather(start, GROUP, axis=1)

    place = np.zeros((group, zq // 2, 2, 4, 2, rows, 3, 2, zq, group, rows), np.float32)
    for r in range(group):
        for a in range(zq):
            for kind, plane in enumerate((0, 0, 1, 2)):
                for p in range(2):
                    for j in range(rows):
                        place[r, a % (zq // 2), a // (zq // 2), kind, p, j, plane, p, a, r, j] = 1.0
    place = place.reshape(group * zq // 2 * nz, 3 * 2 * ny).astype(bf16)
    edge = jnp.stack([1.0 - is_first.astype(f32), 1.0 - is_last.astype(f32)])

    fz, gz = (table(nz, inverse).reshape(2 * nz, 2 * nz) for inverse in (False, True))
    fy, gy = (table(ny, inverse).reshape(2 * ny, 2 * ny) for inverse in (False, True))
    dual_like = jax.ShapeDtypeStruct((2 * ny, zq * coils * nz), f32)
    grad_like = jax.ShapeDtypeStruct((2, nz, ny), bf16)
    image_like = jax.ShapeDtypeStruct((2, nz, ny), f32)

    images_like = jax.ShapeDtypeStruct((2, 2, nz, ny), f32)
    dual, grad, spread_sum, images = call(
        first_kernel, (dual_like, grad_like, image_like, images_like),
        edge, start, place, blocks, mask, fz, fy, gy, gz,
    )
    parts = lax.all_gather(grad, GROUP, axis=0)
    grad, change, guess = call(
        second_kernel, (grad_like, image_like, image_like),
        parts, spread_sum, images, dual, blocks, mask, fz, fy, gy, gz,
    )
    forth = [(int(place_of[i]), int(place_of[i + 1])) for i in range(count - 1)]
    before = lax.ppermute(guess, COLUMN, forth)
    parts = lax.all_gather(grad, GROUP, axis=0)
    place_in_group = lax.axis_index(GROUP).astype(jnp.int32)[None]
    (packed,) = call(
        last_kernel, (jax.ShapeDtypeStruct((count, nx), f32),),
        edge, place_in_group, images, change, guess, before, parts, scratch=[pltpu.VMEM((4, nz, ny), f32)],
    )
    packed = spread(packed)
    targets = np.concatenate([pick, pick[:, 1:], np.zeros_like(pick[:, :1])], 1).astype(bf16)
    (image,) = call(
        result_kernel, (jax.ShapeDtypeStruct(initial_image.shape, f32),), packed, targets, initial_image
    )
    return image


def solution(mesh):
    devices = mesh.devices.reshape(4, 2, 2, 4, 2, 4)
    split = Mesh(devices, ("zq", "zp", "core", "x", "zhi", "y"))
    coil, slab = ("zq", "zp", "core"), ("x", "zhi", "y")
    return jax.shard_map(
        on_device,
        mesh=split,
        in_specs=(
            P(coil, None, None, slab, None),
            P(coil, None, slab, None, None),
            P(coil, None, slab),
            P(None, slab, coil, None),
        ),
        out_specs=P(None, slab, coil, None),
        check_vma=False,
    )
```
